32 devices in a mesh: parts: 1, tile: 16 (over z, y, core), face: 2 (over x), sub: 1.
Axes of the slice: x: 2, y: 2, z: 4, core: 2. Of those that a mesh axis runs over, the one named last changes fastest.
Arguments:
- fields: bfloat16 [96, 4, 32, 96], P('sub', 'face', 'tile', 'parts'), may hold values from -6 to 6
- upstream: bfloat16 [96, 4, 32, 96], P('sub', 'face', 'tile', 'parts'), may hold values from -6 to 6
- kernel_one: bfloat16 [3, 3, 96, 96], replicated, may hold values from -0.21875 to 0.21875
- kernel_two: bfloat16 [3, 3, 96, 96], replicated, may hold values from -0.21875 to 0.21875
Outputs:
- result: bfloat16 [96, 4, 32, 96], P('sub', 'face', 'tile', 'parts')
- fields_grad: bfloat16 [96, 4, 32, 96], P('sub', 'face', 'tile', 'parts')
- kernel_one_grad: float32 [3, 3, 96, 96], P('parts', None, None, 'sub')
- kernel_two_grad: float32 [3, 3, 96, 96], P('parts', None, None, 'sub')
The draws below stay inside these ranges and needn't reach their ends.
All inputs are finite; a program needn't handle non-finite values.
Results may differ from the reference program's by a relative error of at most 0.0049.
Values may be sent and summed in bfloat16 or wider, within the bound.
No kernel may reach another device: no remote copies, remote signals or barrier semaphores. Data moves between devices by JAX's collectives and lax.ppermute only.
A program may use at most 128 MiB of HBM per device.

```python
import jax
import jax.numpy as jnp
from jax import lax

C = 96
SIDE = 32


def level_of(key, shape, shards, smallest, largest):
    def one(dim, shards_of):
        steps = jax.random.uniform(jax.random.fold_in(jax.random.fold_in(key, 6), dim), (shards_of,), jnp.float32, smallest / len(shards), largest / len(shards))
        return jnp.repeat(jnp.exp(steps), shape[dim] // shards_of).reshape((-1,) + (1,) * (len(shape) - dim - 1))

    gain = one(*shards[0])
    for cut in shards[1:]:
        gain = gain * one(*cut)
    return gain


def scatter_about(own_key, dims, scale, reach, shards=(), kind=jnp.bfloat16):
    entries = jax.random.normal(own_key, dims, jnp.float32) * scale
    if len(shards) > 0:
        entries = level_of(own_key, dims, shards, -0.22, 0.18) * entries
    return jnp.clip(entries, min=-reach, max=reach).astype(kind)


def setup_inputs(seed: int = 0, part: int = 0) -> dict:
    key_list = jax.random.split(jax.random.key(seed), 5)
    own_keys = jax.random.split(jax.random.fold_in(key_list[4], part), 5)
    fields = scatter_about(own_keys[0], (C, 4, SIDE, 3 * SIDE), 1.0, 6.0, ((1, 2), (2, 16)))
    upstream = scatter_about(own_keys[1], (C, 4, SIDE, 3 * SIDE), 1.0, 6.0, ((1, 2), (2, 16)))
    kernel_one = scatter_about(key_list[2], (3, 3, C, C), (9 * C) ** -0.5, 0.21875)
    kernel_two = scatter_about(key_list[3], (3, 3, C, C), (9 * C) ** -0.5, 0.21875)
    return {"fields": fields, "upstream": upstream, "kernel_one": kernel_one, "kernel_two": kernel_two}


def activate(values):
    return jax.nn.gelu(values, approximate=True)

def sphere_pad(field):
    side = field.shape[2]
    before = jnp.roll(field, 1, axis=1)
    after = jnp.roll(field, -1, axis=1)
    top_line = after[:, :, 0, 0:side]
    bottom_line = before[:, :, side - 1, 2 * side:3 * side]
    left_line = jnp.concatenate([before[:, :, 0:side, 0], before[:, :, side - 1, 0:2 * side]], axis=2)
    right_line = jnp.concatenate([after[:, :, 0, side:3 * side], after[:, :, 0:side, 3 * side - 1]], axis=2)
    corner = jnp.zeros(field.shape[0:2] + (1,), field.dtype)
    top_row = jnp.concatenate([corner, top_line, corner], axis=2)
    bottom_row = jnp.concatenate([corner, bottom_line, corner], axis=2)
    middle = jnp.concatenate([left_line[:, :, None, :], field, right_line[:, :, None, :]], axis=2)
    return jnp.concatenate([top_row[:, :, :, None], middle, bottom_row[:, :, :, None]], axis=3)

def sphere_fold(gradient):
    side = gradient.shape[2] - 2
    height = 3 * side
    interior = gradient[:, :, 1:side + 1, 1:height + 1]
    grad_top = gradient[:, :, 1:side + 1, 0]
    grad_bottom = gradient[:, :, 1:side + 1, height + 1]
    grad_left = gradient[:, :, 0, 1:height + 1]
    grad_right = gradient[:, :, side + 1, 1:height + 1]
    to_after = jnp.zeros_like(interior)
    to_after = to_after.at[:, :, 0, 0:side].add(grad_top)
    to_after = to_after.at[:, :, 0, side:height].add(grad_right[:, :, 0:2 * side])
    to_after = to_after.at[:, :, 0:side, height - 1].add(grad_right[:, :, 2 * side:height])
    to_before = jnp.zeros_like(interior)
    to_before = to_before.at[:, :, side - 1, 2 * side:height].add(grad_bottom)
    to_before = to_before.at[:, :, 0:side, 0].add(grad_left[:, :, 0:side])
    to_before = to_before.at[:, :, side - 1, 0:2 * side].add(grad_left[:, :, side:height])
    return interior + jnp.roll(to_after, 1, axis=1) + jnp.roll(to_before, -1, axis=1)

def convolve(padded, kernel):
    return lax.conv_general_dilated(padded.astype(jnp.float32), kernel.astype(jnp.float32), (1, 1), 'VALID', dimension_numbers=('CNHW', 'HWIO', 'CNHW'), precision=lax.Precision.HIGHEST, preferred_element_type=jnp.float32)

def spread(cotangent, kernel):
    flipped = jnp.flip(kernel, (0, 1)).transpose(0, 1, 3, 2)
    return lax.conv_general_dilated(cotangent.astype(jnp.float32), flipped.astype(jnp.float32), (1, 1), ((2, 2), (2, 2)), dimension_numbers=('CNHW', 'HWIO', 'CNHW'), precision=lax.Precision.HIGHEST, preferred_element_type=jnp.float32)

def weight_terms(padded, cotangent):
    columns = cotangent.shape[2]
    height = cotangent.shape[3]
    flat_cot = cotangent.astype(jnp.float32).reshape(cotangent.shape[0], -1)
    tap_rows = []
    for col_tap in range(3):
        row_list = []
        for row_tap in range(3):
            tap_cells = padded[:, :, col_tap:col_tap + columns, row_tap:row_tap + height]
            tap_cells = tap_cells.astype(jnp.float32).reshape(padded.shape[0], -1)
            row_list.append(lax.dot_general(tap_cells, flat_cot, (((1,), (1,)), ((), ())), precision=lax.Precision.HIGHEST, preferred_element_type=jnp.float32))
        tap_rows.append(jnp.stack(row_list))
    return jnp.stack(tap_rows)

def reference(fields, upstream, kernel_one, kernel_two):
    face_side = fields.shape[2]
    cell_scale = 1.0 / (face_side * jnp.sqrt(jnp.float32(12.0)))
    padded_one = sphere_pad(fields)
    pre_one = convolve(padded_one, kernel_one)
    hidden = activate(pre_one).astype(jnp.bfloat16)
    padded_two = sphere_pad(hidden)
    result = convolve(padded_two, kernel_two).astype(jnp.bfloat16)
    hidden_grad = sphere_fold(spread(upstream, kernel_two))
    unused, pullback = jax.vjp(activate, pre_one)
    pre_grad = pullback(hidden_grad)[0].astype(jnp.bfloat16)
    fields_grad = sphere_fold(spread(pre_grad, kernel_one)).astype(jnp.bfloat16)
    kernel_one_grad = weight_terms(padded_one, pre_grad) * cell_scale
    kernel_two_grad = weight_terms(padded_two, upstream) * cell_scale
    return (result, fields_grad, kernel_one_grad, kernel_two_grad)
```

```python
import functools

import jax
import jax.numpy as jnp
import numpy as np
from jax import lax
from jax.experimental import pallas as pl
from jax.experimental.pallas import tpu as pltpu
from jax.sharding import PartitionSpec as P

BOTH = ("tile", "face")
F32 = jnp.float32
BF16 = jnp.bfloat16
GELU_A = 0.7978845608028654
GELU_B = 0.044715


def up_to(value, step):
    return -(-value // step) * step


class Plan:
    def __init__(self, mesh_shape, block):
        self.tiles = mesh_shape["tile"]
        self.faces = mesh_shape["face"]
        self.stacks, self.cols, self.height = block[1:4]
        self.side = self.height // 3
        self.lanes = up_to(self.height + 2, 128)
        self.channels = block[0] * mesh_shape["sub"]
        self.own = block[0]
        w = self.cols
        self.a_line, self.b_line = 0, w + 2
        self.a_row, self.b_row = 2 * (w + 2), 2 * (w + 2) + w
        self.cells = up_to(4 * w + 4, 16)
        self.kinds = 2 if self.stacks > 1 else 1
        self.near = 2
        self.mid = 2 * self.faces
        self.far = self.tiles // 4
        self.terms = 2 * 9 * self.channels
        self.piece = up_to(-(-self.terms // (self.near * self.mid)), 16)

    def send_table(self):
        t, k, c = self.tiles, self.kinds, self.cells
        g, w, n = self.stacks, self.cols, self.lanes
        table = np.zeros((t, k, c, g, w, n), np.float32)
        for dest in range(t):
            for kind in range(k):
                same = kind == 0 and k == 2
                from_a = 1 if same else 0
                from_b = 0 if same else g - 1
                for e in range(w + 2):
                    row = w * dest - 1 + e
                    if row >= 0:
                        table[dest, kind, self.a_line + e, from_a, 0, row] = 1
                    row = 2 * self.side + w * dest - 1 + e
                    if row < self.height:
                        table[dest, kind, self.b_line + e, from_b, w - 1, row] = 1
                for e in range(w):
                    table[dest, kind, self.a_row + e, from_a, e, self.height - 1] = 1
                    table[dest, kind, self.b_row + e, from_b, e, 0] = 1
        return jnp.asarray(table.reshape(t * k * c, g * w * n), BF16)

    def take_tables(self):
        t, c, w, n = self.tiles, self.cells, self.cols, self.lanes
        from_a = np.zeros((t, c, 2 * n), np.float32)
        from_b = np.zeros((t, c, 2 * n), np.float32)
        for src in range(t):
            for e in range(w):
                from_a[src, self.a_row + e, 2 * self.side + src * w + e] = 1
                from_b[src, self.b_row + e, src * w + e] = 1
        for e in range(w + 2):
            from_a[0, self.a_line + e, n + e] = 1
            from_b[t - 1, self.b_line + e, n + e] = 1
        shape = (t * c, 2 * n)
        return jnp.asarray(from_a.reshape(shape), BF16), jnp.asarray(from_b.reshape(shape), BF16)


def pack_blocks(plan, face, columns, table, blocks_ref):
    t, c = plan.tiles, plan.cells
    for k in range(2):
        flat = jnp.concatenate([x for per in columns[k] for x in per], axis=1)
        picked = lax.dot_general(
            table, flat, (((1,), (1,)), ((), ())), preferred_element_type=F32
        ).astype(BF16)
        picked = picked.reshape(t, plan.kinds, c, flat.shape[0])
        for dest in range(plan.faces):
            if plan.kinds == 2:
                block = jnp.where(face == dest, picked[:, 0], picked[:, 1])
            else:
                block = picked[:, 0]
            blocks_ref[:, dest, k * c : (k + 1) * c, :] = block


def shift(x, by):
    return pltpu.roll(x, by % x.shape[1], 1)


def halos(plan, ids_ref, k, left_ref, right_ref, cross_ref, got_ref, tab_a, tab_b):
    first = ids_ref[0] == 0
    last = ids_ref[0] == plan.tiles - 1
    face = ids_ref[1]
    after = lax.rem(face + 1, plan.faces)
    before = lax.rem(face + plan.faces - 1, plan.faces)
    c = plan.cells
    result = []
    for g in range(plan.stacks):
        face_a = face if g < plan.stacks - 1 else after
        face_b = face if g > 0 else before
        seams = []
        for at, table in ((face_a, tab_a), (face_b, tab_b)):
            rows = got_ref[:, at, k * c : (k + 1) * c, :]
            rows = rows.reshape(plan.tiles * c, rows.shape[-1])
            seams.append(
                lax.dot_general(
                    rows, table, (((0,), (0,)), ((), ())), preferred_element_type=F32
                )
            )
        end_l = left_ref[k, g - 1] if g > 0 else cross_ref[k]
        end_r = right_ref[k, g + 1] if g < plan.stacks - 1 else cross_ref[k]
        n = plan.lanes
        result.append(
            dict(
                first=first,
                last=last,
                left=left_ref[k, g].astype(F32),
                right=right_ref[k, g].astype(F32),
                row_l=seams[1][:, :n],
                row_r=seams[0][:, :n],
                col_l=shift(end_l.astype(F32), plan.side),
                col_r=shift(end_r.astype(F32), -plan.side),
                top=[seams[0][:, n + e : n + e + 1] for e in range(plan.cols + 2)],
                bottom=[seams[1][:, n + e : n + e + 1] for e in range(plan.cols + 2)],
            )
        )
    return result


def forward_operand(plan, own, halo, taps_ref):
    w, n, side, height = plan.cols, plan.lanes, plan.side, plan.height
    c = plan.channels
    lane = lax.broadcasted_iota(jnp.int32, (c, n), 1)
    for g in range(plan.stacks):
        h = halo[g]
        edge_l = jnp.where(lane < side, h["row_l"], jnp.where(lane < height, h["col_l"], 0.0))
        edge_r = jnp.where(
            lane < 2 * side, h["col_r"], jnp.where(lane < height, h["row_r"], 0.0)
        )
        columns = [h["left"]] + own[g] + [h["right"]]
        for j in range(w + 2):
            x = jnp.where(lane == height, h["bottom"][j], columns[j])
            x = jnp.where(lane == n - 1, h["top"][j], x)
            if j == 0:
                x = jnp.where(h["first"], edge_l, x)
            if j == w + 1:
                x = jnp.where(h["last"], edge_r, x)
            for b in range(3):
                y = (x if b == 1 else shift(x, 1 - b)).astype(BF16)
                for a in range(3):
                    out = j - a
                    if 0 <= out < w:
                        at = (g * w + out) * n
                        row = (a * 3 + b) * c
                        taps_ref[row : row + c, at : at + n] = y


def backward_operand(plan, own, halo, taps_ref):
    w, n, side, height = plan.cols, plan.lanes, plan.side, plan.height
    c = plan.channels
    lane = lax.broadcasted_iota(jnp.int32, (c, n), 1)
    zero = jnp.zeros((c, n), BF16)
    for g in range(plan.stacks):
        h = halo[g]
        first, last = h["first"], h["last"]
        edge_l = jnp.where((lane >= side) & (lane <= height), h["col_l"], 0.0)
        edge_r = jnp.where((lane < 2 * side) | (lane == n - 1), h["col_r"], 0.0)
        columns = [jnp.where(first, edge_l, h["left"])] + own[g]
        columns += [jnp.where(last, edge_r, h["right"])]
        keep_l = (lane >= side) | jnp.logical_not(first)
        keep_r = (lane < 2 * side) | jnp.logical_not(last)
        for j in range(w + 2):
            for b in range(3):
                y = columns[j] if b == 1 else shift(columns[j], b - 1)
                if j == 0:
                    y = jnp.where(keep_l, y, 0.0)
                if j == w + 1:
                    y = jnp.where(keep_r, y, 0.0)
                y = y.astype(BF16)
                for a in range(3):
                    out = j - 2 + a
                    if 0 <= out < w:
                        at = (g * w + out) * n
                        row = (a * 3 + b) * c
                        taps_ref[row : row + c, at : at + n] = y
        seam_l = first & (lane < side)
        seam_r = last & (lane >= 2 * side) & (lane < height)
        for out in range(w):
            at = (g * w + out) * n
            for b in range(3):
                y = jnp.where(lane == 0, h["top"][out + 2 - b], 0.0).astype(BF16)
                taps_ref[(9 + b) * c : (10 + b) * c, at : at + n] = y
                y = jnp.where(lane == height - 1, h["bottom"][out + 2 - b], 0.0).astype(BF16)
                taps_ref[(12 + b) * c : (13 + b) * c, at : at + n] = y
                y = zero
                if out == 0:
                    y = jnp.where(seam_l, shift(h["row_l"], b - 1), 0.0).astype(BF16)
                taps_ref[(15 + b) * c : (16 + b) * c, at : at + n] = y
                y = zero
                if out == w - 1:
                    y = jnp.where(seam_r, shift(h["row_r"], b - 1), 0.0).astype(BF16)
                taps_ref[(18 + b) * c : (19 + b) * c, at : at + n] = y


def own_columns(plan, refs, k):
    return [
        [refs[w][k, g].astype(F32) for w in range(plan.cols)] for g in range(plan.stacks)
    ]


def first_kernel(plan, ids_ref, table_ref, *refs):
    columns = refs[: plan.cols]
    blocks_ref = refs[plan.cols]
    parts = [
        [[columns[w][k, g] for w in range(plan.cols)] for g in range(plan.stacks)]
        for k in range(2)
    ]
    pack_blocks(plan, ids_ref[1], parts, table_ref[...], blocks_ref)


def middle_kernel(plan, ids_ref, *refs):
    w, n, g_count, c = plan.cols, plan.lanes, plan.stacks, plan.channels
    columns, refs = refs[:w], refs[w:]
    left, right, cross, got, table, tab_a, tab_b, w_one, w_two = refs[:9]
    refs = refs[9:]
    new_columns, refs = refs[:w], refs[w:]
    blocks_ref, mine_ref, theirs_ref, fwd_ref, bwd_ref, sums_ref = refs
    tab_a, tab_b = tab_a[...], tab_b[...]
    halo = halos(plan, ids_ref, 0, left, right, cross, got, tab_a, tab_b)
    forward_operand(plan, own_columns(plan, columns, 0), halo, fwd_ref)
    halo = halos(plan, ids_ref, 1, left, right, cross, got, tab_a, tab_b)
    upstream = own_columns(plan, columns, 1)
    backward_operand(plan, upstream, halo, bwd_ref)
    pre = jnp.dot(w_one[...], fwd_ref[...], preferred_element_type=F32)
    grad = jnp.dot(w_two[...], bwd_ref[...], preferred_element_type=F32)
    lane = lax.broadcasted_iota(jnp.int32, pre.shape, 1) % n
    inside = lane < plan.height
    bend = jnp.tanh(GELU_A * (pre + GELU_B * (pre * pre * pre)))
    half = 0.5 * (1.0 + bend)
    slope = half + 0.5 * pre * (1.0 - bend * bend) * (
        GELU_A * (1.0 + (3.0 * GELU_B) * (pre * pre))
    )
    hidden = jnp.where(inside, pre * half, 0.0).astype(BF16)
    pre_grad = jnp.where(inside, grad * slope, 0.0).astype(BF16)
    both = (hidden, pre_grad)
    parts = [
        [[both[k][:, (g * w + i) * n : (g * w + i + 1) * n] for i in range(w)] for g in range(g_count)]
        for k in range(2)
    ]
    for k in range(2):
        for g in range(g_count):
            for i in range(w):
                new_columns[i][k, g] = parts[k][g][i]
    pack_blocks(plan, ids_ref[1], parts, table[...], blocks_ref)
    own = plan.own
    half_at = ids_ref[2]
    cot = pre_grad
    terms = lax.dot_general(
        fwd_ref[...], cot, (((1,), (1,)), ((), ())), preferred_element_type=F32
    )
    turned = lax.dot_general(
        bwd_ref[...], hidden, (((1,), (1,)), ((), ())), preferred_element_type=F32
    )
    tap = [turned[i * c : (i + 1) * c] for i in range(21)]
    for b in range(3):
        tap[b] = tap[b] + tap[9 + b]
        tap[6 + b] = tap[6 + b] + tap[12 + b]
    for a in range(3):
        tap[3 * a] = tap[3 * a] + tap[15 + a]
        tap[3 * a + 2] = tap[3 * a + 2] + tap[18 + a]
    sums_ref[0 : 9 * c, :] = terms
    for i in range(9):
        sums_ref[(9 + i) * c : (10 + i) * c, :] = jnp.transpose(tap[i])
    rest = sums_ref.shape[0] - 18 * c
    if rest:
        sums_ref[18 * c :, :] = jnp.zeros((rest, c), F32)
    near, mid = ids_ref[3], ids_ref[4]
    for d in range(plan.mid):
        spot = jnp.bitwise_xor(mid, d)
        for other, ref in ((0, mine_ref), (1, theirs_ref)):
            at = (jnp.bitwise_xor(near, other) * plan.mid + spot) * plan.piece
            rows = sums_ref[pl.ds(pl.multiple_of(at, 16), plan.piece), :]
            ref[d] = rows.astype(ref.dtype)


def last_kernel(plan, ids_ref, *refs):
    w, n = plan.cols, plan.lanes
    columns, refs = refs[:w], refs[w:]
    left, right, cross, got, tab_a, tab_b, w_two, w_one, out_ref, back_ref, fwd_ref, bwd_ref = refs
    tab_a, tab_b = tab_a[...], tab_b[...]
    halo = halos(plan, ids_ref, 0, left, right, cross, got, tab_a, tab_b)
    forward_operand(plan, own_columns(plan, columns, 0), halo, fwd_ref)
    halo = halos(plan, ids_ref, 1, left, right, cross, got, tab_a, tab_b)
    backward_operand(plan, own_columns(plan, columns, 1), halo, bwd_ref)
    out = jnp.dot(w_two[...], fwd_ref[...], preferred_element_type=F32).astype(BF16)
    back = jnp.dot(w_one[...], bwd_ref[...], preferred_element_type=F32).astype(BF16)
    for g in range(plan.stacks):
        for i in range(w):
            at = (g * w + i) * n
            out_ref[g, i] = out[:, at : at + plan.height]
            back_ref[g, i] = back[:, at : at + plan.height]


def sum_kernel(plan, scale, ids_ref, mine_ref, theirs_ref, sums_ref):
    near, mid = ids_ref[3], ids_ref[4]
    for d in range(plan.mid):
        spot = jnp.bitwise_xor(mid, d)
        for other, ref in ((0, mine_ref), (1, theirs_ref)):
            at = (jnp.bitwise_xor(near, other) * plan.mid + spot) * plan.piece
            sums_ref[pl.ds(pl.multiple_of(at, 16), plan.piece), :] = ref[d].astype(F32) * scale


VMEM = pl.BlockSpec(memory_space=pltpu.VMEM)
SMEM = pl.BlockSpec(memory_space=pltpu.SMEM)


def call(body, ids, inputs, outs, scratch=()):
    return pl.pallas_call(
        body,
        out_shape=outs,
        in_specs=[SMEM] + [VMEM] * len(inputs),
        out_specs=[VMEM] * len(outs),
        scratch_shapes=list(scratch),
        compiler_params=pltpu.CompilerParams(vmem_limit_bytes=48 * 2**20),
    )(ids, *inputs)


def tile_ring(plan, x, step):
    count = plan.tiles
    pairs = [(i, (i + step) % count) for i in range(count)]
    if plan.stacks == 1:
        pairs = [(i, j) for i, j in pairs if j == i + step]
    return lax.ppermute(x, "tile", pairs)


def swap_ends(plan, columns):
    t, f = plan.tiles, plan.faces
    first = lax.axis_index("tile") == 0
    sent = jnp.where(first, columns[0][:, 0], columns[-1][:, plan.stacks - 1])
    pairs = [((t - 1) * f + i, (i + 1) % f) for i in range(f)]
    pairs += [((i + 1) % f, (t - 1) * f + i) for i in range(f)]
    return lax.ppermute(sent, BOTH, pairs)


def exchange(plan, columns, blocks):
    left = tile_ring(plan, columns[-1], 1)
    right = tile_ring(plan, columns[0], -1)
    cross = swap_ends(plan, columns)
    count = plan.tiles * plan.faces
    flat = blocks.reshape((count,) + blocks.shape[2:])
    got = lax.all_to_all(flat, BOTH, 0, 0, tiled=True).reshape(blocks.shape)
    return left, right, cross, got


def swapped(plan, x, near=0, mid=0, far=0):
    f = plan.faces
    pairs = []
    for i in range(plan.tiles * f):
        tile, face = i // f, i % f
        tile = tile ^ near ^ ((mid // f) << 1) ^ (far << 2)
        pairs.append((i, tile * f + (face ^ (mid % f))))
    return lax.ppermute(x, BOTH, pairs)


def tree_sum(values):
    while len(values) > 1:
        values = [a + b for a, b in zip(values[::2], values[1::2])]
    return values[0]


def sum_all(plan, mine, theirs):
    half = mine + swapped(plan, theirs, near=1).astype(F32)
    short = half.astype(BF16)
    got = [swapped(plan, short[d], mid=d).astype(F32) for d in range(1, plan.mid)]
    piece = tree_sum([half[0]] + got).astype(BF16)
    got = [swapped(plan, piece, far=d) for d in range(1, plan.far)]
    piece = tree_sum([x.astype(F32) for x in [piece] + got]).astype(BF16)
    pieces = [piece] + [swapped(plan, piece, mid=d) for d in range(1, plan.mid)]
    half = jnp.stack(pieces)
    return half, swapped(plan, half, near=1)


def seam_weights(kernel):
    lines = [kernel.reshape(kernel.shape[0], 9, -1), kernel[:, 0], kernel[:, 2]]
    lines += [kernel[:, :, 0], kernel[:, :, 2]]
    return jnp.concatenate(lines, axis=1).reshape(kernel.shape[0], -1)


def on_device(mesh_shape, fields, upstream, kernel_one, kernel_two):
    plan = Plan(mesh_shape, fields.shape)
    c, own, w, n = plan.channels, plan.own, plan.cols, plan.lanes
    g, h = plan.stacks, plan.height
    tile, face = lax.axis_index("tile"), lax.axis_index("face")
    sub = lax.axis_index("sub")
    mid = ((tile >> 1) & 1) * plan.faces + face
    ids = jnp.stack([tile, face, sub, tile & 1, mid]).astype(jnp.int32)
    if mesh_shape["sub"] > 1:
        fields = lax.all_gather(fields, "sub", axis=0, tiled=True)
        upstream = lax.all_gather(upstream, "sub", axis=0, tiled=True)

    def column(at):
        both = jnp.stack([fields[:, :, at], upstream[:, :, at]])
        return jnp.pad(both.transpose(0, 2, 1, 3), ((0, 0), (0, 0), (0, 0), (0, n - h)))

    columns = [column(i) for i in range(w)]
    table = plan.send_table()
    tab_a, tab_b = plan.take_tables()
    blocks_shape = jax.ShapeDtypeStruct((plan.tiles, plan.faces, 2 * plan.cells, c), BF16)
    (blocks,) = call(
        functools.partial(first_kernel, plan), ids, [table] + columns, [blocks_shape]
    )
    halo = exchange(plan, columns, blocks)

    fwd_one = kernel_one.transpose(3, 0, 1, 2).reshape(c, -1)
    bwd_two = seam_weights(kernel_two.transpose(2, 0, 1, 3))
    fwd_two = lax.dynamic_slice_in_dim(kernel_two, sub * own, own, 3)
    fwd_two = fwd_two.transpose(3, 0, 1, 2).reshape(own, -1)
    bwd_one = lax.dynamic_slice_in_dim(kernel_one, sub * own, own, 2)
    bwd_one = seam_weights(bwd_one.transpose(2, 0, 1, 3))

    taps = [
        pltpu.VMEM((9 * c, g * w * n), BF16),
        pltpu.VMEM((21 * c, g * w * n), BF16),
    ]
    column_shape = jax.ShapeDtypeStruct((2, g, c, n), BF16)
    piece = (plan.mid, plan.piece, c)
    rows = plan.near * plan.mid * plan.piece
    results = call(
        functools.partial(middle_kernel, plan),
        ids,
        columns + list(halo) + [table, tab_a, tab_b, fwd_one, bwd_two],
        [column_shape] * w
        + [blocks_shape, jax.ShapeDtypeStruct(piece, F32), jax.ShapeDtypeStruct(piece, BF16)],
        taps + [pltpu.VMEM((rows, c), F32)],
    )
    columns, (blocks, mine, theirs) = list(results[:w]), results[w:]
    halo = exchange(plan, columns, blocks)
    mine, theirs = sum_all(plan, mine, theirs)
    out_shape = jax.ShapeDtypeStruct((g, w, own, h), BF16)
    result, fields_grad = call(
        functools.partial(last_kernel, plan),
        ids,
        columns + list(halo) + [tab_a, tab_b, fwd_two, bwd_one],
        [out_shape, out_shape],
        taps,
    )
    scale = 1.0 / (plan.side * 12.0**0.5)
    (sums,) = call(
        functools.partial(sum_kernel, plan, scale),
        ids,
        [mine, theirs],
        [jax.ShapeDtypeStruct((rows, c), F32)],
    )
    grads = []
    for i in range(2):
        grad = sums[9 * c * i : 9 * c * (i + 1)].reshape(3, 3, c, c)
        grads.append(lax.dynamic_slice_in_dim(grad, sub * own, own, 3))
    return (
        result.transpose(2, 0, 1, 3),
        fields_grad.transpose(2, 0, 1, 3),
        grads[0],
        grads[1],
    )


def solution(mesh):
    placed = (P("sub", "face", "tile", "parts"), P("sub", "face", "tile", "parts"), P(), P())
    return jax.shard_map(
        functools.partial(on_device, dict(mesh.shape)),
        mesh=mesh,
        in_specs=placed,
        out_specs=(
            P("sub", "face", "tile", "parts"),
            P("sub", "face", "tile", "parts"),
            P("parts", None, None, "sub"),
            P("parts", None, None, "sub"),
        ),
        check_vma=False,
    )
```

```python
import functools

import jax
import jax.numpy as jnp
import numpy as np
from jax import lax
from jax.experimental import pallas as pl
from jax.experimental.pallas import tpu as pltpu
from jax.sharding import PartitionSpec as P

BOTH = ("tile", "face")
F32 = jnp.float32
BF16 = jnp.bfloat16
GELU_A = 0.7978845608028654
GELU_B = 0.044715


def up_to(value, step):
    return -(-value // step) * step


class Plan:
    def __init__(self, mesh_shape, block):
        self.tiles = mesh_shape["tile"]
        self.faces = mesh_shape["face"]
        self.stacks, self.cols, self.height = block[1:4]
        self.side = self.height // 3
        self.lanes = up_to(self.height + 2, 128)
        self.channels = block[0] * mesh_shape["sub"]
        self.own = block[0]
        w = self.cols
        self.reach = w + 4
        self.line = (0, self.reach)
        self.row = (2 * self.reach, 2 * self.reach + w)
        self.cells = up_to(2 * self.reach + 2 * w, 16)
        self.poles = up_to(2 * 3 * self.stacks, 16)
        self.block = 2 * self.cells + self.poles
        self.kinds = 2 if self.stacks > 1 else 1
        self.segments = self.stacks * (w + 2) + 1
        self.rim = up_to(2 * self.stacks * 8, 1)
        self.near = 2
        self.mid = 2 * self.faces
        self.far = self.tiles // 4
        self.terms = 2 * 9 * self.channels
        self.piece = up_to(-(-self.terms // (self.near * self.mid)), 16)

    def segment(self, stack, slot):
        if 1 <= slot <= self.cols:
            return stack * self.cols + slot - 1
        return self.stacks * self.cols + 2 * stack + (1 if slot else 0)

    def send_tables(self):
        t, k, c = self.tiles, self.kinds, self.cells
        g, w, n = self.stacks, self.cols, self.lanes
        high = self.height - 1
        table = np.zeros((2, t, k, c, g, w, n), np.float32)
        poles = np.zeros((2, self.poles // 2, g, w, n), np.float32)
        for dest in range(t):
            for kind in range(k):
                same = kind == 0 and k == 2
                from_a = 1 if same else 0
                from_b = 0 if same else g - 1
                for e in range(self.reach):
                    for depth in range(2):
                        spot = self.line[depth] + e
                        row = w * dest - 2 + e
                        if 0 <= row:
                            table[0, dest, kind, spot, from_a, depth, row] = 1
                        row = 2 * self.side + w * dest - 2 + e
                        if row <= high:
                            table[1, dest, kind, spot, from_b, w - 1 - depth, row] = 1
                for e in range(w):
                    for depth in range(2):
                        spot = self.row[depth] + e
                        if dest == 0:
                            table[:, dest, kind, spot, from_b, e, depth] = 1
                        if dest == t - 1:
                            table[:, dest, kind, spot, from_a, e, high - depth] = 1
        for stack in range(g):
            for i, (col, row) in enumerate(((0, 0), (1, 0), (0, 1))):
                poles[0, 3 * stack + i, stack, col, row] = 1
                poles[1, 3 * stack + i, stack, w - 1 - col, high - row] = 1
        return (
            jnp.asarray(table.reshape(2, t * k * c, g * w * n), BF16),
            jnp.asarray(poles.reshape(2, -1, g * w * n), BF16),
        )

    def take_tables(self):
        t, c, w, n = self.tiles, self.cells, self.cols, self.lanes
        from_a = np.zeros((t, c, 4, n), np.float32)
        from_b = np.zeros((t, c, 4, n), np.float32)
        for depth in range(2):
            for src in range(t):
                for e in range(w):
                    spot = self.row[depth] + e
                    from_a[src, spot, depth, 2 * self.side + src * w + e] = 1
                    from_b[src, spot, depth, src * w + e] = 1
            for e in range(self.reach):
                from_a[0, self.line[depth] + e, 2 + depth, e] = 1
                from_b[t - 1, self.line[depth] + e, 2 + depth, 8 + e] = 1
        ends = np.zeros((self.reach, n, n), np.float32)
        for e in range(self.reach):
            ends[e, 0, e] = 1
            ends[e, self.height - 1, 8 + e] = 1
        shape = (t * c, 4 * n)
        return (
            jnp.asarray(from_a.reshape(shape), BF16),
            jnp.asarray(from_b.reshape(shape), BF16),
            jnp.asarray(ends.reshape(-1, n), BF16),
            jnp.asarray(np.eye(2 * self.poles, n), BF16),
        )


def first_kernel(plan, ids_ref, table_ref, poles_ref, columns_ref, blocks_ref):
    t, c, g, w = plan.tiles, plan.cells, plan.stacks, plan.cols
    face = ids_ref[1]
    end = jnp.where(ids_ref[0] == plan.tiles - 1, 1, 0)
    poles = []
    for k in range(2):
        flat = jnp.concatenate([columns_ref[i, k, j] for j in range(g) for i in range(w)], axis=1)
        picked = product(table_ref[end], flat, 1, 1).astype(BF16)
        picked = picked.reshape(t, plan.kinds, c, flat.shape[0])
        for dest in range(plan.faces):
            if plan.kinds == 2:
                block = jnp.where(face == dest, picked[:, 0], picked[:, 1])
            else:
                block = picked[:, 0]
            blocks_ref[:, dest, k * c : (k + 1) * c, :] = block
        poles.append(product(poles_ref[end], flat, 1, 1))
    poles = jnp.concatenate(poles, axis=0).astype(BF16)
    for dest in range(plan.faces):
        blocks_ref[:, dest, 2 * c :, :] = jnp.broadcast_to(poles[None], (t,) + poles.shape)


def product(x, y, x_dim, y_dim):
    return lax.dot_general(x, y, (((x_dim,), (y_dim,)), ((), ())), preferred_element_type=F32)


def shift(x, by):
    return pltpu.roll(x, by % x.shape[1], 1)


def surroundings(plan, ids_ref, k, columns_ref, near_l, near_r, wrap_ref, cross_ref, got_ref, tables):
    w, n, c = plan.cols, plan.lanes, plan.cells
    high, g_count = plan.height, plan.stacks
    first = ids_ref[0] == 0
    last = ids_ref[0] == plan.tiles - 1
    face = ids_ref[1]
    after = lax.rem(face + 1, plan.faces)
    before = lax.rem(face + plan.faces - 1, plan.faces)
    across = lax.rem(face + 2 // g_count, plan.faces)
    tab_a, tab_b, tab_ends, tab_eye = tables
    pole_rows = [got_ref[at, across, 2 * c :, :] for at in (0, plan.tiles - 1)]
    poles = product(jnp.concatenate(pole_rows, axis=0), tab_eye, 0, 0)
    shape = (plan.channels, n)
    lane = lax.broadcasted_iota(jnp.int32, shape, 1)
    stacks = []
    line, deep, ends = [jnp.zeros(shape, F32) for _ in range(3)]
    for g in range(g_count):
        face_a = face if g < g_count - 1 else after
        face_b = face if g > 0 else before
        seams = []
        for at, table in ((face_a, tab_a), (face_b, tab_b)):
            rows = got_ref[:, at, k * c : (k + 1) * c, :]
            rows = rows.reshape(plan.tiles * c, rows.shape[-1])
            out = product(rows, table, 0, 0)
            seams.append([out[:, i * n : (i + 1) * n] for i in range(4)])
        line += shift(seams[0][2] + seams[1][2], 16 * g)
        deep += shift(seams[0][3] + seams[1][3], 16 * g)
        raw = [near_l[i, k, g] for i in range(2)]
        raw += [columns_ref[i, k, g] for i in range(w)]
        raw += [near_r[i, k, g] for i in range(2)]
        ends += shift(product(jnp.concatenate(raw, axis=1), tab_ends, 1, 0), 16 * g)
        end_l = [(wrap_ref[i, k, g - 1] if g > 0 else cross_ref[i, k]) for i in range(2)]
        end_r = [(wrap_ref[i, k, g] if g < g_count - 1 else cross_ref[i, k]) for i in range(2)]
        pole = []
        for at in range(2):
            base = at * plan.poles + k * (plan.poles // 2) + 3 * g
            pole.append([poles[:, base + i : base + i + 1] for i in range(3)])
        stacks.append(
            dict(
                raw=[x.astype(F32) for x in raw],
                row_l=seams[1][:2],
                row_r=seams[0][:2],
                col_l=[shift(x.astype(F32), plan.side) for x in end_l],
                col_r=[shift(x.astype(F32), -plan.side) for x in end_r],
                north=pole[0],
                south=pole[1],
            )
        )
    spot = lane % 8
    ends = jnp.where(first & (spot < 2), 0.0, ends)
    ends = jnp.where(last & (spot >= w + 2), 0.0, ends)
    rim = dict(line=line, deep=deep, ends=ends, spot=spot, is_top=(lane % 16) < 8)
    return stacks, rim, lane, first, last


def rim_cell(plan, lane, g, bottom, e):
    return lane == 16 * g + 8 * bottom + e


def wide_forward(plan, found, taps_ref):
    stacks, rim, lane, first, last = found
    w, n, side, high, c = plan.cols, plan.lanes, plan.side, plan.height, plan.channels

    def put(a, b, segment, value):
        row = (a * 3 + b) * c
        taps_ref[row : row + c, segment * n : (segment + 1) * n] = value.astype(BF16)

    rows_r = (lane >= 2 * side) & (lane < high)
    for g, h in enumerate(stacks):
        raw = h["raw"]
        x = []
        for q in range(w + 4):
            at = 16 * g + q
            y = jnp.where(lane == high, rim["line"][:, at + 8 : at + 9], raw[q])
            x.append(jnp.where(lane == n - 1, rim["line"][:, at : at + 1], y))
        edge_l = jnp.where(lane < side, h["row_l"][0], jnp.where(lane < high, h["col_l"][1], 0.0))
        edge_r = jnp.where(lane < 2 * side, h["col_r"][0], jnp.where(rows_r, h["row_r"][0], 0.0))
        x[0] = jnp.where(first, h["col_l"][0], x[0])
        x[1] = jnp.where(first, edge_l, x[1])
        x[w + 2] = jnp.where(last, edge_r, x[w + 2])
        x[w + 3] = jnp.where(last, h["col_r"][1], x[w + 3])
        moved = [[shift(y, 1 - b) if b != 1 else y for b in range(3)] for y in x]
        own0, own1, own30, own31 = raw[2], raw[3], raw[w], raw[w + 1]
        north, south = h["north"], h["south"]
        turned_l = [jnp.where(lane < side, own0, 0.0)]
        turned_r = []
        for d in range(2):
            y = jnp.where(lane < side, h["row_l"][d], shift(own0, -d))
            turned_l.append(jnp.where(lane == n - 1, north[d], y))
            y = jnp.where(rows_r, h["row_r"][d], shift(own31, d))
            turned_r.append(jnp.where(lane == high, south[d], y))
        turned_l[1:] = [
            jnp.where((lane > side) & (lane < n - 1), 0.0, y) for y in turned_l[1:]
        ]
        turned_r = [turned_r[1], turned_r[0], jnp.where(rows_r, own31, 0.0)]
        for b in range(3):
            for a in range(3):
                for j in range(1, w + 1):
                    put(a, b, plan.segment(g, j), moved[j + a][b])
                y = shift(h["col_l"][1], 1 - b) if a == 1 else moved[a][b]
                y = jnp.where(lane < side, shift(turned_l[b], 1 - a), y)
                if b == 0:
                    over = shift(own0, 2 - a) if a < 2 else 0.0
                    y = jnp.where(lane == side, over, y)
                elif a == 2:
                    y = jnp.where(lane == high, shift((own0, own1)[b - 1], 1), y)
                    if b == 2:
                        y = jnp.where(lane == high - 1, own0, y)
                put(a, b, plan.segment(g, 0), jnp.where(first, y, moved[a][b]))
                y = shift(h["col_r"][0], 1 - b) if a == 1 else moved[w + 1 + a][b]
                y = jnp.where(rows_r, shift(turned_r[b], 1 - a), y)
                if b == 2:
                    over = shift(own31, -a) if a > 0 else 0.0
                    y = jnp.where(lane == 2 * side - 1, over, y)
                if a == 0:
                    if b == 0:
                        y = jnp.where(lane == 0, own31, y)
                    y = jnp.where(lane == n - 1, shift(own30 if b == 0 else own31, -1), y)
                put(a, b, plan.segment(g, w + 1), jnp.where(last, y, moved[w + 1 + a][b]))
    line, deep, ends = rim["line"], rim["deep"], rim["ends"]
    is_top, spot = rim["is_top"], rim["spot"]
    ends = jnp.where(last & is_top & (spot == w + 2), shift(ends, 1), ends)
    ends = jnp.where(first & jnp.logical_not(is_top) & (spot == 1), shift(ends, -1), ends)
    for g, h in enumerate(stacks):
        north = first & rim_cell(plan, lane, g, 0, 1)
        south = last & rim_cell(plan, lane, g, 1, w + 2)
        line = jnp.where(north, h["north"][0], line)
        deep = jnp.where(north, h["north"][2], deep)
        line = jnp.where(south, h["south"][0], line)
        deep = jnp.where(south, h["south"][2], deep)
    by_a = (jnp.where(is_top, ends, deep), line, jnp.where(is_top, deep, ends))
    for a in range(3):
        for b in range(3):
            put(a, b, plan.segments - 1, shift(by_a[a], -b) if b else by_a[a])


def wide_backward(plan, found, taps_ref):
    stacks, rim, lane, first, last = found
    w, n, side, high, c = plan.cols, plan.lanes, plan.side, plan.height, plan.channels

    def put(row, segment, value):
        taps_ref[row * c : (row + 1) * c, segment * n : (segment + 1) * n] = value.astype(BF16)

    zero = jnp.zeros(lane.shape, F32)
    rows_l = lane < side
    rows_r = (lane >= 2 * side) & (lane < high)
    for g, h in enumerate(stacks):
        raw = h["raw"]
        z = list(raw)
        edge_l = jnp.where((lane >= side) & (lane <= high), h["col_l"][1], 0.0)
        edge_r = jnp.where((lane < 2 * side) | (lane == n - 1), h["col_r"][0], 0.0)
        z[1] = jnp.where(first, edge_l, z[1])
        z[w + 2] = jnp.where(last, edge_r, z[w + 2])
        moved = [[shift(y, b - 1) if b != 1 else y for b in range(3)] for y in z]
        keep_l = (lane >= side) | jnp.logical_not(first)
        keep_r = (lane < 2 * side) | jnp.logical_not(last)
        own0, own1, own30, own31 = raw[2], raw[3], raw[w], raw[w + 1]
        north, south = h["north"], h["south"]
        line_l = [jnp.where(rows_l, y, 0.0) for y in h["row_l"]]
        line_r = [jnp.where(rows_r, y, 0.0) for y in h["row_r"]]
        line_l = [line_l[1], line_l[0], zero]
        line_r = [zero, line_r[0], line_r[1]]
        keep = (lane >= side) & (lane <= high + 1)
        deep_l = [zero] + [jnp.where(keep, h["col_l"][i], 0.0) for i in (1, 0)]
        keep = (lane < 2 * side) | (lane >= n - 2)
        deep_r = [jnp.where(keep, h["col_r"][i], 0.0) for i in (1, 0)] + [zero]
        for b in range(3):
            for a in range(3):
                tap = a * 3 + b
                for j in range(1, w + 1):
                    y = moved[j + 2 - a][b]
                    if j == 1 and a == 2:
                        y = jnp.where(keep_l, y, 0.0)
                    if j == w and a == 0:
                        y = jnp.where(keep_r, y, 0.0)
                    put(tap, plan.segment(g, j), y)
                y = jnp.where(rows_l, shift(line_l[b], a - 1), shift(deep_l[a], b - 1))
                if a == 0:
                    y = jnp.where(lane == side - 1, shift(own0, b - 2), y)
                    y = jnp.where(lane == side, shift(own0, b), y)
                put(tap, plan.segment(g, 0), jnp.where(first, y, moved[2 - a][b]))
                y = jnp.where(rows_r, shift(line_r[b], a - 1), shift(deep_r[a], b - 1))
                if a == 2:
                    y = jnp.where(lane == 2 * side - 1, shift(own31, b - 2), y)
                    y = jnp.where(lane == 2 * side, shift(own31, b), y)
                put(tap, plan.segment(g, w + 1), jnp.where(last, y, moved[w + 3 - a][b]))
        for j in range(w + 2):
            segment = plan.segment(g, j)
            for b in range(3):
                at = 16 * g + j + 2 - b
                top = jnp.where(lane == 0, rim["line"][:, at : at + 1], 0.0)
                bottom = jnp.where(lane == high - 1, rim["line"][:, at + 8 : at + 9], 0.0)
                left = right = zero
                if j == 0:
                    own = jnp.where(lane < high, shift(own0, b - 1), 0.0)
                    top = jnp.where(first, own, top)
                    bottom = jnp.where(first, 0.0, bottom)
                    if b < 2:
                        left = jnp.where(first & (lane == 0), north[1 - b], 0.0)
                        right = jnp.where(first & (lane == high), shift((own1, own0)[b], 1), 0.0)
                if j == 1:
                    left = jnp.where(first & rows_l, shift(line_l[1], b - 1), 0.0)
                if j == w:
                    right = jnp.where(last & rows_r, shift(line_r[1], b - 1), 0.0)
                if j == w + 1:
                    own = jnp.where(lane < high, shift(own31, b - 1), 0.0)
                    bottom = jnp.where(last, own, bottom)
                    top = jnp.where(last, 0.0, top)
                    if b > 0:
                        over = shift((own31, own30)[b - 1], -1)
                        left = jnp.where(last & (lane == n - 1), over, 0.0)
                        right = jnp.where(last & (lane == high - 1), south[b - 1], 0.0)
                for i, y in enumerate((top, bottom, left, right)):
                    put(9 + 3 * i + b, segment, y)
    line, deep, ends = rim["line"], rim["deep"], rim["ends"]
    is_top = rim["is_top"]
    tops = [jnp.where(is_top, y, 0.0) for y in (deep, ends)]
    bottoms = [jnp.where(is_top, 0.0, y) for y in (deep, ends)]
    by_a = (tops[0], line, bottoms[0])
    segment = plan.segments - 1
    for b in range(3):
        for a in range(3):
            put(a * 3 + b, segment, shift(by_a[a], b - 2))
        top = bottom = zero
        for g, h in enumerate(stacks):
            if b < 2:
                over = h["north"][2 * (1 - b)]
                top = jnp.where(first & rim_cell(plan, lane, g, 0, 1), over, top)
            if b > 0:
                over = h["south"][2 * (b - 1)]
                bottom = jnp.where(last & rim_cell(plan, lane, g, 1, w), over, bottom)
        put(9 + b, segment, top)
        put(12 + b, segment, bottom)
        put(15 + b, segment, shift(tops[1], b - 2))
        put(18 + b, segment, shift(bottoms[1], b - 2))


def second_halos(plan, ids_ref, ref):
    w, n, high, side = plan.cols, plan.lanes, plan.height, plan.side
    first = ids_ref[0] == 0
    last = ids_ref[0] == plan.tiles - 1
    start = (plan.segments - 1) * n
    rim = ref[:, start : start + n].astype(F32)
    lane = lax.broadcasted_iota(jnp.int32, rim.shape, 1)
    result = []
    for g in range(plan.stacks):
        left, right = [
            ref[:, plan.segment(g, j) * n : (plan.segment(g, j) + 1) * n].astype(F32)
            for j in (0, w + 1)
        ]
        top = [rim[:, 16 * g + e : 16 * g + e + 1] for e in range(w + 2)]
        bottom = [rim[:, 16 * g + 8 + e : 16 * g + 9 + e] for e in range(w + 2)]
        top[0] = jnp.where(first, 0.0, top[0])
        bottom[0] = jnp.where(first, left[:, high - 1 : high], bottom[0])
        top[w + 1] = jnp.where(last, right[:, 0:1], top[w + 1])
        bottom[w + 1] = jnp.where(last, 0.0, bottom[w + 1])
        result.append(
            dict(
                first=first,
                last=last,
                left=left,
                right=right,
                row_l=jnp.where(lane < side, left, 0.0),
                row_r=jnp.where((lane >= 2 * side) & (lane < high), right, 0.0),
                col_l=left,
                col_r=right,
                top=top,
                bottom=bottom,
            )
        )
    return result


def forward_operand(plan, own, halo, taps_ref):
    w, n, side, height = plan.cols, plan.lanes, plan.side, plan.height
    c = plan.channels
    lane = lax.broadcasted_iota(jnp.int32, (c, n), 1)
    for g in range(plan.stacks):
        h = halo[g]
        edge_l = jnp.where(lane < side, h["row_l"], jnp.where(lane < height, h["col_l"], 0.0))
        edge_r = jnp.where(
            lane < 2 * side, h["col_r"], jnp.where(lane < height, h["row_r"], 0.0)
        )
        columns = [h["left"]] + own[g] + [h["right"]]
        for j in range(w + 2):
            x = jnp.where(lane == height, h["bottom"][j], columns[j])
            x = jnp.where(lane == n - 1, h["top"][j], x)
            if j == 0:
                x = jnp.where(h["first"], edge_l, x)
            if j == w + 1:
                x = jnp.where(h["last"], edge_r, x)
            for b in range(3):
                y = (x if b == 1 else shift(x, 1 - b)).astype(BF16)
                for a in range(3):
                    out = j - a
                    if 0 <= out < w:
                        at = (g * w + out) * n
                        row = (a * 3 + b) * c
                        taps_ref[row : row + c, at : at + n] = y


def backward_operand(plan, own, halo, taps_ref):
    w, n, side, height = plan.cols, plan.lanes, plan.side, plan.height
    c = plan.channels
    lane = lax.broadcasted_iota(jnp.int32, (c, n), 1)
    zero = jnp.zeros((c, n), BF16)
    for g in range(plan.stacks):
        h = halo[g]
        first, last = h["first"], h["last"]
        edge_l = jnp.where((lane >= side) & (lane <= height), h["col_l"], 0.0)
        edge_r = jnp.where((lane < 2 * side) | (lane == n - 1), h["col_r"], 0.0)
        columns = [jnp.where(first, edge_l, h["left"])] + own[g]
        columns += [jnp.where(last, edge_r, h["right"])]
        keep_l = (lane >= side) | jnp.logical_not(first)
        keep_r = (lane < 2 * side) | jnp.logical_not(last)
        for j in range(w + 2):
            for b in range(3):
                y = columns[j] if b == 1 else shift(columns[j], b - 1)
                if j == 0:
                    y = jnp.where(keep_l, y, 0.0)
                if j == w + 1:
                    y = jnp.where(keep_r, y, 0.0)
                y = y.astype(BF16)
                for a in range(3):
                    out = j - 2 + a
                    if 0 <= out < w:
                        at = (g * w + out) * n
                        row = (a * 3 + b) * c
                        taps_ref[row : row + c, at : at + n] = y
        seam_l = first & (lane < side)
        seam_r = last & (lane >= 2 * side) & (lane < height)
        for out in range(w):
            at = (g * w + out) * n
            for b in range(3):
                y = jnp.where(lane == 0, h["top"][out + 2 - b], 0.0).astype(BF16)
                taps_ref[(9 + b) * c : (10 + b) * c, at : at + n] = y
                y = jnp.where(lane == height - 1, h["bottom"][out + 2 - b], 0.0).astype(BF16)
                taps_ref[(12 + b) * c : (13 + b) * c, at : at + n] = y
                y = zero
                if out == 0:
                    y = jnp.where(seam_l, shift(h["row_l"], b - 1), 0.0).astype(BF16)
                taps_ref[(15 + b) * c : (16 + b) * c, at : at + n] = y
                y = zero
                if out == w - 1:
                    y = jnp.where(seam_r, shift(h["row_r"], b - 1), 0.0).astype(BF16)
                taps_ref[(18 + b) * c : (19 + b) * c, at : at + n] = y


def own_columns(plan, ref):
    w, n = plan.cols, plan.lanes
    return [
        [ref[:, (g * w + i) * n : (g * w + i + 1) * n].astype(F32) for i in range(w)]
        for g in range(plan.stacks)
    ]


def middle_kernel(plan, ids_ref, *refs):
    w, n, g_count, c = plan.cols, plan.lanes, plan.stacks, plan.channels
    around, tables, (w_one, w_two), refs = refs[:6], refs[6:10], refs[10:12], refs[12:]
    hidden_ref, pre_grad_ref, mine_ref, theirs_ref, fwd_ref, bwd_ref, sums_ref = refs
    tables = [x[...] for x in tables]
    wide_forward(plan, surroundings(plan, ids_ref, 0, *around, tables), fwd_ref)
    wide_backward(plan, surroundings(plan, ids_ref, 1, *around, tables), bwd_ref)
    pre = jnp.dot(w_one[...], fwd_ref[...], preferred_element_type=F32)
    grad = jnp.dot(w_two[...], bwd_ref[...], preferred_element_type=F32)
    bend = jnp.tanh(GELU_A * (pre + GELU_B * (pre * pre * pre)))
    half = 0.5 * (1.0 + bend)
    slope = half + 0.5 * pre * (1.0 - bend * bend) * (
        GELU_A * (1.0 + (3.0 * GELU_B) * (pre * pre))
    )
    first = ids_ref[0] == 0
    last = ids_ref[0] == plan.tiles - 1
    flat = lax.broadcasted_iota(jnp.int32, pre.shape, 1)
    segment, lane = flat // n, flat % n
    own_end = g_count * w
    left = (segment >= own_end) & ((segment - own_end) % 2 == 0)
    right = (segment >= own_end) & ((segment - own_end) % 2 == 1)
    inside = (lane < plan.height) | (segment == plan.segments - 1)
    inside = inside | (left & first & (lane == plan.height))
    inside = inside | (right & last & (lane == n - 1))
    hidden = jnp.where(inside, pre * half, 0.0).astype(BF16)
    pre_grad = jnp.where(inside, grad * slope, 0.0).astype(BF16)
    hidden_ref[...] = hidden
    pre_grad_ref[...] = pre_grad
    own_end *= n
    terms = product(fwd_ref[:, :own_end], pre_grad[:, :own_end], 1, 1)
    turned = product(bwd_ref[:, :own_end], hidden[:, :own_end], 1, 1)
    tap = [turned[i * c : (i + 1) * c] for i in range(21)]
    for b in range(3):
        tap[b] = tap[b] + tap[9 + b]
        tap[6 + b] = tap[6 + b] + tap[12 + b]
    for a in range(3):
        tap[3 * a] = tap[3 * a] + tap[15 + a]
        tap[3 * a + 2] = tap[3 * a + 2] + tap[18 + a]
    sums_ref[0 : 9 * c, :] = terms
    for i in range(9):
        sums_ref[(9 + i) * c : (10 + i) * c, :] = jnp.transpose(tap[i])
    rest = sums_ref.shape[0] - 18 * c
    if rest:
        sums_ref[18 * c :, :] = jnp.zeros((rest, c), F32)
    near, mid = ids_ref[3], ids_ref[4]
    for d in range(plan.mid):
        spot = jnp.bitwise_xor(mid, d)
        for other, ref in ((0, mine_ref), (1, theirs_ref)):
            at = (jnp.bitwise_xor(near, other) * plan.mid + spot) * plan.piece
            rows = sums_ref[pl.ds(pl.multiple_of(at, 16), plan.piece), :]
            ref[d] = rows.astype(ref.dtype)


def last_kernel(plan, ids_ref, hidden_ref, pre_grad_ref, w_two, w_one, *refs):
    out_ref, back_ref, fwd_ref, bwd_ref = refs
    w, n = plan.cols, plan.lanes
    halo = second_halos(plan, ids_ref, hidden_ref)
    forward_operand(plan, own_columns(plan, hidden_ref), halo, fwd_ref)
    halo = second_halos(plan, ids_ref, pre_grad_ref)
    backward_operand(plan, own_columns(plan, pre_grad_ref), halo, bwd_ref)
    out = jnp.dot(w_two[...], fwd_ref[...], preferred_element_type=F32).astype(BF16)
    back = jnp.dot(w_one[...], bwd_ref[...], preferred_element_type=F32).astype(BF16)
    for g in range(plan.stacks):
        for i in range(w):
            at = (g * w + i) * n
            out_ref[g, i] = out[:, at : at + plan.height]
            back_ref[g, i] = back[:, at : at + plan.height]


def sum_kernel(plan, scale, ids_ref, mine_ref, theirs_ref, sums_ref):
    near, mid = ids_ref[3], ids_ref[4]
    for d in range(plan.mid):
        spot = jnp.bitwise_xor(mid, d)
        for other, ref in ((0, mine_ref), (1, theirs_ref)):
            at = (jnp.bitwise_xor(near, other) * plan.mid + spot) * plan.piece
            sums_ref[pl.ds(pl.multiple_of(at, 16), plan.piece), :] = ref[d].astype(F32) * scale


VMEM = pl.BlockSpec(memory_space=pltpu.VMEM)
SMEM = pl.BlockSpec(memory_space=pltpu.SMEM)


def call(body, ids, inputs, outs, scratch=()):
    return pl.pallas_call(
        body,
        out_shape=outs,
        in_specs=[SMEM] + [VMEM] * len(inputs),
        out_specs=[VMEM] * len(outs),
        scratch_shapes=list(scratch),
        compiler_params=pltpu.CompilerParams(vmem_limit_bytes=48 * 2**20),
    )(ids, *inputs)


def tile_ring(plan, x, step):
    pairs = [(i, i + step) for i in range(plan.tiles) if 0 <= i + step < plan.tiles]
    return lax.ppermute(x, "tile", pairs)


def swap_ends(plan, columns):
    t, f, g = plan.tiles, plan.faces, plan.stacks
    first = lax.axis_index("tile") == 0
    head, tail = columns[:2], columns[plan.cols - 2 :]
    pairs = [((t - 1) * f + i, (i + 1) % f) for i in range(f)]
    pairs += [((i + 1) % f, (t - 1) * f + i) for i in range(f)]
    cross = lax.ppermute(jnp.where(first, head[:, :, 0], tail[:, :, g - 1]), BOTH, pairs)
    if g == 1:
        return cross[:, :, None], cross
    sent = jnp.where(first, head[:, :, 1:], tail[:, :, : g - 1])
    return lax.ppermute(sent, "tile", [(0, t - 1), (t - 1, 0)]), cross


def exchange(plan, columns, blocks):
    left = tile_ring(plan, columns[plan.cols - 2 :], 1)
    right = tile_ring(plan, columns[:2], -1)
    wrap, cross = swap_ends(plan, columns)
    count = plan.tiles * plan.faces
    flat = blocks.reshape((count,) + blocks.shape[2:])
    got = lax.all_to_all(flat, BOTH, 0, 0, tiled=True).reshape(blocks.shape)
    return left, right, wrap, cross, got


def swapped(plan, x, near=0, mid=0, far=0):
    f = plan.faces
    pairs = []
    for i in range(plan.tiles * f):
        tile, face = i // f, i % f
        tile = tile ^ near ^ ((mid // f) << 1) ^ (far << 2)
        pairs.append((i, tile * f + (face ^ (mid % f))))
    return lax.ppermute(x, BOTH, pairs)


def tree_sum(values):
    while len(values) > 1:
        values = [a + b for a, b in zip(values[::2], values[1::2])]
    return values[0]


def sum_all(plan, mine, theirs):
    half = mine + swapped(plan, theirs, near=1).astype(F32)
    short = half.astype(BF16)
    got = [swapped(plan, short[d], mid=d).astype(F32) for d in range(1, plan.mid)]
    piece = tree_sum([half[0]] + got).astype(BF16)
    got = [swapped(plan, piece, far=d) for d in range(1, plan.far)]
    piece = tree_sum([x.astype(F32) for x in [piece] + got]).astype(BF16)
    pieces = [piece] + [swapped(plan, piece, mid=d) for d in range(1, plan.mid)]
    half = jnp.stack(pieces)
    return half, swapped(plan, half, near=1)


def seam_weights(kernel):
    lines = [kernel.reshape(kernel.shape[0], 9, -1), kernel[:, 0], kernel[:, 2]]
    lines += [kernel[:, :, 0], kernel[:, :, 2]]
    return jnp.concatenate(lines, axis=1).reshape(kernel.shape[0], -1)


def on_device(mesh_shape, fields, upstream, kernel_one, kernel_two):
    plan = Plan(mesh_shape, fields.shape)
    c, own, w, n = plan.channels, plan.own, plan.cols, plan.lanes
    g, h = plan.stacks, plan.height
    tile, face = lax.axis_index("tile"), lax.axis_index("face")
    sub = lax.axis_index("sub")
    mid = ((tile >> 1) & 1) * plan.faces + face
    ids = jnp.stack([tile, face, sub, tile & 1, mid]).astype(jnp.int32)
    if mesh_shape["sub"] > 1:
        fields = lax.all_gather(fields, "sub", axis=0, tiled=True)
        upstream = lax.all_gather(upstream, "sub", axis=0, tiled=True)

    both = jnp.stack([fields, upstream]).transpose(3, 0, 2, 1, 4)
    columns = jnp.pad(both, ((0, 0),) * 4 + ((0, n - h),))
    blocks_shape = jax.ShapeDtypeStruct((plan.tiles, plan.faces, plan.block, c), BF16)
    (blocks,) = call(
        functools.partial(first_kernel, plan),
        ids,
        [*plan.send_tables(), columns],
        [blocks_shape],
    )
    halo = exchange(plan, columns, blocks)

    fwd_one = kernel_one.transpose(3, 0, 1, 2).reshape(c, -1)
    bwd_two = seam_weights(kernel_two.transpose(2, 0, 1, 3))
    fwd_two = lax.dynamic_slice_in_dim(kernel_two, sub * own, own, 3)
    fwd_two = fwd_two.transpose(3, 0, 1, 2).reshape(own, -1)
    bwd_one = lax.dynamic_slice_in_dim(kernel_one, sub * own, own, 2)
    bwd_one = seam_weights(bwd_one.transpose(2, 0, 1, 3))

    def taps(width):
        return [pltpu.VMEM((9 * c, width), BF16), pltpu.VMEM((21 * c, width), BF16)]

    piece = (plan.mid, plan.piece, c)
    rows = plan.near * plan.mid * plan.piece
    wide = plan.segments * n
    hidden, pre_grad, mine, theirs = call(
        functools.partial(middle_kernel, plan),
        ids,
        [columns, *halo, *plan.take_tables(), fwd_one, bwd_two],
        [jax.ShapeDtypeStruct((c, wide), BF16)] * 2
        + [jax.ShapeDtypeStruct(piece, F32), jax.ShapeDtypeStruct(piece, BF16)],
        taps(wide) + [pltpu.VMEM((rows, c), F32)],
    )
    mine, theirs = sum_all(plan, mine, theirs)
    out_shape = jax.ShapeDtypeStruct((g, w, own, h), BF16)
    result, fields_grad = call(
        functools.partial(last_kernel, plan),
        ids,
        [hidden, pre_grad, fwd_two, bwd_one],
        [out_shape, out_shape],
        taps(g * w * n),
    )
    scale = 1.0 / (plan.side * 12.0**0.5)
    (sums,) = call(
        functools.partial(sum_kernel, plan, scale),
        ids,
        [mine, theirs],
        [jax.ShapeDtypeStruct((rows, c), F32)],
    )
    grads = []
    for i in range(2):
        grad = sums[9 * c * i : 9 * c * (i + 1)].reshape(3, 3, c, c)
        grads.append(lax.dynamic_slice_in_dim(grad, sub * own, own, 3))
    return (
        result.transpose(2, 0, 1, 3),
        fields_grad.transpose(2, 0, 1, 3),
        grads[0],
        grads[1],
    )


def solution(mesh):
    placed = (P("sub", "face", "tile", "parts"), P("sub", "face", "tile", "parts"), P(), P())
    return jax.shard_map(
        functools.partial(on_device, dict(mesh.shape)),
        mesh=mesh,
        in_specs=placed,
        out_specs=(
            P("sub", "face", "tile", "parts"),
            P("sub", "face", "tile", "parts"),
            P("parts", None, None, "sub"),
            P("parts", None, None, "sub"),
        ),
        check_vma=False,
    )
```

```python
import functools

import jax
import jax.numpy as jnp
import numpy as np
from jax import lax
from jax.experimental import pallas as pl
from jax.experimental.pallas import tpu as pltpu
from jax.sharding import PartitionSpec as P

BOTH = ("tile", "face")
F32 = jnp.float32
BF16 = jnp.bfloat16
GELU_A = 0.7978845608028654
GELU_B = 0.044715


def up_to(value, step):
    return -(-value // step) * step


class Plan:
    def __init__(self, mesh_shape, block):
        self.tiles = mesh_shape["tile"]
        self.faces = mesh_shape["face"]
        self.stacks, self.cols, self.height = block[1:4]
        self.side = self.height // 3
        self.lanes = up_to(self.height + 2, 128)
        self.channels = block[0] * mesh_shape["sub"]
        self.own = block[0]
        w = self.cols
        self.reach = w + 4
        self.line = (0, self.reach)
        self.row = (2 * self.reach, 2 * self.reach + w)
        self.cells = up_to(2 * self.reach + 2 * w, 16)
        self.poles = up_to(2 * 3 * self.stacks, 16)
        self.block = 2 * self.cells + self.poles
        self.kinds = 2 if self.stacks > 1 else 1
        self.segments = self.stacks * (w + 2) + 1
        self.rim = up_to(2 * self.stacks * 8, 1)
        self.near = 2
        self.mid = 2 * self.faces
        self.far = self.tiles // 4
        self.terms = 2 * 9 * self.channels
        self.piece = up_to(-(-self.terms // (self.near * self.mid)), 16)

    def segment(self, stack, slot):
        if 1 <= slot <= self.cols:
            return stack * self.cols + slot - 1
        return self.stacks * self.cols + 2 * stack + (1 if slot else 0)

    def send_tables(self):
        t, k, c = self.tiles, self.kinds, self.cells
        g, w, n = self.stacks, self.cols, self.lanes
        high = self.height - 1
        table = np.zeros((2, t, k, c, g, w, n), np.float32)
        poles = np.zeros((2, self.poles // 2, g, w, n), np.float32)
        for dest in range(t):
            for kind in range(k):
                same = kind == 0 and k == 2
                from_a = 1 if same else 0
                from_b = 0 if same else g - 1
                for e in range(self.reach):
                    for depth in range(2):
                        spot = self.line[depth] + e
                        row = w * dest - 2 + e
                        if 0 <= row:
                            table[0, dest, kind, spot, from_a, depth, row] = 1
                        row = 2 * self.side + w * dest - 2 + e
                        if row <= high:
                            table[1, dest, kind, spot, from_b, w - 1 - depth, row] = 1
                for e in range(w):
                    for depth in range(2):
                        spot = self.row[depth] + e
                        if dest == 0:
                            table[:, dest, kind, spot, from_b, e, depth] = 1
                        if dest == t - 1:
                            table[:, dest, kind, spot, from_a, e, high - depth] = 1
        for stack in range(g):
            for i, (col, row) in enumerate(((0, 0), (1, 0), (0, 1))):
                poles[0, 3 * stack + i, stack, col, row] = 1
                poles[1, 3 * stack + i, stack, w - 1 - col, high - row] = 1
        return (
            jnp.asarray(table.reshape(2, t * k * c, g * w * n), BF16),
            jnp.asarray(poles.reshape(2, -1, g * w * n), BF16),
        )

    def take_tables(self):
        t, c, w, n = self.tiles, self.cells, self.cols, self.lanes
        from_a = np.zeros((t, c, 4, n), np.float32)
        from_b = np.zeros((t, c, 4, n), np.float32)
        for depth in range(2):
            for src in range(t):
                for e in range(w):
                    spot = self.row[depth] + e
                    from_a[src, spot, depth, 2 * self.side + src * w + e] = 1
                    from_b[src, spot, depth, src * w + e] = 1
            for e in range(self.reach):
                from_a[0, self.line[depth] + e, 2 + depth, e] = 1
                from_b[t - 1, self.line[depth] + e, 2 + depth, 8 + e] = 1
        ends = np.zeros((self.reach, n, n), np.float32)
        for e in range(self.reach):
            ends[e, 0, e] = 1
            ends[e, self.height - 1, 8 + e] = 1
        shape = (t * c, 4 * n)
        return (
            jnp.asarray(from_a.reshape(shape), BF16),
            jnp.asarray(from_b.reshape(shape), BF16),
            jnp.asarray(ends.reshape(-1, n), BF16),
            jnp.asarray(np.eye(2 * self.poles, n), BF16),
        )


def first_kernel(plan, ids_ref, table_ref, poles_ref, columns_ref, blocks_ref):
    t, c, g, w = plan.tiles, plan.cells, plan.stacks, plan.cols
    face = ids_ref[1]
    end = jnp.where(ids_ref[0] == plan.tiles - 1, 1, 0)
    poles = []
    for k in range(2):
        flat = jnp.concatenate([columns_ref[i, k, j] for j in range(g) for i in range(w)], axis=1)
        picked = product(table_ref[end], flat, 1, 1).astype(BF16)
        picked = picked.reshape(t, plan.kinds, c, flat.shape[0])
        for dest in range(plan.faces):
            if plan.kinds == 2:
                block = jnp.where(face == dest, picked[:, 0], picked[:, 1])
            else:
                block = picked[:, 0]
            blocks_ref[:, dest, k * c : (k + 1) * c, :] = block
        poles.append(product(poles_ref[end], flat, 1, 1))
    poles = jnp.concatenate(poles, axis=0).astype(BF16)
    for dest in range(plan.faces):
        blocks_ref[:, dest, 2 * c :, :] = jnp.broadcast_to(poles[None], (t,) + poles.shape)


def product(x, y, x_dim, y_dim):
    return lax.dot_general(x, y, (((x_dim,), (y_dim,)), ((), ())), preferred_element_type=F32)


def shift(x, by):
    return pltpu.roll(x, by % x.shape[1], 1)


def surroundings(plan, ids_ref, k, columns_ref, inner_ref, outer_ref, got_ref, tables):
    w, n, c = plan.cols, plan.lanes, plan.cells
    high, g_count = plan.height, plan.stacks
    first = ids_ref[0] == 0
    last = ids_ref[0] == plan.tiles - 1
    even = lax.rem(ids_ref[0], 2) == 0
    face = ids_ref[1]
    after = lax.rem(face + 1, plan.faces)
    before = lax.rem(face + plan.faces - 1, plan.faces)
    across = lax.rem(face + 2 // g_count, plan.faces)
    tab_a, tab_b, tab_ends, tab_eye = tables
    pole_rows = [got_ref[at, across, 2 * c :, :] for at in (0, plan.tiles - 1)]
    poles = product(jnp.concatenate(pole_rows, axis=0), tab_eye, 0, 0)
    shape = (plan.channels, n)
    lane = lax.broadcasted_iota(jnp.int32, shape, 1)
    stacks = []
    line, deep, ends = [jnp.zeros(shape, F32) for _ in range(3)]
    for g in range(g_count):
        face_a = face if g < g_count - 1 else after
        face_b = face if g > 0 else before
        seams = []
        for at, table in ((face_a, tab_a), (face_b, tab_b)):
            rows = got_ref[:, at, k * c : (k + 1) * c, :]
            rows = rows.reshape(plan.tiles * c, rows.shape[-1])
            out = product(rows, table, 0, 0)
            seams.append([out[:, i * n : (i + 1) * n] for i in range(4)])
        line += shift(seams[0][2] + seams[1][2], 16 * g)
        deep += shift(seams[0][3] + seams[1][3], 16 * g)
        raw = [jnp.where(even, outer_ref[i, k, g], inner_ref[i, k, g]) for i in range(2)]
        raw += [columns_ref[i, k, g] for i in range(w)]
        raw += [jnp.where(even, inner_ref[i, k, g], outer_ref[i, k, g]) for i in range(2)]
        ends += shift(product(jnp.concatenate(raw, axis=1), tab_ends, 1, 0), 16 * g)
        raw = [x.astype(F32) for x in raw]
        pole = []
        for at in range(2):
            base = at * plan.poles + k * (plan.poles // 2) + 3 * g
            pole.append([poles[:, base + i : base + i + 1] for i in range(3)])
        stacks.append(
            dict(
                raw=raw,
                row_l=seams[1][:2],
                row_r=seams[0][:2],
                col_l=[shift(x, plan.side) for x in raw[:2]],
                col_r=[shift(x, -plan.side) for x in raw[w + 2 :]],
                north=pole[0],
                south=pole[1],
            )
        )
    spot = lane % 8
    ends = jnp.where(first & (spot < 2), 0.0, ends)
    ends = jnp.where(last & (spot >= w + 2), 0.0, ends)
    rim = dict(line=line, deep=deep, ends=ends, spot=spot, is_top=(lane % 16) < 8)
    return stacks, rim, lane, first, last


def rim_cell(plan, lane, g, bottom, e):
    return lane == 16 * g + 8 * bottom + e


def wide_forward(plan, found, taps_ref):
    stacks, rim, lane, first, last = found
    w, n, side, high, c = plan.cols, plan.lanes, plan.side, plan.height, plan.channels

    def put(a, b, segment, value):
        row = (a * 3 + b) * c
        taps_ref[row : row + c, segment * n : (segment + 1) * n] = value.astype(BF16)

    rows_r = (lane >= 2 * side) & (lane < high)
    for g, h in enumerate(stacks):
        raw = h["raw"]
        x = []
        for q in range(w + 4):
            at = 16 * g + q
            y = jnp.where(lane == high, rim["line"][:, at + 8 : at + 9], raw[q])
            x.append(jnp.where(lane == n - 1, rim["line"][:, at : at + 1], y))
        edge_l = jnp.where(lane < side, h["row_l"][0], jnp.where(lane < high, h["col_l"][1], 0.0))
        edge_r = jnp.where(lane < 2 * side, h["col_r"][0], jnp.where(rows_r, h["row_r"][0], 0.0))
        x[0] = jnp.where(first, h["col_l"][0], x[0])
        x[1] = jnp.where(first, edge_l, x[1])
        x[w + 2] = jnp.where(last, edge_r, x[w + 2])
        x[w + 3] = jnp.where(last, h["col_r"][1], x[w + 3])
        moved = [[shift(y, 1 - b) if b != 1 else y for b in range(3)] for y in x]
        own0, own1, own30, own31 = raw[2], raw[3], raw[w], raw[w + 1]
        north, south = h["north"], h["south"]
        turned_l = [jnp.where(lane < side, own0, 0.0)]
        turned_r = []
        for d in range(2):
            y = jnp.where(lane < side, h["row_l"][d], shift(own0, -d))
            turned_l.append(jnp.where(lane == n - 1, north[d], y))
            y = jnp.where(rows_r, h["row_r"][d], shift(own31, d))
            turned_r.append(jnp.where(lane == high, south[d], y))
        turned_l[1:] = [
            jnp.where((lane > side) & (lane < n - 1), 0.0, y) for y in turned_l[1:]
        ]
        turned_r = [turned_r[1], turned_r[0], jnp.where(rows_r, own31, 0.0)]
        for b in range(3):
            for a in range(3):
                for j in range(1, w + 1):
                    put(a, b, plan.segment(g, j), moved[j + a][b])
                y = shift(h["col_l"][1], 1 - b) if a == 1 else moved[a][b]
                y = jnp.where(lane < side, shift(turned_l[b], 1 - a), y)
                if b == 0:
                    over = shift(own0, 2 - a) if a < 2 else 0.0
                    y = jnp.where(lane == side, over, y)
                elif a == 2:
                    y = jnp.where(lane == high, shift((own0, own1)[b - 1], 1), y)
                    if b == 2:
                        y = jnp.where(lane == high - 1, own0, y)
                put(a, b, plan.segment(g, 0), jnp.where(first, y, moved[a][b]))
                y = shift(h["col_r"][0], 1 - b) if a == 1 else moved[w + 1 + a][b]
                y = jnp.where(rows_r, shift(turned_r[b], 1 - a), y)
                if b == 2:
                    over = shift(own31, -a) if a > 0 else 0.0
                    y = jnp.where(lane == 2 * side - 1, over, y)
                if a == 0:
                    if b == 0:
                        y = jnp.where(lane == 0, own31, y)
                    y = jnp.where(lane == n - 1, shift(own30 if b == 0 else own31, -1), y)
                put(a, b, plan.segment(g, w + 1), jnp.where(last, y, moved[w + 1 + a][b]))
    line, deep, ends = rim["line"], rim["deep"], rim["ends"]
    is_top, spot = rim["is_top"], rim["spot"]
    ends = jnp.where(last & is_top & (spot == w + 2), shift(ends, 1), ends)
    ends = jnp.where(first & jnp.logical_not(is_top) & (spot == 1), shift(ends, -1), ends)
    for g, h in enumerate(stacks):
        north = first & rim_cell(plan, lane, g, 0, 1)
        south = last & rim_cell(plan, lane, g, 1, w + 2)
        line = jnp.where(north, h["north"][0], line)
        deep = jnp.where(north, h["north"][2], deep)
        line = jnp.where(south, h["south"][0], line)
        deep = jnp.where(south, h["south"][2], deep)
    by_a = (jnp.where(is_top, ends, deep), line, jnp.where(is_top, deep, ends))
    for a in range(3):
        for b in range(3):
            put(a, b, plan.segments - 1, shift(by_a[a], -b) if b else by_a[a])


def wide_backward(plan, found, taps_ref):
    stacks, rim, lane, first, last = found
    w, n, side, high, c = plan.cols, plan.lanes, plan.side, plan.height, plan.channels

    def put(row, segment, value):
        taps_ref[row * c : (row + 1) * c, segment * n : (segment + 1) * n] = value.astype(BF16)

    zero = jnp.zeros(lane.shape, F32)
    rows_l = lane < side
    rows_r = (lane >= 2 * side) & (lane < high)
    for g, h in enumerate(stacks):
        raw = h["raw"]
        z = list(raw)
        edge_l = jnp.where((lane >= side) & (lane <= high), h["col_l"][1], 0.0)
        edge_r = jnp.where((lane < 2 * side) | (lane == n - 1), h["col_r"][0], 0.0)
        z[1] = jnp.where(first, edge_l, z[1])
        z[w + 2] = jnp.where(last, edge_r, z[w + 2])
        moved = [[shift(y, b - 1) if b != 1 else y for b in range(3)] for y in z]
        keep_l = (lane >= side) | jnp.logical_not(first)
        keep_r = (lane < 2 * side) | jnp.logical_not(last)
        own0, own1, own30, own31 = raw[2], raw[3], raw[w], raw[w + 1]
        north, south = h["north"], h["south"]
        line_l = [jnp.where(rows_l, y, 0.0) for y in h["row_l"]]
        line_r = [jnp.where(rows_r, y, 0.0) for y in h["row_r"]]
        line_l = [line_l[1], line_l[0], zero]
        line_r = [zero, line_r[0], line_r[1]]
        keep = (lane >= side) & (lane <= high + 1)
        deep_l = [zero] + [jnp.where(keep, h["col_l"][i], 0.0) for i in (1, 0)]
        keep = (lane < 2 * side) | (lane >= n - 2)
        deep_r = [jnp.where(keep, h["col_r"][i], 0.0) for i in (1, 0)] + [zero]
        for b in range(3):
            for a in range(3):
                tap = a * 3 + b
                for j in range(1, w + 1):
                    y = moved[j + 2 - a][b]
                    if j == 1 and a == 2:
                        y = jnp.where(keep_l, y, 0.0)
                    if j == w and a == 0:
                        y = jnp.where(keep_r, y, 0.0)
                    put(tap, plan.segment(g, j), y)
                y = jnp.where(rows_l, shift(line_l[b], a - 1), shift(deep_l[a], b - 1))
                if a == 0:
                    y = jnp.where(lane == side - 1, shift(own0, b - 2), y)
                    y = jnp.where(lane == side, shift(own0, b), y)
                put(tap, plan.segment(g, 0), jnp.where(first, y, moved[2 - a][b]))
                y = jnp.where(rows_r, shift(line_r[b], a - 1), shift(deep_r[a], b - 1))
                if a == 2:
                    y = jnp.where(lane == 2 * side - 1, shift(own31, b - 2), y)
                    y = jnp.where(lane == 2 * side, shift(own31, b), y)
                put(tap, plan.segment(g, w + 1), jnp.where(last, y, moved[w + 3 - a][b]))
        for j in range(w + 2):
            segment = plan.segment(g, j)
            for b in range(3):
                at = 16 * g + j + 2 - b
                top = jnp.where(lane == 0, rim["line"][:, at : at + 1], 0.0)
                bottom = jnp.where(lane == high - 1, rim["line"][:, at + 8 : at + 9], 0.0)
                left = right = zero
                if j == 0:
                    own = jnp.where(lane < high, shift(own0, b - 1), 0.0)
                    top = jnp.where(first, own, top)
                    bottom = jnp.where(first, 0.0, bottom)
                    if b < 2:
                        left = jnp.where(first & (lane == 0), north[1 - b], 0.0)
                        right = jnp.where(first & (lane == high), shift((own1, own0)[b], 1), 0.0)
                if j == 1:
                    left = jnp.where(first & rows_l, shift(line_l[1], b - 1), 0.0)
                if j == w:
                    right = jnp.where(last & rows_r, shift(line_r[1], b - 1), 0.0)
                if j == w + 1:
                    own = jnp.where(lane < high, shift(own31, b - 1), 0.0)
                    bottom = jnp.where(last, own, bottom)
                    top = jnp.where(last, 0.0, top)
                    if b > 0:
                        over = shift((own31, own30)[b - 1], -1)
                        left = jnp.where(last & (lane == n - 1), over, 0.0)
                        right = jnp.where(last & (lane == high - 1), south[b - 1], 0.0)
                for i, y in enumerate((top, bottom, left, right)):
                    put(9 + 3 * i + b, segment, y)
    line, deep, ends = rim["line"], rim["deep"], rim["ends"]
    is_top = rim["is_top"]
    tops = [jnp.where(is_top, y, 0.0) for y in (deep, ends)]
    bottoms = [jnp.where(is_top, 0.0, y) for y in (deep, ends)]
    by_a = (tops[0], line, bottoms[0])
    segment = plan.segments - 1
    for b in range(3):
        for a in range(3):
            put(a * 3 + b, segment, shift(by_a[a], b - 2))
        top = bottom = zero
        for g, h in enumerate(stacks):
            if b < 2:
                over = h["north"][2 * (1 - b)]
                top = jnp.where(first & rim_cell(plan, lane, g, 0, 1), over, top)
            if b > 0:
                over = h["south"][2 * (b - 1)]
                bottom = jnp.where(last & rim_cell(plan, lane, g, 1, w), over, bottom)
        put(9 + b, segment, top)
        put(12 + b, segment, bottom)
        put(15 + b, segment, shift(tops[1], b - 2))
        put(18 + b, segment, shift(bottoms[1], b - 2))


def second_halos(plan, ids_ref, ref):
    w, n, high, side = plan.cols, plan.lanes, plan.height, plan.side
    first = ids_ref[0] == 0
    last = ids_ref[0] == plan.tiles - 1
    start = (plan.segments - 1) * n
    rim = ref[:, start : start + n].astype(F32)
    lane = lax.broadcasted_iota(jnp.int32, rim.shape, 1)
    result = []
    for g in range(plan.stacks):
        left, right = [
            ref[:, plan.segment(g, j) * n : (plan.segment(g, j) + 1) * n].astype(F32)
            for j in (0, w + 1)
        ]
        top = [rim[:, 16 * g + e : 16 * g + e + 1] for e in range(w + 2)]
        bottom = [rim[:, 16 * g + 8 + e : 16 * g + 9 + e] for e in range(w + 2)]
        top[0] = jnp.where(first, 0.0, top[0])
        bottom[0] = jnp.where(first, left[:, high - 1 : high], bottom[0])
        top[w + 1] = jnp.where(last, right[:, 0:1], top[w + 1])
        bottom[w + 1] = jnp.where(last, 0.0, bottom[w + 1])
        result.append(
            dict(
                first=first,
                last=last,
                left=left,
                right=right,
                row_l=jnp.where(lane < side, left, 0.0),
                row_r=jnp.where((lane >= 2 * side) & (lane < high), right, 0.0),
                col_l=left,
                col_r=right,
                top=top,
                bottom=bottom,
            )
        )
    return result


def forward_operand(plan, own, halo, taps_ref):
    w, n, side, height = plan.cols, plan.lanes, plan.side, plan.height
    c = plan.channels
    lane = lax.broadcasted_iota(jnp.int32, (c, n), 1)
    for g in range(plan.stacks):
        h = halo[g]
        edge_l = jnp.where(lane < side, h["row_l"], jnp.where(lane < height, h["col_l"], 0.0))
        edge_r = jnp.where(
            lane < 2 * side, h["col_r"], jnp.where(lane < height, h["row_r"], 0.0)
        )
        columns = [h["left"]] + own[g] + [h["right"]]
        for j in range(w + 2):
            x = jnp.where(lane == height, h["bottom"][j], columns[j])
            x = jnp.where(lane == n - 1, h["top"][j], x)
            if j == 0:
                x = jnp.where(h["first"], edge_l, x)
            if j == w + 1:
                x = jnp.where(h["last"], edge_r, x)
            for b in range(3):
                y = (x if b == 1 else shift(x, 1 - b)).astype(BF16)
                for a in range(3):
                    out = j - a
                    if 0 <= out < w:
                        at = (g * w + out) * n
                        row = (a * 3 + b) * c
                        taps_ref[row : row + c, at : at + n] = y


def backward_operand(plan, own, halo, taps_ref):
    w, n, side, height = plan.cols, plan.lanes, plan.side, plan.height
    c = plan.channels
    lane = lax.broadcasted_iota(jnp.int32, (c, n), 1)
    zero = jnp.zeros((c, n), BF16)
    for g in range(plan.stacks):
        h = halo[g]
        first, last = h["first"], h["last"]
        edge_l = jnp.where((lane >= side) & (lane <= height), h["col_l"], 0.0)
        edge_r = jnp.where((lane < 2 * side) | (lane == n - 1), h["col_r"], 0.0)
        columns = [jnp.where(first, edge_l, h["left"])] + own[g]
        columns += [jnp.where(last, edge_r, h["right"])]
        keep_l = (lane >= side) | jnp.logical_not(first)
        keep_r = (lane < 2 * side) | jnp.logical_not(last)
        for j in range(w + 2):
            for b in range(3):
                y = columns[j] if b == 1 else shift(columns[j], b - 1)
                if j == 0:
                    y = jnp.where(keep_l, y, 0.0)
                if j == w + 1:
                    y = jnp.where(keep_r, y, 0.0)
                y = y.astype(BF16)
                for a in range(3):
                    out = j - 2 + a
                    if 0 <= out < w:
                        at = (g * w + out) * n
                        row = (a * 3 + b) * c
                        taps_ref[row : row + c, at : at + n] = y
        seam_l = first & (lane < side)
        seam_r = last & (lane >= 2 * side) & (lane < height)
        for out in range(w):
            at = (g * w + out) * n
            for b in range(3):
                y = jnp.where(lane == 0, h["top"][out + 2 - b], 0.0).astype(BF16)
                taps_ref[(9 + b) * c : (10 + b) * c, at : at + n] = y
                y = jnp.where(lane == height - 1, h["bottom"][out + 2 - b], 0.0).astype(BF16)
                taps_ref[(12 + b) * c : (13 + b) * c, at : at + n] = y
                y = zero
                if out == 0:
                    y = jnp.where(seam_l, shift(h["row_l"], b - 1), 0.0).astype(BF16)
                taps_ref[(15 + b) * c : (16 + b) * c, at : at + n] = y
                y = zero
                if out == w - 1:
                    y = jnp.where(seam_r, shift(h["row_r"], b - 1), 0.0).astype(BF16)
                taps_ref[(18 + b) * c : (19 + b) * c, at : at + n] = y


def seam_weights(kernel_ref):
    order = list(range(9)) + [0, 1, 2, 6, 7, 8, 0, 3, 6, 2, 5, 8]
    return jnp.concatenate([kernel_ref[tap] for tap in order], axis=1)


def own_columns(plan, ref):
    w, n = plan.cols, plan.lanes
    return [
        [ref[:, (g * w + i) * n : (g * w + i + 1) * n].astype(F32) for i in range(w)]
        for g in range(plan.stacks)
    ]


def middle_kernel(plan, ids_ref, *refs):
    w, n, g_count, c = plan.cols, plan.lanes, plan.stacks, plan.channels
    around, tables, (w_one, w_two), refs = refs[:4], refs[4:8], refs[8:10], refs[10:]
    hidden_ref, pre_grad_ref, mine_ref, theirs_ref, fwd_ref, bwd_ref, sums_ref = refs
    tables = [x[...] for x in tables]
    wide_forward(plan, surroundings(plan, ids_ref, 0, *around, tables), fwd_ref)
    wide_backward(plan, surroundings(plan, ids_ref, 1, *around, tables), bwd_ref)
    pre = product(w_one[...], fwd_ref[...], 0, 0)
    grad = product(seam_weights(w_two), bwd_ref[...], 1, 0)
    bend = jnp.tanh(GELU_A * (pre + GELU_B * (pre * pre * pre)))
    half = 0.5 * (1.0 + bend)
    slope = half + 0.5 * pre * (1.0 - bend * bend) * (
        GELU_A * (1.0 + (3.0 * GELU_B) * (pre * pre))
    )
    first = ids_ref[0] == 0
    last = ids_ref[0] == plan.tiles - 1
    flat = lax.broadcasted_iota(jnp.int32, pre.shape, 1)
    segment, lane = flat // n, flat % n
    own_end = g_count * w
    left = (segment >= own_end) & ((segment - own_end) % 2 == 0)
    right = (segment >= own_end) & ((segment - own_end) % 2 == 1)
    inside = (lane < plan.height) | (segment == plan.segments - 1)
    inside = inside | (left & first & (lane == plan.height))
    inside = inside | (right & last & (lane == n - 1))
    hidden = jnp.where(inside, pre * half, 0.0).astype(BF16)
    pre_grad = jnp.where(inside, grad * slope, 0.0).astype(BF16)
    hidden_ref[...] = hidden
    pre_grad_ref[...] = pre_grad
    own_end *= n
    terms = product(fwd_ref[:, :own_end], pre_grad[:, :own_end], 1, 1)
    turned = product(bwd_ref[:, :own_end], hidden[:, :own_end], 1, 1)
    tap = [turned[i * c : (i + 1) * c] for i in range(21)]
    for b in range(3):
        tap[b] = tap[b] + tap[9 + b]
        tap[6 + b] = tap[6 + b] + tap[12 + b]
    for a in range(3):
        tap[3 * a] = tap[3 * a] + tap[15 + a]
        tap[3 * a + 2] = tap[3 * a + 2] + tap[18 + a]
    sums_ref[0 : 9 * c, :] = terms
    for i in range(9):
        sums_ref[(9 + i) * c : (10 + i) * c, :] = jnp.transpose(tap[i])
    rest = sums_ref.shape[0] - 18 * c
    if rest:
        sums_ref[18 * c :, :] = jnp.zeros((rest, c), F32)
    near, mid = ids_ref[3], ids_ref[4]
    for d in range(plan.mid):
        spot = jnp.bitwise_xor(mid, d)
        for other, ref in ((0, mine_ref), (1, theirs_ref)):
            at = (jnp.bitwise_xor(near, other) * plan.mid + spot) * plan.piece
            rows = sums_ref[pl.ds(pl.multiple_of(at, 16), plan.piece), :]
            ref[d] = rows.astype(ref.dtype)


def last_kernel(plan, ids_ref, hidden_ref, pre_grad_ref, w_two, w_one, *refs):
    out_ref, back_ref, fwd_ref, bwd_ref = refs
    w, n = plan.cols, plan.lanes
    halo = second_halos(plan, ids_ref, hidden_ref)
    forward_operand(plan, own_columns(plan, hidden_ref), halo, fwd_ref)
    halo = second_halos(plan, ids_ref, pre_grad_ref)
    backward_operand(plan, own_columns(plan, pre_grad_ref), halo, bwd_ref)
    out = product(w_two[...], fwd_ref[...], 0, 0).astype(BF16)
    back = product(seam_weights(w_one), bwd_ref[...], 1, 0).astype(BF16)
    for g in range(plan.stacks):
        for i in range(w):
            at = (g * w + i) * n
            out_ref[:, g, i, :] = out[:, at : at + plan.height]
            back_ref[:, g, i, :] = back[:, at : at + plan.height]


def sum_kernel(plan, scale, ids_ref, mine_ref, theirs_ref, one_ref, two_ref, sums_ref):
    near, mid = ids_ref[3], ids_ref[4]
    for d in range(plan.mid):
        spot = jnp.bitwise_xor(mid, d)
        for other, ref in ((0, mine_ref), (1, theirs_ref)):
            at = (jnp.bitwise_xor(near, other) * plan.mid + spot) * plan.piece
            sums_ref[pl.ds(pl.multiple_of(at, 16), plan.piece), :] = ref[d].astype(F32) * scale
    rows = one_ref.shape[0]
    one_ref[...] = sums_ref[:rows]
    two_ref[...] = sums_ref[rows : 2 * rows]


VMEM = pl.BlockSpec(memory_space=pltpu.VMEM)
SMEM = pl.BlockSpec(memory_space=pltpu.SMEM)


def call(body, ids, inputs, outs, scratch=()):
    return pl.pallas_call(
        body,
        out_shape=outs,
        in_specs=[SMEM] + [VMEM] * len(inputs),
        out_specs=[VMEM] * len(outs),
        scratch_shapes=list(scratch),
        compiler_params=pltpu.CompilerParams(vmem_limit_bytes=48 * 2**20),
    )(ids, *inputs)


def end_stacks(plan, columns):
    t, f = plan.tiles, plan.faces
    first = lax.axis_index("tile") == 0
    sent = jnp.where(first, columns[:2, :, 0], columns[plan.cols - 2 :, :, plan.stacks - 1])
    pairs = [((t - 1) * f + i, (t - 1) * f + (i + 1) % f) for i in range(f)]
    pairs += [((i + 1) % f, i) for i in range(f)]
    return lax.ppermute(sent, BOTH, pairs)


def pair_up(plan, columns, passed):
    t, g = plan.tiles, plan.stacks
    tile = lax.axis_index("tile")
    even = tile % 2 == 0
    head, tail = columns[:2], columns[plan.cols - 2 :]
    inner = jnp.where(even, tail, head)
    outer = jnp.where(even, head, tail)
    passed = passed[:, :, None]
    to_last = jnp.concatenate([head[:, :, 1:], passed], axis=2)
    to_first = jnp.concatenate([passed, tail[:, :, : g - 1]], axis=2)
    outer = jnp.where(tile == 0, to_last, jnp.where(tile == t - 1, to_first, outer))
    inner = lax.ppermute(inner, "tile", [(i, i ^ 1) for i in range(t)])
    outer = lax.ppermute(outer, "tile", [(i, ((i + 1) ^ 1) - 1 if i else t - 1) for i in range(t - 1)] + [(t - 1, 0)])
    return inner, outer


def spread_blocks(plan, blocks):
    count = plan.tiles * plan.faces
    flat = blocks.reshape((count,) + blocks.shape[2:])
    return lax.all_to_all(flat, BOTH, 0, 0, tiled=True).reshape(blocks.shape)


def swapped(plan, x, near=0, mid=0, far=0):
    f = plan.faces
    pairs = []
    for i in range(plan.tiles * f):
        tile, face = i // f, i % f
        tile = tile ^ near ^ ((mid // f) << 1) ^ (far << 2)
        pairs.append((i, tile * f + (face ^ (mid % f))))
    return lax.ppermute(x, BOTH, pairs)


def tree_sum(values):
    while len(values) > 1:
        values = [a + b for a, b in zip(values[::2], values[1::2])]
    return values[0]


def sum_all(plan, mine, theirs, beside):
    half = mine + swapped(plan, theirs, near=1).astype(F32)
    short = half.astype(BF16)
    got = [swapped(plan, short[d], mid=d) for d in range(1, plan.mid)]
    got, beside = lax.optimization_barrier((got, beside))
    piece = tree_sum([half[0]] + [x.astype(F32) for x in got]).astype(BF16)
    got = [swapped(plan, piece, far=d) for d in range(1, plan.far)]
    piece = tree_sum([x.astype(F32) for x in [piece] + got]).astype(BF16)
    pieces = [piece] + [swapped(plan, piece, mid=d) for d in range(1, plan.mid)]
    half = jnp.stack(pieces)
    return half, swapped(plan, half, near=1), beside


def on_device(mesh_shape, fields, upstream, kernel_one, kernel_two):
    plan = Plan(mesh_shape, fields.shape)
    c, own, w, n = plan.channels, plan.own, plan.cols, plan.lanes
    g, h = plan.stacks, plan.height
    tile, face = lax.axis_index("tile"), lax.axis_index("face")
    sub = lax.axis_index("sub")
    mid = ((tile >> 1) & 1) * plan.faces + face
    ids = jnp.stack([tile, face, sub, tile & 1, mid]).astype(jnp.int32)
    if mesh_shape["sub"] > 1:
        fields = lax.all_gather(fields, "sub", axis=0, tiled=True)
        upstream = lax.all_gather(upstream, "sub", axis=0, tiled=True)

    both = jnp.stack([fields, upstream]).transpose(3, 0, 2, 1, 4)
    columns = jnp.pad(both, ((0, 0),) * 4 + ((0, n - h),))
    blocks_shape = jax.ShapeDtypeStruct((plan.tiles, plan.faces, plan.block, c), BF16)
    (blocks,) = call(
        functools.partial(first_kernel, plan),
        ids,
        [*plan.send_tables(), columns],
        [blocks_shape],
    )
    passed = end_stacks(plan, columns)
    got = spread_blocks(plan, blocks)
    sent, passed, _ = lax.optimization_barrier((columns, passed, blocks))
    halo = (*pair_up(plan, sent, passed), got)

    fwd_one = kernel_one.reshape(9 * c, c)
    bwd_two = kernel_two.reshape(9, c, c)
    fwd_two = lax.dynamic_slice_in_dim(kernel_two, sub * own, own, 3).reshape(9 * c, own)
    bwd_one = lax.dynamic_slice_in_dim(kernel_one, sub * own, own, 2).reshape(9, own, c)

    def taps(width):
        return [pltpu.VMEM((9 * c, width), BF16), pltpu.VMEM((21 * c, width), BF16)]

    piece = (plan.mid, plan.piece, c)
    rows = plan.near * plan.mid * plan.piece
    wide = plan.segments * n
    hidden, pre_grad, mine, theirs = call(
        functools.partial(middle_kernel, plan),
        ids,
        [columns, *halo, *plan.take_tables(), fwd_one, bwd_two],
        [jax.ShapeDtypeStruct((c, wide), BF16)] * 2
        + [jax.ShapeDtypeStruct(piece, F32), jax.ShapeDtypeStruct(piece, BF16)],
        taps(wide) + [pltpu.VMEM((rows, c), F32)],
    )
    out_shape = jax.ShapeDtypeStruct((own, g, w, h), BF16)
    beside = call(
        functools.partial(last_kernel, plan),
        ids,
        [hidden, pre_grad, fwd_two, bwd_one],
        [out_shape, out_shape],
        taps(g * w * n),
    )
    mine, theirs, (result, fields_grad) = sum_all(plan, mine, theirs, list(beside))
    scale = 1.0 / (plan.side * 12.0**0.5)
    sums = call(
        functools.partial(sum_kernel, plan, scale),
        ids,
        [mine, theirs],
        [jax.ShapeDtypeStruct((9 * c, c), F32)] * 2,
        [pltpu.VMEM((rows, c), F32)],
    )
    grads = []
    for i in range(2):
        grad = sums[i].reshape(3, 3, c, c)
        grads.append(lax.dynamic_slice_in_dim(grad, sub * own, own, 3))
    return (
        result,
        fields_grad,
        grads[0],
        grads[1],
    )


def solution(mesh):
    placed = (P("sub", "face", "tile", "parts"), P("sub", "face", "tile", "parts"), P(), P())
    return jax.shard_map(
        functools.partial(on_device, dict(mesh.shape)),
        mesh=mesh,
        in_specs=placed,
        out_specs=(
            P("sub", "face", "tile", "parts"),
            P("sub", "face", "tile", "parts"),
            P("parts", None, None, "sub"),
            P("parts", None, None, "sub"),
        ),
        check_vma=False,
    )
```

```python
import functools

import jax
import jax.numpy as jnp
import numpy as np
from jax import lax
from jax.experimental import pallas as pl
from jax.experimental.pallas import tpu as pltpu
from jax.sharding import PartitionSpec as P

BOTH = ("tile", "face")
F32 = jnp.float32
BF16 = jnp.bfloat16
GELU_A = 0.7978845608028654
GELU_B = 0.044715


def up_to(value, step):
    return -(-value // step) * step


class Plan:
    def __init__(self, mesh_shape, block):
        self.tiles = mesh_shape["tile"]
        self.faces = mesh_shape["face"]
        self.stacks, self.cols, self.height = block[1:4]
        self.side = self.height // 3
        self.lanes = up_to(self.height + 2, 128)
        self.channels = block[0] * mesh_shape["sub"]
        self.own = block[0]
        w = self.cols
        assert w == 2
        self.reach = w + 4
        self.cells = 2 * self.reach
        self.block = 2 * self.cells
        self.kinds = 2 if self.stacks > 1 else 1
        self.segments = self.stacks * (w + 2) + 1
        self.near = 2
        self.mid = 2 * self.faces
        self.far = self.tiles // 4
        self.terms = 2 * 9 * self.channels
        self.wide = self.channels
        rest = -self.channels % 128
        self.folds = 1
        if rest and self.channels % rest == 0 and self.terms % (8 * (self.channels // rest + 1)) == 0:
            self.folds = self.channels // rest + 1
            self.wide = self.channels + rest
        self.fold_rows = self.terms // self.folds
        packed = self.fold_rows * max(self.folds - 1, 1)
        self.piece = up_to(-(-packed // (self.near * self.mid)), 16)

    def segment(self, stack, slot):
        if 1 <= slot <= self.cols:
            return stack * self.cols + slot - 1
        return self.stacks * self.cols + 2 * stack + (1 if slot else 0)

    def spot(self, depth, e):
        return depth * self.reach + e

    def send_table(self):
        t, k, c = self.tiles, self.kinds, self.block
        g, w, n = self.stacks, self.cols, self.lanes
        high = self.height - 1
        table = np.full((3, t, k, c), -1, np.int32)
        for dest in range(t):
            for kind in range(k):
                same = kind == 0 and k == 2
                from_a = 1 if same else 0
                from_b = 0 if same else g - 1

                def cell(stack, col, row):
                    return (stack * w + col) * n + row

                for depth in range(2):
                    for e in range(self.reach):
                        at = self.spot(depth, e)
                        row = w * dest - 2 + e
                        if 0 <= row:
                            table[0, dest, kind, at] = cell(from_a, depth, row)
                        row = 2 * self.side + w * dest - 2 + e
                        if row <= high:
                            table[2, dest, kind, at] = cell(from_b, w - 1 - depth, row)
                    for e in range(w):
                        if dest == 0:
                            table[:2, dest, kind, self.spot(depth, e)] = cell(from_b, e, depth)
                        if dest == t - 1:
                            at = self.spot(depth, w + 2 + e)
                            table[1:, dest, kind, at] = cell(from_a, e, high - depth)
        return jnp.asarray(table.reshape(3, 1, -1))

    def take_tables(self):
        t, c, w, n = self.tiles, self.block, self.cols, self.lanes
        from_a = np.zeros((t, 2, self.cells, 2, 4, n), np.float32)
        from_b = np.zeros((t, 2, self.cells, 2, 4, n), np.float32)
        for depth in range(2):
            for k in range(2):
                for src in range(t):
                    for e in range(w):
                        if src > 0:
                            at = self.spot(depth, w + 2 + e)
                            from_a[src, k, at, k, depth, 2 * self.side + src * w + e] = 1
                        if src < t - 1:
                            from_b[src, k, self.spot(depth, e), k, depth, src * w + e] = 1
                for e in range(self.reach):
                    at = self.spot(depth, e)
                    from_a[0, k, at, k, 2 + depth, e] = 1
                    from_b[t - 1, k, at, k, 2 + depth, 8 + e] = 1
        ends = np.zeros((self.reach, n, n), np.float32)
        for e in range(self.reach):
            ends[e, 0, e] = 1
            ends[e, self.height - 1, 8 + e] = 1
        shape = (t * c, 8 * n)
        return (
            jnp.asarray(from_a.reshape(shape), BF16),
            jnp.asarray(from_b.reshape(shape), BF16),
            jnp.asarray(ends.reshape(-1, n), BF16),
        )


def first_kernel(plan, ids_ref, table_ref, columns_ref, blocks_ref):
    t, c, g, w = plan.tiles, plan.block, plan.stacks, plan.cols
    face = ids_ref[1]
    flat = [
        jnp.concatenate([columns_ref[i, k, j] for j in range(g) for i in range(w)], axis=1)
        for k in range(2)
    ]
    wanted = table_ref[ids_ref[5]]
    cell = lax.broadcasted_iota(jnp.int32, (flat[0].shape[1], wanted.shape[1]), 0)
    pick = jnp.where(cell == wanted, 1.0, 0.0).astype(BF16)
    picked = [jnp.transpose(product(x, pick, 1, 0)) for x in flat]
    both = picked[0] + pltpu.roll(picked[1], plan.cells, 0)
    both = both.reshape(t, plan.kinds, c, both.shape[-1])
    for dest in range(plan.faces):
        if plan.kinds == 2:
            block = jnp.where(face == dest, both[:, 0], both[:, 1])
        else:
            block = both[:, 0]
        blocks_ref[:, dest] = block.astype(BF16)


def product(x, y, x_dim, y_dim):
    return lax.dot_general(x, y, (((x_dim,), (y_dim,)), ((), ())), preferred_element_type=F32)


def shift(x, by):
    return pltpu.roll(x, by % x.shape[1], 1)


def seam_cells(plan, ids_ref, got_ref, tab_a, tab_b):
    face = ids_ref[1]
    after = lax.rem(face + 1, plan.faces)
    before = lax.rem(face + plan.faces - 1, plan.faces)
    result = []
    for g in range(plan.stacks):
        face_a = face if g < plan.stacks - 1 else after
        face_b = face if g > 0 else before
        pair = []
        for at, table in ((face_a, tab_a), (face_b, tab_b)):
            rows = got_ref[:, at].astype(F32)
            rows = rows.reshape(plan.tiles * plan.block, rows.shape[-1])
            pair.append(product(rows.astype(BF16), table[...], 0, 0))
        result.append(pair)
    return result


def surroundings(plan, ids_ref, k, columns_ref, inner_ref, outer_ref, across_ref, seams_of, tab_ends):
    w, n, side = plan.cols, plan.lanes, plan.side
    high, g_count = plan.height, plan.stacks
    first = ids_ref[0] == 0
    last = ids_ref[0] == plan.tiles - 1
    even = lax.rem(ids_ref[0], 2) == 0
    shape = (plan.channels, n)
    lane = lax.broadcasted_iota(jnp.int32, shape, 1)
    stacks = []
    line, deep, ends = [jnp.zeros(shape, F32) for _ in range(3)]
    for g in range(g_count):
        start = 4 * k * n
        seams = [
            [x[:, start + i * n : start + (i + 1) * n] for i in range(4)] for x in seams_of[g]
        ]
        line += shift(seams[0][2] + seams[1][2], 16 * g)
        deep += shift(seams[0][3] + seams[1][3], 16 * g)
        raw = [jnp.where(even, outer_ref[i, k, g], inner_ref[i, k, g]) for i in range(2)]
        raw += [columns_ref[i, k, g] for i in range(w)]
        raw += [jnp.where(even, inner_ref[i, k, g], outer_ref[i, k, g]) for i in range(2)]
        ends += shift(product(jnp.concatenate(raw, axis=1), tab_ends[...], 1, 0), 16 * g)
        raw = [x.astype(F32) for x in raw]
        for d in range(2):
            for i in range(2):
                here = lane == side - 2 + i
                seams[1][d] = jnp.where(here, shift(raw[i], side - 2 + i - d), seams[1][d])
                here = lane == 2 * side + i
                by = 2 * side + i - (high - 1 - d)
                seams[0][d] = jnp.where(here, shift(raw[w + 2 + i], by), seams[0][d])
        pole = [across_ref[i, k, g].astype(F32) for i in range(2)]
        north = [pole[0][:, :1], pole[1][:, :1], pole[0][:, 1:2]]
        south = [pole[1][:, high - 1 : high], pole[0][:, high - 1 : high]]
        south.append(pole[1][:, high - 2 : high - 1])
        stacks.append(
            dict(
                raw=raw,
                row_l=seams[1][:2],
                row_r=seams[0][:2],
                col_l=[shift(x, plan.side) for x in raw[:2]],
                col_r=[shift(x, -plan.side) for x in raw[w + 2 :]],
                north=north,
                south=south,
            )
        )
    spot = lane % 8
    is_top = (lane % 16) < 8
    unsent = (first & is_top & (spot < 2)) | (last & jnp.logical_not(is_top) & (spot >= w + 2))
    line = jnp.where(unsent, 0.0, line)
    deep = jnp.where(unsent, 0.0, deep)
    ends = jnp.where(first & (spot < 2), 0.0, ends)
    ends = jnp.where(last & (spot >= w + 2), 0.0, ends)
    rim = dict(line=line, deep=deep, ends=ends, spot=spot, is_top=is_top)
    return stacks, rim, lane, first, last


def rim_cell(plan, lane, g, bottom, e):
    return lane == 16 * g + 8 * bottom + e


def wide_forward(plan, found, taps_ref):
    stacks, rim, lane, first, last = found
    w, n, side, high, c = plan.cols, plan.lanes, plan.side, plan.height, plan.channels

    def put(a, b, segment, value):
        row = (a * 3 + b) * c
        taps_ref[row : row + c, segment * n : (segment + 1) * n] = value.astype(BF16)

    rows_r = (lane >= 2 * side) & (lane < high)
    for g, h in enumerate(stacks):
        raw = h["raw"]
        x = []
        for q in range(w + 4):
            at = 16 * g + q
            y = jnp.where(lane == high, rim["line"][:, at + 8 : at + 9], raw[q])
            x.append(jnp.where(lane == n - 1, rim["line"][:, at : at + 1], y))
        edge_l = jnp.where(lane < side, h["row_l"][0], jnp.where(lane < high, h["col_l"][1], 0.0))
        edge_r = jnp.where(lane < 2 * side, h["col_r"][0], jnp.where(rows_r, h["row_r"][0], 0.0))
        x[0] = jnp.where(first, h["col_l"][0], x[0])
        x[1] = jnp.where(first, edge_l, x[1])
        x[w + 2] = jnp.where(last, edge_r, x[w + 2])
        x[w + 3] = jnp.where(last, h["col_r"][1], x[w + 3])
        moved = [[shift(y, 1 - b) if b != 1 else y for b in range(3)] for y in x]
        own0, own1, own30, own31 = raw[2], raw[3], raw[w], raw[w + 1]
        north, south = h["north"], h["south"]
        turned_l = [jnp.where(lane < side, own0, 0.0)]
        turned_r = []
        for d in range(2):
            y = jnp.where(lane < side, h["row_l"][d], shift(own0, -d))
            turned_l.append(jnp.where(lane == n - 1, north[d], y))
            y = jnp.where(rows_r, h["row_r"][d], shift(own31, d))
            turned_r.append(jnp.where(lane == high, south[d], y))
        turned_l[1:] = [
            jnp.where((lane > side) & (lane < n - 1), 0.0, y) for y in turned_l[1:]
        ]
        turned_r = [turned_r[1], turned_r[0], jnp.where(rows_r, own31, 0.0)]
        for b in range(3):
            for a in range(3):
                for j in range(1, w + 1):
                    put(a, b, plan.segment(g, j), moved[j + a][b])
                y = shift(h["col_l"][1], 1 - b) if a == 1 else moved[a][b]
                y = jnp.where(lane < side, shift(turned_l[b], 1 - a), y)
                if b == 0:
                    over = shift(own0, 2 - a) if a < 2 else 0.0
                    y = jnp.where(lane == side, over, y)
                elif a == 2:
                    y = jnp.where(lane == high, shift((own0, own1)[b - 1], 1), y)
                    if b == 2:
                        y = jnp.where(lane == high - 1, own0, y)
                put(a, b, plan.segment(g, 0), jnp.where(first, y, moved[a][b]))
                y = shift(h["col_r"][0], 1 - b) if a == 1 else moved[w + 1 + a][b]
                y = jnp.where(rows_r, shift(turned_r[b], 1 - a), y)
                if b == 2:
                    over = shift(own31, -a) if a > 0 else 0.0
                    y = jnp.where(lane == 2 * side - 1, over, y)
                if a == 0:
                    if b == 0:
                        y = jnp.where(lane == 0, own31, y)
                    y = jnp.where(lane == n - 1, shift(own30 if b == 0 else own31, -1), y)
                put(a, b, plan.segment(g, w + 1), jnp.where(last, y, moved[w + 1 + a][b]))
    line, deep, ends = rim["line"], rim["deep"], rim["ends"]
    is_top, spot = rim["is_top"], rim["spot"]
    ends = jnp.where(last & is_top & (spot == w + 2), shift(ends, 1), ends)
    ends = jnp.where(first & jnp.logical_not(is_top) & (spot == 1), shift(ends, -1), ends)
    for g, h in enumerate(stacks):
        north = first & rim_cell(plan, lane, g, 0, 1)
        south = last & rim_cell(plan, lane, g, 1, w + 2)
        line = jnp.where(north, h["north"][0], line)
        deep = jnp.where(north, h["north"][2], deep)
        line = jnp.where(south, h["south"][0], line)
        deep = jnp.where(south, h["south"][2], deep)
    by_a = (jnp.where(is_top, ends, deep), line, jnp.where(is_top, deep, ends))
    for a in range(3):
        for b in range(3):
            put(a, b, plan.segments - 1, shift(by_a[a], -b) if b else by_a[a])


def wide_backward(plan, found, taps_ref):
    stacks, rim, lane, first, last = found
    w, n, side, high, c = plan.cols, plan.lanes, plan.side, plan.height, plan.channels

    def put(row, segment, value):
        taps_ref[row * c : (row + 1) * c, segment * n : (segment + 1) * n] = value.astype(BF16)

    zero = jnp.zeros(lane.shape, F32)
    rows_l = lane < side
    rows_r = (lane >= 2 * side) & (lane < high)
    for g, h in enumerate(stacks):
        raw = h["raw"]
        z = list(raw)
        edge_l = jnp.where((lane >= side) & (lane <= high), h["col_l"][1], 0.0)
        edge_r = jnp.where((lane < 2 * side) | (lane == n - 1), h["col_r"][0], 0.0)
        z[1] = jnp.where(first, edge_l, z[1])
        z[w + 2] = jnp.where(last, edge_r, z[w + 2])
        moved = [[shift(y, b - 1) if b != 1 else y for b in range(3)] for y in z]
        keep_l = (lane >= side) | jnp.logical_not(first)
        keep_r = (lane < 2 * side) | jnp.logical_not(last)
        own0, own1, own30, own31 = raw[2], raw[3], raw[w], raw[w + 1]
        north, south = h["north"], h["south"]
        line_l = [jnp.where(rows_l, y, 0.0) for y in h["row_l"]]
        line_r = [jnp.where(rows_r, y, 0.0) for y in h["row_r"]]
        line_l = [line_l[1], line_l[0], zero]
        line_r = [zero, line_r[0], line_r[1]]
        keep = (lane >= side) & (lane <= high + 1)
        deep_l = [zero] + [jnp.where(keep, h["col_l"][i], 0.0) for i in (1, 0)]
        keep = (lane < 2 * side) | (lane >= n - 2)
        deep_r = [jnp.where(keep, h["col_r"][i], 0.0) for i in (1, 0)] + [zero]
        for b in range(3):
            for a in range(3):
                tap = a * 3 + b
                for j in range(1, w + 1):
                    y = moved[j + 2 - a][b]
                    if j == 1 and a == 2:
                        y = jnp.where(keep_l, y, 0.0)
                    if j == w and a == 0:
                        y = jnp.where(keep_r, y, 0.0)
                    put(tap, plan.segment(g, j), y)
                y = jnp.where(rows_l, shift(line_l[b], a - 1), shift(deep_l[a], b - 1))
                if a == 0:
                    y = jnp.where(lane == side - 1, shift(own0, b - 2), y)
                    y = jnp.where(lane == side, shift(own0, b), y)
                put(tap, plan.segment(g, 0), jnp.where(first, y, moved[2 - a][b]))
                y = jnp.where(rows_r, shift(line_r[b], a - 1), shift(deep_r[a], b - 1))
                if a == 2:
                    y = jnp.where(lane == 2 * side - 1, shift(own31, b - 2), y)
                    y = jnp.where(lane == 2 * side, shift(own31, b), y)
                put(tap, plan.segment(g, w + 1), jnp.where(last, y, moved[w + 3 - a][b]))
        for j in range(w + 2):
            segment = plan.segment(g, j)
            for b in range(3):
                at = 16 * g + j + 2 - b
                top = jnp.where(lane == 0, rim["line"][:, at : at + 1], 0.0)
                bottom = jnp.where(lane == high - 1, rim["line"][:, at + 8 : at + 9], 0.0)
                left = right = zero
                if j == 0:
                    own = jnp.where(lane < high, shift(own0, b - 1), 0.0)
                    top = jnp.where(first, own, top)
                    bottom = jnp.where(first, 0.0, bottom)
                    if b < 2:
                        left = jnp.where(first & (lane == 0), north[1 - b], 0.0)
                        right = jnp.where(first & (lane == high), shift((own1, own0)[b], 1), 0.0)
                if j == 1:
                    left = jnp.where(first & rows_l, shift(line_l[1], b - 1), 0.0)
                if j == w:
                    right = jnp.where(last & rows_r, shift(line_r[1], b - 1), 0.0)
                if j == w + 1:
                    own = jnp.where(lane < high, shift(own31, b - 1), 0.0)
                    bottom = jnp.where(last, own, bottom)
                    top = jnp.where(last, 0.0, top)
                    if b > 0:
                        over = shift((own31, own30)[b - 1], -1)
                        left = jnp.where(last & (lane == n - 1), over, 0.0)
                        right = jnp.where(last & (lane == high - 1), south[b - 1], 0.0)
                for i, y in enumerate((top, bottom, left, right)):
                    put(9 + 3 * i + b, segment, y)
    line, deep, ends = rim["line"], rim["deep"], rim["ends"]
    is_top = rim["is_top"]
    tops = [jnp.where(is_top, y, 0.0) for y in (deep, ends)]
    bottoms = [jnp.where(is_top, 0.0, y) for y in (deep, ends)]
    by_a = (tops[0], line, bottoms[0])
    segment = plan.segments - 1
    for b in range(3):
        for a in range(3):
            put(a * 3 + b, segment, shift(by_a[a], b - 2))
        top = bottom = zero
        for g, h in enumerate(stacks):
            if b < 2:
                over = h["north"][2 * (1 - b)]
                top = jnp.where(first & rim_cell(plan, lane, g, 0, 1), over, top)
            if b > 0:
                over = h["south"][2 * (b - 1)]
                bottom = jnp.where(last & rim_cell(plan, lane, g, 1, w), over, bottom)
        put(9 + b, segment, top)
        put(12 + b, segment, bottom)
        put(15 + b, segment, shift(tops[1], b - 2))
        put(18 + b, segment, shift(bottoms[1], b - 2))


def second_halos(plan, ids_ref, ref):
    w, n, high, side = plan.cols, plan.lanes, plan.height, plan.side
    first = ids_ref[0] == 0
    last = ids_ref[0] == plan.tiles - 1
    start = (plan.segments - 1) * n
    rim = ref[:, start : start + n].astype(F32)
    lane = lax.broadcasted_iota(jnp.int32, rim.shape, 1)
    result = []
    for g in range(plan.stacks):
        left, right = [
            ref[:, plan.segment(g, j) * n : (plan.segment(g, j) + 1) * n].astype(F32)
            for j in (0, w + 1)
        ]
        top = [rim[:, 16 * g + e : 16 * g + e + 1] for e in range(w + 2)]
        bottom = [rim[:, 16 * g + 8 + e : 16 * g + 9 + e] for e in range(w + 2)]
        top[0] = jnp.where(first, 0.0, top[0])
        bottom[0] = jnp.where(first, left[:, high - 1 : high], bottom[0])
        top[w + 1] = jnp.where(last, right[:, 0:1], top[w + 1])
        bottom[w + 1] = jnp.where(last, 0.0, bottom[w + 1])
        result.append(
            dict(
                first=first,
                last=last,
                left=left,
                right=right,
                row_l=jnp.where(lane < side, left, 0.0),
                row_r=jnp.where((lane >= 2 * side) & (lane < high), right, 0.0),
                col_l=left,
                col_r=right,
                top=top,
                bottom=bottom,
            )
        )
    return result


def forward_operand(plan, own, halo, taps_ref):
    w, n, side, height = plan.cols, plan.lanes, plan.side, plan.height
    c = plan.channels
    lane = lax.broadcasted_iota(jnp.int32, (c, n), 1)
    for g in range(plan.stacks):
        h = halo[g]
        edge_l = jnp.where(lane < side, h["row_l"], jnp.where(lane < height, h["col_l"], 0.0))
        edge_r = jnp.where(
            lane < 2 * side, h["col_r"], jnp.where(lane < height, h["row_r"], 0.0)
        )
        columns = [h["left"]] + own[g] + [h["right"]]
        for j in range(w + 2):
            x = jnp.where(lane == height, h["bottom"][j], columns[j])
            x = jnp.where(lane == n - 1, h["top"][j], x)
            if j == 0:
                x = jnp.where(h["first"], edge_l, x)
            if j == w + 1:
                x = jnp.where(h["last"], edge_r, x)
            for b in range(3):
                y = (x if b == 1 else shift(x, 1 - b)).astype(BF16)
                for a in range(3):
                    out = j - a
                    if 0 <= out < w:
                        at = (g * w + out) * n
                        row = (a * 3 + b) * c
                        taps_ref[row : row + c, at : at + n] = y


def backward_operand(plan, own, halo, taps_ref):
    w, n, side, height = plan.cols, plan.lanes, plan.side, plan.height
    c = plan.channels
    lane = lax.broadcasted_iota(jnp.int32, (c, n), 1)
    zero = jnp.zeros((c, n), BF16)
    for g in range(plan.stacks):
        h = halo[g]
        first, last = h["first"], h["last"]
        edge_l = jnp.where((lane >= side) & (lane <= height), h["col_l"], 0.0)
        edge_r = jnp.where((lane < 2 * side) | (lane == n - 1), h["col_r"], 0.0)
        columns = [jnp.where(first, edge_l, h["left"])] + own[g]
        columns += [jnp.where(last, edge_r, h["right"])]
        keep_l = (lane >= side) | jnp.logical_not(first)
        keep_r = (lane < 2 * side) | jnp.logical_not(last)
        for j in range(w + 2):
            for b in range(3):
                y = columns[j] if b == 1 else shift(columns[j], b - 1)
                if j == 0:
                    y = jnp.where(keep_l, y, 0.0)
                if j == w + 1:
                    y = jnp.where(keep_r, y, 0.0)
                y = y.astype(BF16)
                for a in range(3):
                    out = j - 2 + a
                    if 0 <= out < w:
                        at = (g * w + out) * n
                        row = (a * 3 + b) * c
                        taps_ref[row : row + c, at : at + n] = y
        seam_l = first & (lane < side)
        seam_r = last & (lane >= 2 * side) & (lane < height)
        for out in range(w):
            at = (g * w + out) * n
            for b in range(3):
                y = jnp.where(lane == 0, h["top"][out + 2 - b], 0.0).astype(BF16)
                taps_ref[(9 + b) * c : (10 + b) * c, at : at + n] = y
                y = jnp.where(lane == height - 1, h["bottom"][out + 2 - b], 0.0).astype(BF16)
                taps_ref[(12 + b) * c : (13 + b) * c, at : at + n] = y
                y = zero
                if out == 0:
                    y = jnp.where(seam_l, shift(h["row_l"], b - 1), 0.0).astype(BF16)
                taps_ref[(15 + b) * c : (16 + b) * c, at : at + n] = y
                y = zero
                if out == w - 1:
                    y = jnp.where(seam_r, shift(h["row_r"], b - 1), 0.0).astype(BF16)
                taps_ref[(18 + b) * c : (19 + b) * c, at : at + n] = y


def seam_weights(kernel_ref):
    order = list(range(9)) + [0, 1, 2, 6, 7, 8, 0, 3, 6, 2, 5, 8]
    return jnp.concatenate([kernel_ref[tap] for tap in order], axis=1)


def own_columns(plan, ref):
    w, n = plan.cols, plan.lanes
    return [
        [ref[:, (g * w + i) * n : (g * w + i + 1) * n].astype(F32) for i in range(w)]
        for g in range(plan.stacks)
    ]


def middle_kernel(plan, ids_ref, *refs):
    w, n, g_count, c = plan.cols, plan.lanes, plan.stacks, plan.channels
    around, tables, (w_one, w_two), refs = refs[:5], refs[5:8], refs[8:10], refs[10:]
    hidden_ref, pre_grad_ref, mine_ref, theirs_ref, fwd_ref, bwd_ref, sums_ref, packed_ref = refs
    *around, got = around
    seams = seam_cells(plan, ids_ref, got, *tables[:2])
    found = [
        surroundings(plan, ids_ref, k, *around, seams, tables[2]) for k in range(2)
    ]
    wide_forward(plan, found[0], fwd_ref)
    wide_backward(plan, found[1], bwd_ref)
    pre = product(w_one[...], fwd_ref[...], 0, 0)
    grad = product(seam_weights(w_two), bwd_ref[...], 1, 0)
    bend = jnp.tanh(GELU_A * (pre + GELU_B * (pre * pre * pre)))
    half = 0.5 * (1.0 + bend)
    slope = half + 0.5 * pre * (1.0 - bend * bend) * (
        GELU_A * (1.0 + (3.0 * GELU_B) * (pre * pre))
    )
    first = ids_ref[0] == 0
    last = ids_ref[0] == plan.tiles - 1
    flat = lax.broadcasted_iota(jnp.int32, pre.shape, 1)
    segment, lane = flat // n, flat % n
    own_end = g_count * w
    left = (segment >= own_end) & ((segment - own_end) % 2 == 0)
    right = (segment >= own_end) & ((segment - own_end) % 2 == 1)
    inside = (lane < plan.height) | (segment == plan.segments - 1)
    inside = inside | (left & first & (lane == plan.height))
    inside = inside | (right & last & (lane == n - 1))
    hidden = jnp.where(inside, pre * half, 0.0).astype(BF16)
    pre_grad = jnp.where(inside, grad * slope, 0.0).astype(BF16)
    hidden_ref[...] = hidden
    pre_grad_ref[...] = pre_grad
    own_end *= n
    terms = product(fwd_ref[:, :own_end], pre_grad[:, :own_end], 1, 1)
    turned = product(bwd_ref[:, :own_end], hidden[:, :own_end], 1, 1)
    tap = [turned[i * c : (i + 1) * c] for i in range(21)]
    for b in range(3):
        tap[b] = tap[b] + tap[9 + b]
        tap[6 + b] = tap[6 + b] + tap[12 + b]
    for a in range(3):
        tap[3 * a] = tap[3 * a] + tap[15 + a]
        tap[3 * a + 2] = tap[3 * a + 2] + tap[18 + a]
    sums_ref[0 : 9 * c, :] = terms
    for i in range(9):
        sums_ref[(9 + i) * c : (10 + i) * c, :] = jnp.transpose(tap[i])
    packed_rows = max(plan.folds - 1, 1) * plan.fold_rows
    shared = (plan.folds - 1) * plan.fold_rows
    for i in range(max(plan.folds - 1, 1)):
        at = i * plan.fold_rows
        block = sums_ref[at : at + plan.fold_rows, :]
        if plan.folds > 1:
            rest = plan.wide - c
            more = sums_ref[shared : shared + plan.fold_rows, i * rest : (i + 1) * rest]
            block = jnp.concatenate([block, more], axis=1)
        packed_ref[at : at + plan.fold_rows, :] = block
    spare = packed_ref.shape[0] - packed_rows
    if spare:
        packed_ref[packed_rows:, :] = jnp.zeros((spare, plan.wide), F32)
    near, mid = ids_ref[3], ids_ref[4]
    for d in range(plan.mid):
        spot = jnp.bitwise_xor(mid, d)
        for other, ref in ((0, mine_ref), (1, theirs_ref)):
            at = (jnp.bitwise_xor(near, other) * plan.mid + spot) * plan.piece
            rows = packed_ref[pl.ds(pl.multiple_of(at, 16), plan.piece), :]
            ref[d] = rows.astype(ref.dtype)


def last_kernel(plan, ids_ref, hidden_ref, pre_grad_ref, w_two, w_one, *refs):
    out_ref, back_ref, fwd_ref, bwd_ref = refs
    w, n = plan.cols, plan.lanes
    halo = second_halos(plan, ids_ref, hidden_ref)
    forward_operand(plan, own_columns(plan, hidden_ref), halo, fwd_ref)
    halo = second_halos(plan, ids_ref, pre_grad_ref)
    backward_operand(plan, own_columns(plan, pre_grad_ref), halo, bwd_ref)
    out = product(w_two[...], fwd_ref[...], 0, 0).astype(BF16)
    back = product(seam_weights(w_one), bwd_ref[...], 1, 0).astype(BF16)
    for g in range(plan.stacks):
        for i in range(w):
            at = (g * w + i) * n
            out_ref[:, g, i, :] = out[:, at : at + plan.height]
            back_ref[:, g, i, :] = back[:, at : at + plan.height]


def sum_kernel(plan, scale, ids_ref, mine_ref, theirs_ref, one_ref, two_ref, packed_ref, sums_ref):
    near, mid = ids_ref[3], ids_ref[4]
    for d in range(plan.mid):
        spot = jnp.bitwise_xor(mid, d)
        for other, ref in ((0, mine_ref), (1, theirs_ref)):
            at = (jnp.bitwise_xor(near, other) * plan.mid + spot) * plan.piece
            packed_ref[pl.ds(pl.multiple_of(at, 16), plan.piece), :] = ref[d].astype(F32) * scale
    c, shared = plan.channels, (plan.folds - 1) * plan.fold_rows
    more = []
    for i in range(max(plan.folds - 1, 1)):
        at = i * plan.fold_rows
        block = packed_ref[at : at + plan.fold_rows, :]
        sums_ref[at : at + plan.fold_rows, :] = block[:, :c]
        more.append(block[:, c:])
    if plan.folds > 1:
        sums_ref[shared : shared + plan.fold_rows, :] = jnp.concatenate(more, axis=1)
    rows = one_ref.shape[0]
    one_ref[...] = sums_ref[:rows]
    two_ref[...] = sums_ref[rows : 2 * rows]


VMEM = pl.BlockSpec(memory_space=pltpu.VMEM)
SMEM = pl.BlockSpec(memory_space=pltpu.SMEM)


def call(body, ids, inputs, outs, scratch=()):
    return pl.pallas_call(
        body,
        out_shape=outs,
        in_specs=[SMEM] + [VMEM] * len(inputs),
        out_specs=[VMEM] * len(outs),
        scratch_shapes=list(scratch),
        compiler_params=pltpu.CompilerParams(vmem_limit_bytes=48 * 2**20),
    )(ids, *inputs)


def across_faces(plan, columns, step):
    t, f = plan.tiles, plan.faces
    first = lax.axis_index("tile") == 0
    sent = jnp.where(first, columns[:2], columns[plan.cols - 2 :])
    pairs = [((t - 1) * f + i, (t - 1) * f + (i + step) % f) for i in range(f)]
    pairs += [((i + step) % f, i) for i in range(f)]
    return lax.ppermute(sent, BOTH, pairs)


def pair_up(plan, columns, passed):
    t, g = plan.tiles, plan.stacks
    tile = lax.axis_index("tile")
    even = tile % 2 == 0
    head, tail = columns[:2], columns[plan.cols - 2 :]
    inner = jnp.where(even, tail, head)
    outer = jnp.where(even, head, tail)
    passed = jnp.where(tile == 0, passed[:, :, :1], passed[:, :, g - 1 :])
    to_last = jnp.concatenate([head[:, :, 1:], passed], axis=2)
    to_first = jnp.concatenate([passed, tail[:, :, : g - 1]], axis=2)
    outer = jnp.where(tile == 0, to_last, jnp.where(tile == t - 1, to_first, outer))
    inner = lax.ppermute(inner, "tile", [(i, i ^ 1) for i in range(t)])
    outer = lax.ppermute(outer, "tile", [(i, ((i + 1) ^ 1) - 1 if i else t - 1) for i in range(t - 1)] + [(t - 1, 0)])
    return inner, outer


def spread_blocks(plan, blocks):
    count = plan.tiles * plan.faces
    flat = blocks.reshape((count,) + blocks.shape[2:])
    return lax.all_to_all(flat, BOTH, 0, 0, tiled=True).reshape(blocks.shape)


def swapped(plan, x, near=0, mid=0, far=0):
    f = plan.faces
    pairs = []
    for i in range(plan.tiles * f):
        tile, face = i // f, i % f
        tile = tile ^ near ^ ((mid // f) << 1) ^ (far << 2)
        pairs.append((i, tile * f + (face ^ (mid % f))))
    return lax.ppermute(x, BOTH, pairs)


def tree_sum(values):
    while len(values) > 1:
        values = [a + b for a, b in zip(values[::2], values[1::2])]
    return values[0]


def sum_all(plan, mine, theirs, beside):
    half = mine + swapped(plan, theirs, near=1).astype(F32)
    short = half.astype(BF16)
    got = [swapped(plan, short[d], mid=d) for d in range(1, plan.mid)]
    got, beside = lax.optimization_barrier((got, beside))
    piece = tree_sum([half[0]] + [x.astype(F32) for x in got]).astype(BF16)
    got = [swapped(plan, piece, far=d) for d in range(1, plan.far)]
    piece = tree_sum([x.astype(F32) for x in [piece] + got]).astype(BF16)
    pieces = [piece] + [swapped(plan, piece, mid=d) for d in range(1, plan.mid)]
    half = jnp.stack(pieces)
    return half, swapped(plan, half, near=1), beside


def on_device(mesh_shape, fields, upstream, kernel_one, kernel_two):
    plan = Plan(mesh_shape, fields.shape)
    c, own, w, n = plan.channels, plan.own, plan.cols, plan.lanes
    g, h = plan.stacks, plan.height
    tile, face = lax.axis_index("tile"), lax.axis_index("face")
    sub = lax.axis_index("sub")
    mid = ((tile >> 1) & 1) * plan.faces + face
    kind = jnp.where(tile == 0, 0, jnp.where(tile == plan.tiles - 1, 2, 1))
    ids = jnp.stack([tile, face, sub, tile & 1, mid, kind]).astype(jnp.int32)
    if mesh_shape["sub"] > 1:
        fields = lax.all_gather(fields, "sub", axis=0, tiled=True)
        upstream = lax.all_gather(upstream, "sub", axis=0, tiled=True)

    both = jnp.stack([fields, upstream]).transpose(3, 0, 2, 1, 4)
    columns = jnp.pad(both, ((0, 0),) * 4 + ((0, n - h),))
    blocks_shape = jax.ShapeDtypeStruct((plan.tiles, plan.faces, plan.block, c), BF16)
    (blocks,) = call(
        functools.partial(first_kernel, plan), ids, [plan.send_table(), columns], [blocks_shape]
    )
    passed = across_faces(plan, columns, 1)
    across = passed if g == 2 else across_faces(plan, columns, 2)
    got = spread_blocks(plan, blocks)
    sent, passed, _ = lax.optimization_barrier((columns, passed, blocks))
    halo = (*pair_up(plan, sent, passed), across, got)

    fwd_one = kernel_one.reshape(9 * c, c)
    bwd_two = kernel_two.reshape(9, c, c)
    fwd_two = lax.dynamic_slice_in_dim(kernel_two, sub * own, own, 3).reshape(9 * c, own)
    bwd_one = lax.dynamic_slice_in_dim(kernel_one, sub * own, own, 2).reshape(9, own, c)

    def taps(width):
        return [pltpu.VMEM((9 * c, width), BF16), pltpu.VMEM((21 * c, width), BF16)]

    piece = (plan.mid, plan.piece, plan.wide)
    rows = plan.near * plan.mid * plan.piece
    wide = plan.segments * n
    hidden, pre_grad, mine, theirs = call(
        functools.partial(middle_kernel, plan),
        ids,
        [columns, *halo, *plan.take_tables(), fwd_one, bwd_two],
        [jax.ShapeDtypeStruct((c, wide), BF16)] * 2
        + [jax.ShapeDtypeStruct(piece, F32), jax.ShapeDtypeStruct(piece, BF16)],
        taps(wide) + [pltpu.VMEM((plan.terms, c), F32), pltpu.VMEM((rows, plan.wide), F32)],
    )
    out_shape = jax.ShapeDtypeStruct((own, g, w, h), BF16)
    beside = call(
        functools.partial(last_kernel, plan),
        ids,
        [hidden, pre_grad, fwd_two, bwd_one],
        [out_shape, out_shape],
        taps(g * w * n),
    )
    mine, theirs, (result, fields_grad) = sum_all(plan, mine, theirs, list(beside))
    scale = 1.0 / (plan.side * 12.0**0.5)
    sums = call(
        functools.partial(sum_kernel, plan, scale),
        ids,
        [mine, theirs],
        [jax.ShapeDtypeStruct((9 * c, c), F32)] * 2,
        [pltpu.VMEM((rows, plan.wide), F32), pltpu.VMEM((plan.terms, c), F32)],
    )
    grads = []
    for i in range(2):
        grad = sums[i].reshape(3, 3, c, c)
        grads.append(lax.dynamic_slice_in_dim(grad, sub * own, own, 3))
    return (
        result,
        fields_grad,
        grads[0],
        grads[1],
    )


def solution(mesh):
    placed = (P("sub", "face", "tile", "parts"), P("sub", "face", "tile", "parts"), P(), P())
    return jax.shard_map(
        functools.partial(on_device, dict(mesh.shape)),
        mesh=mesh,
        in_specs=placed,
        out_specs=(
            P("sub", "face", "tile", "parts"),
            P("sub", "face", "tile", "parts"),
            P("parts", None, None, "sub"),
            P("parts", None, None, "sub"),
        ),
        check_vma=False,
    )
```

```python
import functools

import jax
import jax.numpy as jnp
import numpy as np
from jax import lax
from jax.experimental import pallas as pl
from jax.experimental.pallas import tpu as pltpu
from jax.sharding import PartitionSpec as P

BOTH = ("tile", "face")
F32 = jnp.float32
BF16 = jnp.bfloat16
GELU_A = 0.7978845608028654
GELU_B = 0.044715


def up_to(value, step):
    return -(-value // step) * step


class Plan:
    def __init__(self, mesh_shape, block):
        self.tiles = mesh_shape["tile"]
        self.faces = mesh_shape["face"]
        self.stacks, self.cols, self.height = block[1:4]
        self.side = self.height // 3
        self.lanes = up_to(self.height + 2, 128)
        self.channels = block[0] * mesh_shape["sub"]
        self.own = block[0]
        w = self.cols
        assert w == 2
        self.reach = w + 4
        self.cells = 2 * self.reach
        self.block = 2 * self.cells
        self.kinds = 2 if self.stacks > 1 else 1
        self.inner = self.stacks * w
        self.outer = self.stacks * 2 + 1
        self.near = 2
        self.mid = 2 * self.faces
        self.far = self.tiles // 4
        self.terms = 2 * 9 * self.channels
        self.wide = self.channels
        rest = -self.channels % 128
        self.folds = 1
        if rest and self.channels % rest == 0 and self.terms % (8 * (self.channels // rest + 1)) == 0:
            self.folds = self.channels // rest + 1
            self.wide = self.channels + rest
        self.fold_rows = self.terms // self.folds
        packed = self.fold_rows * max(self.folds - 1, 1)
        self.piece = up_to(-(-packed // (self.near * self.mid)), 16)

    def segment(self, stack, slot):
        if 1 <= slot <= self.cols:
            return stack * self.cols + slot - 1
        return self.inner + 2 * stack + (1 if slot else 0)

    def spot(self, depth, e):
        return depth * self.reach + e

    def send_table(self):
        t, k, c = self.tiles, self.kinds, self.block
        g, w, n = self.stacks, self.cols, self.lanes
        high = self.height - 1
        table = np.full((3, t, k, c), -1, np.int32)
        for dest in range(t):
            for kind in range(k):
                same = kind == 0 and k == 2
                from_a = 1 if same else 0
                from_b = 0 if same else g - 1

                def cell(stack, col, row):
                    return (stack * w + col) * n + row

                for depth in range(2):
                    for e in range(self.reach):
                        at = self.spot(depth, e)
                        row = w * dest - 2 + e
                        if 0 <= row:
                            table[0, dest, kind, at] = cell(from_a, depth, row)
                        row = 2 * self.side + w * dest - 2 + e
                        if row <= high:
                            table[2, dest, kind, at] = cell(from_b, w - 1 - depth, row)
                    for e in range(w):
                        if dest == 0:
                            table[:2, dest, kind, self.spot(depth, e)] = cell(from_b, e, depth)
                        if dest == t - 1:
                            at = self.spot(depth, w + 2 + e)
                            table[1:, dest, kind, at] = cell(from_a, e, high - depth)
        return jnp.asarray(table.reshape(3, 1, -1))

    def take_tables(self):
        t, c, w, n = self.tiles, self.block, self.cols, self.lanes
        from_a = np.zeros((t, 2, self.cells, 2, 4, n), np.float32)
        from_b = np.zeros((t, 2, self.cells, 2, 4, n), np.float32)
        for depth in range(2):
            for k in range(2):
                for src in range(t):
                    for e in range(w):
                        if src > 0:
                            at = self.spot(depth, w + 2 + e)
                            from_a[src, k, at, k, depth, 2 * self.side + src * w + e] = 1
                        if src < t - 1:
                            from_b[src, k, self.spot(depth, e), k, depth, src * w + e] = 1
                for e in range(self.reach):
                    at = self.spot(depth, e)
                    from_a[0, k, at, k, 2 + depth, e] = 1
                    from_b[t - 1, k, at, k, 2 + depth, 8 + e] = 1
        ends = np.zeros((self.reach, n, n), np.float32)
        for e in range(self.reach):
            ends[e, 0, e] = 1
            ends[e, self.height - 1, 8 + e] = 1
        shape = (t * c, 8 * n)
        return (
            jnp.asarray(from_a.reshape(shape), BF16),
            jnp.asarray(from_b.reshape(shape), BF16),
            jnp.asarray(ends.reshape(-1, n), BF16),
        )


def first_kernel(plan, ids_ref, table_ref, columns_ref, blocks_ref):
    t, c, g, w = plan.tiles, plan.block, plan.stacks, plan.cols
    face = ids_ref[1]
    flat = [
        jnp.concatenate([columns_ref[i, k, j] for j in range(g) for i in range(w)], axis=1)
        for k in range(2)
    ]
    wanted = table_ref[ids_ref[5]]
    cell = lax.broadcasted_iota(jnp.int32, (flat[0].shape[1], wanted.shape[1]), 0)
    pick = jnp.where(cell == wanted, 1.0, 0.0).astype(BF16)
    picked = [jnp.transpose(product(x, pick, 1, 0)) for x in flat]
    both = picked[0] + pltpu.roll(picked[1], plan.cells, 0)
    both = both.reshape(t, plan.kinds, c, both.shape[-1])
    for dest in range(plan.faces):
        if plan.kinds == 2:
            block = jnp.where(face == dest, both[:, 0], both[:, 1])
        else:
            block = both[:, 0]
        blocks_ref[:, dest] = block.astype(BF16)


def product(x, y, x_dim, y_dim):
    return lax.dot_general(x, y, (((x_dim,), (y_dim,)), ((), ())), preferred_element_type=F32)


def shift(x, by):
    return pltpu.roll(x, by % x.shape[1], 1)


def seam_cells(plan, ids_ref, got_ref, tab_a, tab_b):
    face = ids_ref[1]
    after = lax.rem(face + 1, plan.faces)
    before = lax.rem(face + plan.faces - 1, plan.faces)
    result = []
    for g in range(plan.stacks):
        face_a = face if g < plan.stacks - 1 else after
        face_b = face if g > 0 else before
        pair = []
        for at, table in ((face_a, tab_a), (face_b, tab_b)):
            rows = got_ref[:, at].astype(F32)
            rows = rows.reshape(plan.tiles * plan.block, rows.shape[-1])
            pair.append(product(rows.astype(BF16), table[...], 0, 0))
        result.append(pair)
    return result


def surroundings(plan, ids_ref, k, columns_ref, inner_ref, outer_ref, across_ref, seams_of, tab_ends):
    w, n, side = plan.cols, plan.lanes, plan.side
    high, g_count = plan.height, plan.stacks
    first = ids_ref[0] == 0
    last = ids_ref[0] == plan.tiles - 1
    even = lax.rem(ids_ref[0], 2) == 0
    shape = (plan.channels, n)
    lane = lax.broadcasted_iota(jnp.int32, shape, 1)
    stacks = []
    line, deep, ends = [jnp.zeros(shape, F32) for _ in range(3)]
    for g in range(g_count):
        start = 4 * k * n
        seams = [
            [x[:, start + i * n : start + (i + 1) * n] for i in range(4)] for x in seams_of[g]
        ]
        line += shift(seams[0][2] + seams[1][2], 16 * g)
        deep += shift(seams[0][3] + seams[1][3], 16 * g)
        raw = [jnp.where(even, outer_ref[i, k, g], inner_ref[i, k, g]) for i in range(2)]
        raw += [columns_ref[i, k, g] for i in range(w)]
        raw += [jnp.where(even, inner_ref[i, k, g], outer_ref[i, k, g]) for i in range(2)]
        ends += shift(product(jnp.concatenate(raw, axis=1), tab_ends[...], 1, 0), 16 * g)
        raw = [x.astype(F32) for x in raw]
        for d in range(2):
            for i in range(2):
                here = lane == side - 2 + i
                seams[1][d] = jnp.where(here, shift(raw[i], side - 2 + i - d), seams[1][d])
                here = lane == 2 * side + i
                by = 2 * side + i - (high - 1 - d)
                seams[0][d] = jnp.where(here, shift(raw[w + 2 + i], by), seams[0][d])
        pole = [across_ref[i, k, g].astype(F32) for i in range(2)]
        north = [pole[0][:, :1], pole[1][:, :1], pole[0][:, 1:2]]
        south = [pole[1][:, high - 1 : high], pole[0][:, high - 1 : high]]
        south.append(pole[1][:, high - 2 : high - 1])
        stacks.append(
            dict(
                raw=raw,
                row_l=seams[1][:2],
                row_r=seams[0][:2],
                col_l=[shift(x, plan.side) for x in raw[:2]],
                col_r=[shift(x, -plan.side) for x in raw[w + 2 :]],
                north=north,
                south=south,
            )
        )
    spot = lane % 8
    is_top = (lane % 16) < 8
    unsent = (first & is_top & (spot < 2)) | (last & jnp.logical_not(is_top) & (spot >= w + 2))
    line = jnp.where(unsent, 0.0, line)
    deep = jnp.where(unsent, 0.0, deep)
    ends = jnp.where(first & (spot < 2), 0.0, ends)
    ends = jnp.where(last & (spot >= w + 2), 0.0, ends)
    rim = dict(line=line, deep=deep, ends=ends, spot=spot, is_top=is_top)
    return stacks, rim, lane, first, last


def rim_cell(plan, lane, g, bottom, e):
    return lane == 16 * g + 8 * bottom + e


def wide_forward(plan, found, taps_ref, inner):
    stacks, rim, lane, first, last = found
    w, n, side, high, c = plan.cols, plan.lanes, plan.side, plan.height, plan.channels

    def put(a, b, segment, value):
        if (segment < plan.inner) != inner:
            return
        segment -= 0 if inner else plan.inner
        row = (a * 3 + b) * c
        taps_ref[row : row + c, segment * n : (segment + 1) * n] = value.astype(BF16)

    rows_r = (lane >= 2 * side) & (lane < high)
    for g, h in enumerate(stacks):
        raw = h["raw"]
        x = []
        for q in range(w + 4):
            at = 16 * g + q
            y = jnp.where(lane == high, rim["line"][:, at + 8 : at + 9], raw[q])
            x.append(jnp.where(lane == n - 1, rim["line"][:, at : at + 1], y))
        edge_l = jnp.where(lane < side, h["row_l"][0], jnp.where(lane < high, h["col_l"][1], 0.0))
        edge_r = jnp.where(lane < 2 * side, h["col_r"][0], jnp.where(rows_r, h["row_r"][0], 0.0))
        x[0] = jnp.where(first, h["col_l"][0], x[0])
        x[1] = jnp.where(first, edge_l, x[1])
        x[w + 2] = jnp.where(last, edge_r, x[w + 2])
        x[w + 3] = jnp.where(last, h["col_r"][1], x[w + 3])
        moved = [[shift(y, 1 - b) if b != 1 else y for b in range(3)] for y in x]
        own0, own1, own30, own31 = raw[2], raw[3], raw[w], raw[w + 1]
        north, south = h["north"], h["south"]
        turned_l = [jnp.where(lane < side, own0, 0.0)]
        turned_r = []
        for d in range(2):
            y = jnp.where(lane < side, h["row_l"][d], shift(own0, -d))
            turned_l.append(jnp.where(lane == n - 1, north[d], y))
            y = jnp.where(rows_r, h["row_r"][d], shift(own31, d))
            turned_r.append(jnp.where(lane == high, south[d], y))
        turned_l[1:] = [
            jnp.where((lane > side) & (lane < n - 1), 0.0, y) for y in turned_l[1:]
        ]
        turned_r = [turned_r[1], turned_r[0], jnp.where(rows_r, own31, 0.0)]
        for b in range(3):
            for a in range(3):
                for j in range(1, w + 1):
                    put(a, b, plan.segment(g, j), moved[j + a][b])
                y = shift(h["col_l"][1], 1 - b) if a == 1 else moved[a][b]
                y = jnp.where(lane < side, shift(turned_l[b], 1 - a), y)
                if b == 0:
                    over = shift(own0, 2 - a) if a < 2 else 0.0
                    y = jnp.where(lane == side, over, y)
                elif a == 2:
                    y = jnp.where(lane == high, shift((own0, own1)[b - 1], 1), y)
                    if b == 2:
                        y = jnp.where(lane == high - 1, own0, y)
                put(a, b, plan.segment(g, 0), jnp.where(first, y, moved[a][b]))
                y = shift(h["col_r"][0], 1 - b) if a == 1 else moved[w + 1 + a][b]
                y = jnp.where(rows_r, shift(turned_r[b], 1 - a), y)
                if b == 2:
                    over = shift(own31, -a) if a > 0 else 0.0
                    y = jnp.where(lane == 2 * side - 1, over, y)
                if a == 0:
                    if b == 0:
                        y = jnp.where(lane == 0, own31, y)
                    y = jnp.where(lane == n - 1, shift(own30 if b == 0 else own31, -1), y)
                put(a, b, plan.segment(g, w + 1), jnp.where(last, y, moved[w + 1 + a][b]))
    line, deep, ends = rim["line"], rim["deep"], rim["ends"]
    is_top, spot = rim["is_top"], rim["spot"]
    ends = jnp.where(last & is_top & (spot == w + 2), shift(ends, 1), ends)
    ends = jnp.where(first & jnp.logical_not(is_top) & (spot == 1), shift(ends, -1), ends)
    for g, h in enumerate(stacks):
        north = first & rim_cell(plan, lane, g, 0, 1)
        south = last & rim_cell(plan, lane, g, 1, w + 2)
        line = jnp.where(north, h["north"][0], line)
        deep = jnp.where(north, h["north"][2], deep)
        line = jnp.where(south, h["south"][0], line)
        deep = jnp.where(south, h["south"][2], deep)
    by_a = (jnp.where(is_top, ends, deep), line, jnp.where(is_top, deep, ends))
    for a in range(3):
        for b in range(3):
            put(a, b, plan.inner + plan.outer - 1, shift(by_a[a], -b) if b else by_a[a])


def wide_backward(plan, found, taps_ref, inner):
    stacks, rim, lane, first, last = found
    w, n, side, high, c = plan.cols, plan.lanes, plan.side, plan.height, plan.channels

    def put(row, segment, value):
        if (segment < plan.inner) != inner:
            return
        segment -= 0 if inner else plan.inner
        taps_ref[row * c : (row + 1) * c, segment * n : (segment + 1) * n] = value.astype(BF16)

    zero = jnp.zeros(lane.shape, F32)
    rows_l = lane < side
    rows_r = (lane >= 2 * side) & (lane < high)
    for g, h in enumerate(stacks):
        raw = h["raw"]
        z = list(raw)
        edge_l = jnp.where((lane >= side) & (lane <= high), h["col_l"][1], 0.0)
        edge_r = jnp.where((lane < 2 * side) | (lane == n - 1), h["col_r"][0], 0.0)
        z[1] = jnp.where(first, edge_l, z[1])
        z[w + 2] = jnp.where(last, edge_r, z[w + 2])
        moved = [[shift(y, b - 1) if b != 1 else y for b in range(3)] for y in z]
        keep_l = (lane >= side) | jnp.logical_not(first)
        keep_r = (lane < 2 * side) | jnp.logical_not(last)
        own0, own1, own30, own31 = raw[2], raw[3], raw[w], raw[w + 1]
        north, south = h["north"], h["south"]
        line_l = [jnp.where(rows_l, y, 0.0) for y in h["row_l"]]
        line_r = [jnp.where(rows_r, y, 0.0) for y in h["row_r"]]
        line_l = [line_l[1], line_l[0], zero]
        line_r = [zero, line_r[0], line_r[1]]
        keep = (lane >= side) & (lane <= high + 1)
        deep_l = [zero] + [jnp.where(keep, h["col_l"][i], 0.0) for i in (1, 0)]
        keep = (lane < 2 * side) | (lane >= n - 2)
        deep_r = [jnp.where(keep, h["col_r"][i], 0.0) for i in (1, 0)] + [zero]
        for b in range(3):
            for a in range(3):
                tap = a * 3 + b
                for j in range(1, w + 1):
                    y = moved[j + 2 - a][b]
                    if j == 1 and a == 2:
                        y = jnp.where(keep_l, y, 0.0)
                    if j == w and a == 0:
                        y = jnp.where(keep_r, y, 0.0)
                    put(tap, plan.segment(g, j), y)
                y = jnp.where(rows_l, shift(line_l[b], a - 1), shift(deep_l[a], b - 1))
                if a == 0:
                    y = jnp.where(lane == side - 1, shift(own0, b - 2), y)
                    y = jnp.where(lane == side, shift(own0, b), y)
                put(tap, plan.segment(g, 0), jnp.where(first, y, moved[2 - a][b]))
                y = jnp.where(rows_r, shift(line_r[b], a - 1), shift(deep_r[a], b - 1))
                if a == 2:
                    y = jnp.where(lane == 2 * side - 1, shift(own31, b - 2), y)
                    y = jnp.where(lane == 2 * side, shift(own31, b), y)
                put(tap, plan.segment(g, w + 1), jnp.where(last, y, moved[w + 3 - a][b]))
        for j in range(w + 2):
            segment = plan.segment(g, j)
            for b in range(3):
                at = 16 * g + j + 2 - b
                top = jnp.where(lane == 0, rim["line"][:, at : at + 1], 0.0)
                bottom = jnp.where(lane == high - 1, rim["line"][:, at + 8 : at + 9], 0.0)
                left = right = zero
                if j == 0:
                    own = jnp.where(lane < high, shift(own0, b - 1), 0.0)
                    top = jnp.where(first, own, top)
                    bottom = jnp.where(first, 0.0, bottom)
                    if b < 2:
                        left = jnp.where(first & (lane == 0), north[1 - b], 0.0)
                        right = jnp.where(first & (lane == high), shift((own1, own0)[b], 1), 0.0)
                if j == 1:
                    left = jnp.where(first & rows_l, shift(line_l[1], b - 1), 0.0)
                if j == w:
                    right = jnp.where(last & rows_r, shift(line_r[1], b - 1), 0.0)
                if j == w + 1:
                    own = jnp.where(lane < high, shift(own31, b - 1), 0.0)
                    bottom = jnp.where(last, own, bottom)
                    top = jnp.where(last, 0.0, top)
                    if b > 0:
                        over = shift((own31, own30)[b - 1], -1)
                        left = jnp.where(last & (lane == n - 1), over, 0.0)
                        right = jnp.where(last & (lane == high - 1), south[b - 1], 0.0)
                for i, y in enumerate((top, bottom, left, right)):
                    put(9 + 3 * i + b, segment, y)
    line, deep, ends = rim["line"], rim["deep"], rim["ends"]
    is_top = rim["is_top"]
    tops = [jnp.where(is_top, y, 0.0) for y in (deep, ends)]
    bottoms = [jnp.where(is_top, 0.0, y) for y in (deep, ends)]
    by_a = (tops[0], line, bottoms[0])
    segment = plan.inner + plan.outer - 1
    for b in range(3):
        for a in range(3):
            put(a * 3 + b, segment, shift(by_a[a], b - 2))
        top = bottom = zero
        for g, h in enumerate(stacks):
            if b < 2:
                over = h["north"][2 * (1 - b)]
                top = jnp.where(first & rim_cell(plan, lane, g, 0, 1), over, top)
            if b > 0:
                over = h["south"][2 * (b - 1)]
                bottom = jnp.where(last & rim_cell(plan, lane, g, 1, w), over, bottom)
        put(9 + b, segment, top)
        put(12 + b, segment, bottom)
        put(15 + b, segment, shift(tops[1], b - 2))
        put(18 + b, segment, shift(bottoms[1], b - 2))


def second_halos(plan, ids_ref, ref):
    w, n, high, side = plan.cols, plan.lanes, plan.height, plan.side
    first = ids_ref[0] == 0
    last = ids_ref[0] == plan.tiles - 1
    start = (plan.outer - 1) * n
    rim = ref[:, start : start + n].astype(F32)
    lane = lax.broadcasted_iota(jnp.int32, rim.shape, 1)
    result = []
    for g in range(plan.stacks):
        left, right = [
            ref[:, j * n : (j + 1) * n].astype(F32) for j in (2 * g, 2 * g + 1)
        ]
        top = [rim[:, 16 * g + e : 16 * g + e + 1] for e in range(w + 2)]
        bottom = [rim[:, 16 * g + 8 + e : 16 * g + 9 + e] for e in range(w + 2)]
        top[0] = jnp.where(first, 0.0, top[0])
        bottom[0] = jnp.where(first, left[:, high - 1 : high], bottom[0])
        top[w + 1] = jnp.where(last, right[:, 0:1], top[w + 1])
        bottom[w + 1] = jnp.where(last, 0.0, bottom[w + 1])
        result.append(
            dict(
                first=first,
                last=last,
                left=left,
                right=right,
                row_l=jnp.where(lane < side, left, 0.0),
                row_r=jnp.where((lane >= 2 * side) & (lane < high), right, 0.0),
                col_l=left,
                col_r=right,
                top=top,
                bottom=bottom,
            )
        )
    return result


def forward_operand(plan, own, halo, taps_ref):
    w, n, side, height = plan.cols, plan.lanes, plan.side, plan.height
    c = plan.channels
    lane = lax.broadcasted_iota(jnp.int32, (c, n), 1)
    for g in range(plan.stacks):
        h = halo[g]
        edge_l = jnp.where(lane < side, h["row_l"], jnp.where(lane < height, h["col_l"], 0.0))
        edge_r = jnp.where(
            lane < 2 * side, h["col_r"], jnp.where(lane < height, h["row_r"], 0.0)
        )
        columns = [h["left"]] + own[g] + [h["right"]]
        for j in range(w + 2):
            x = jnp.where(lane == height, h["bottom"][j], columns[j])
            x = jnp.where(lane == n - 1, h["top"][j], x)
            if j == 0:
                x = jnp.where(h["first"], edge_l, x)
            if j == w + 1:
                x = jnp.where(h["last"], edge_r, x)
            for b in range(3):
                y = (x if b == 1 else shift(x, 1 - b)).astype(BF16)
                for a in range(3):
                    out = j - a
                    if 0 <= out < w:
                        at = (g * w + out) * n
                        row = (a * 3 + b) * c
                        taps_ref[row : row + c, at : at + n] = y


def backward_operand(plan, own, halo, taps_ref):
    w, n, side, height = plan.cols, plan.lanes, plan.side, plan.height
    c = plan.channels
    lane = lax.broadcasted_iota(jnp.int32, (c, n), 1)
    zero = jnp.zeros((c, n), BF16)
    for g in range(plan.stacks):
        h = halo[g]
        first, last = h["first"], h["last"]
        edge_l = jnp.where((lane >= side) & (lane <= height), h["col_l"], 0.0)
        edge_r = jnp.where((lane < 2 * side) | (lane == n - 1), h["col_r"], 0.0)
        columns = [jnp.where(first, edge_l, h["left"])] + own[g]
        columns += [jnp.where(last, edge_r, h["right"])]
        keep_l = (lane >= side) | jnp.logical_not(first)
        keep_r = (lane < 2 * side) | jnp.logical_not(last)
        for j in range(w + 2):
            for b in range(3):
                y = columns[j] if b == 1 else shift(columns[j], b - 1)
                if j == 0:
                    y = jnp.where(keep_l, y, 0.0)
                if j == w + 1:
                    y = jnp.where(keep_r, y, 0.0)
                y = y.astype(BF16)
                for a in range(3):
                    out = j - 2 + a
                    if 0 <= out < w:
                        at = (g * w + out) * n
                        row = (a * 3 + b) * c
                        taps_ref[row : row + c, at : at + n] = y
        seam_l = first & (lane < side)
        seam_r = last & (lane >= 2 * side) & (lane < height)
        for out in range(w):
            at = (g * w + out) * n
            for b in range(3):
                y = jnp.where(lane == 0, h["top"][out + 2 - b], 0.0).astype(BF16)
                taps_ref[(9 + b) * c : (10 + b) * c, at : at + n] = y
                y = jnp.where(lane == height - 1, h["bottom"][out + 2 - b], 0.0).astype(BF16)
                taps_ref[(12 + b) * c : (13 + b) * c, at : at + n] = y
                y = zero
                if out == 0:
                    y = jnp.where(seam_l, shift(h["row_l"], b - 1), 0.0).astype(BF16)
                taps_ref[(15 + b) * c : (16 + b) * c, at : at + n] = y
                y = zero
                if out == w - 1:
                    y = jnp.where(seam_r, shift(h["row_r"], b - 1), 0.0).astype(BF16)
                taps_ref[(18 + b) * c : (19 + b) * c, at : at + n] = y


def seam_weights(kernel_ref):
    order = list(range(9)) + [0, 1, 2, 6, 7, 8, 0, 3, 6, 2, 5, 8]
    return jnp.concatenate([kernel_ref[tap] for tap in order], axis=1)


def own_columns(plan, ref):
    w, n = plan.cols, plan.lanes
    return [
        [ref[:, (g * w + i) * n : (g * w + i + 1) * n].astype(F32) for i in range(w)]
        for g in range(plan.stacks)
    ]


def kept_lanes(plan, ids_ref, shape, inner):
    flat = lax.broadcasted_iota(jnp.int32, shape, 1)
    segment, lane = flat // plan.lanes, flat % plan.lanes
    inside = lane < plan.height
    if not inner:
        first = ids_ref[0] == 0
        last = ids_ref[0] == plan.tiles - 1
        inside = inside | (segment == plan.outer - 1)
        inside = inside | ((segment % 2 == 0) & first & (lane == plan.height))
        inside = inside | ((segment % 2 == 1) & last & (lane == plan.lanes - 1))
    return inside


def with_seams(plan, ids_ref, around, tables):
    *around, got = around
    seams = seam_cells(plan, ids_ref, got, *tables[:2])
    return (*around, seams, tables[2])


def go_forward(plan, ids_ref, around, weight, fwd_ref, inner):
    wide_forward(plan, surroundings(plan, ids_ref, 0, *around), fwd_ref, inner)
    pre = product(weight[...], fwd_ref[...], 0, 0)
    bend = jnp.tanh(GELU_A * (pre + GELU_B * (pre * pre * pre)))
    half = 0.5 * (1.0 + bend)
    slope = half + 0.5 * pre * (1.0 - bend * bend) * (
        GELU_A * (1.0 + (3.0 * GELU_B) * (pre * pre))
    )
    inside = kept_lanes(plan, ids_ref, pre.shape, inner)
    return jnp.where(inside, pre * half, 0.0).astype(BF16), slope


def go_back(plan, ids_ref, around, weight, slope, bwd_ref, inner):
    wide_backward(plan, surroundings(plan, ids_ref, 1, *around), bwd_ref, inner)
    grad = product(seam_weights(weight), bwd_ref[...], 1, 0)
    inside = kept_lanes(plan, ids_ref, grad.shape, inner)
    return jnp.where(inside, grad * slope, 0.0).astype(BF16)


def outer_forward_kernel(plan, ids_ref, *refs):
    around, tables, (weight, hidden_ref, slope_ref, fwd_ref) = refs[:5], refs[5:8], refs[8:]
    around = with_seams(plan, ids_ref, around, tables)
    hidden_ref[...], slope_ref[...] = go_forward(plan, ids_ref, around, weight, fwd_ref, False)


def outer_back_kernel(plan, ids_ref, *refs):
    around, tables, (weight, slope_ref, pre_grad_ref, bwd_ref) = refs[:5], refs[5:8], refs[8:]
    around = with_seams(plan, ids_ref, around, tables)
    pre_grad_ref[...] = go_back(plan, ids_ref, around, weight, slope_ref[...], bwd_ref, False)


def inner_kernel(plan, ids_ref, *refs):
    c = plan.channels
    around, tables, weights, refs = refs[:5], refs[5:8], refs[8:10], refs[10:]
    hidden_ref, pre_grad_ref, mine_ref, theirs_ref, fwd_ref, bwd_ref, sums_ref, packed_ref = refs
    around = with_seams(plan, ids_ref, around, tables)
    hidden, slope = go_forward(plan, ids_ref, around, weights[0], fwd_ref, True)
    pre_grad = go_back(plan, ids_ref, around, weights[1], slope, bwd_ref, True)
    hidden_ref[...] = hidden
    pre_grad_ref[...] = pre_grad
    terms = product(fwd_ref[...], pre_grad, 1, 1)
    turned = product(bwd_ref[...], hidden, 1, 1)
    tap = [turned[i * c : (i + 1) * c] for i in range(21)]
    for b in range(3):
        tap[b] = tap[b] + tap[9 + b]
        tap[6 + b] = tap[6 + b] + tap[12 + b]
    for a in range(3):
        tap[3 * a] = tap[3 * a] + tap[15 + a]
        tap[3 * a + 2] = tap[3 * a + 2] + tap[18 + a]
    sums_ref[0 : 9 * c, :] = terms
    for i in range(9):
        sums_ref[(9 + i) * c : (10 + i) * c, :] = jnp.transpose(tap[i])
    packed_rows = max(plan.folds - 1, 1) * plan.fold_rows
    shared = (plan.folds - 1) * plan.fold_rows
    for i in range(max(plan.folds - 1, 1)):
        at = i * plan.fold_rows
        block = sums_ref[at : at + plan.fold_rows, :]
        if plan.folds > 1:
            rest = plan.wide - c
            more = sums_ref[shared : shared + plan.fold_rows, i * rest : (i + 1) * rest]
            block = jnp.concatenate([block, more], axis=1)
        packed_ref[at : at + plan.fold_rows, :] = block
    spare = packed_ref.shape[0] - packed_rows
    if spare:
        packed_ref[packed_rows:, :] = jnp.zeros((spare, plan.wide), F32)
    near, mid = ids_ref[3], ids_ref[4]
    for d in range(plan.mid):
        spot = jnp.bitwise_xor(mid, d)
        for other, ref in ((0, mine_ref), (1, theirs_ref)):
            at = (jnp.bitwise_xor(near, other) * plan.mid + spot) * plan.piece
            rows = packed_ref[pl.ds(pl.multiple_of(at, 16), plan.piece), :]
            ref[d] = rows.astype(ref.dtype)


def last_kernel(plan, ids_ref, hidden_ref, pre_grad_ref, hidden_out, pre_grad_out, *refs):
    w_two, w_one, out_ref, back_ref, fwd_ref, bwd_ref = refs
    w, n = plan.cols, plan.lanes
    halo = second_halos(plan, ids_ref, hidden_out)
    forward_operand(plan, own_columns(plan, hidden_ref), halo, fwd_ref)
    halo = second_halos(plan, ids_ref, pre_grad_out)
    backward_operand(plan, own_columns(plan, pre_grad_ref), halo, bwd_ref)
    out = product(w_two[...], fwd_ref[...], 0, 0).astype(BF16)
    back = product(seam_weights(w_one), bwd_ref[...], 1, 0).astype(BF16)
    for g in range(plan.stacks):
        for i in range(w):
            at = (g * w + i) * n
            out_ref[:, g, i, :] = out[:, at : at + plan.height]
            back_ref[:, g, i, :] = back[:, at : at + plan.height]


def sum_kernel(plan, scale, ids_ref, mine_ref, theirs_ref, one_ref, two_ref, packed_ref, sums_ref):
    near, mid = ids_ref[3], ids_ref[4]
    for d in range(plan.mid):
        spot = jnp.bitwise_xor(mid, d)
        for other, ref in ((0, mine_ref), (1, theirs_ref)):
            at = (jnp.bitwise_xor(near, other) * plan.mid + spot) * plan.piece
            packed_ref[pl.ds(pl.multiple_of(at, 16), plan.piece), :] = ref[d].astype(F32) * scale
    c, shared = plan.channels, (plan.folds - 1) * plan.fold_rows
    more = []
    for i in range(max(plan.folds - 1, 1)):
        at = i * plan.fold_rows
        block = packed_ref[at : at + plan.fold_rows, :]
        sums_ref[at : at + plan.fold_rows, :] = block[:, :c]
        more.append(block[:, c:])
    if plan.folds > 1:
        sums_ref[shared : shared + plan.fold_rows, :] = jnp.concatenate(more, axis=1)
    rows = one_ref.shape[0]
    one_ref[...] = sums_ref[:rows]
    two_ref[...] = sums_ref[rows : 2 * rows]


VMEM = pl.BlockSpec(memory_space=pltpu.VMEM)
SMEM = pl.BlockSpec(memory_space=pltpu.SMEM)


def call(body, ids, inputs, outs, scratch=()):
    return pl.pallas_call(
        body,
        out_shape=outs,
        in_specs=[SMEM] + [VMEM] * len(inputs),
        out_specs=[VMEM] * len(outs),
        scratch_shapes=list(scratch),
        compiler_params=pltpu.CompilerParams(vmem_limit_bytes=48 * 2**20),
    )(ids, *inputs)


def across_faces(plan, columns, step):
    t, f = plan.tiles, plan.faces
    first = lax.axis_index("tile") == 0
    sent = jnp.where(first, columns[:2], columns[plan.cols - 2 :])
    pairs = [((t - 1) * f + i, (t - 1) * f + (i + step) % f) for i in range(f)]
    pairs += [((i + step) % f, i) for i in range(f)]
    return lax.ppermute(sent, BOTH, pairs)


def pair_up(plan, columns, passed):
    t, g = plan.tiles, plan.stacks
    tile = lax.axis_index("tile")
    even = tile % 2 == 0
    head, tail = columns[:2], columns[plan.cols - 2 :]
    inner = jnp.where(even, tail, head)
    outer = jnp.where(even, head, tail)
    passed = jnp.where(tile == 0, passed[:, :, :1], passed[:, :, g - 1 :])
    to_last = jnp.concatenate([head[:, :, 1:], passed], axis=2)
    to_first = jnp.concatenate([passed, tail[:, :, : g - 1]], axis=2)
    outer = jnp.where(tile == 0, to_last, jnp.where(tile == t - 1, to_first, outer))
    inner = lax.ppermute(inner, "tile", [(i, i ^ 1) for i in range(t)])
    outer = lax.ppermute(outer, "tile", [(i, ((i + 1) ^ 1) - 1 if i else t - 1) for i in range(t - 1)] + [(t - 1, 0)])
    return inner, outer


def spread_blocks(plan, blocks):
    count = plan.tiles * plan.faces
    flat = blocks.reshape((count,) + blocks.shape[2:])
    return lax.all_to_all(flat, BOTH, 0, 0, tiled=True).reshape(blocks.shape)


def swapped(plan, x, near=0, mid=0, far=0):
    f = plan.faces
    pairs = []
    for i in range(plan.tiles * f):
        tile, face = i // f, i % f
        tile = tile ^ near ^ ((mid // f) << 1) ^ (far << 2)
        pairs.append((i, tile * f + (face ^ (mid % f))))
    return lax.ppermute(x, BOTH, pairs)


def tree_sum(values):
    while len(values) > 1:
        values = [a + b for a, b in zip(values[::2], values[1::2])]
    return values[0]


def sum_all(plan, mine, theirs, beside):
    half = mine + swapped(plan, theirs, near=1).astype(F32)
    short = half.astype(BF16)
    got = [swapped(plan, short[d], mid=d) for d in range(1, plan.mid)]
    got, kept = lax.optimization_barrier((got, beside[0](None)))
    piece = tree_sum([half[0]] + [x.astype(F32) for x in got]).astype(BF16)
    got = [swapped(plan, piece, far=d) for d in range(1, plan.far)]
    got, kept = lax.optimization_barrier((got, beside[1](kept)))
    piece = tree_sum([x.astype(F32) for x in [piece] + got]).astype(BF16)
    pieces = [piece] + [swapped(plan, piece, mid=d) for d in range(1, plan.mid)]
    pieces, kept = lax.optimization_barrier((pieces, beside[2](kept)))
    half = jnp.stack(pieces)
    return half, swapped(plan, half, near=1), kept


def on_device(mesh_shape, fields, upstream, kernel_one, kernel_two):
    plan = Plan(mesh_shape, fields.shape)
    c, own, w, n = plan.channels, plan.own, plan.cols, plan.lanes
    g, h = plan.stacks, plan.height
    tile, face = lax.axis_index("tile"), lax.axis_index("face")
    sub = lax.axis_index("sub")
    mid = ((tile >> 1) & 1) * plan.faces + face
    kind = jnp.where(tile == 0, 0, jnp.where(tile == plan.tiles - 1, 2, 1))
    ids = jnp.stack([tile, face, sub, tile & 1, mid, kind]).astype(jnp.int32)
    if mesh_shape["sub"] > 1:
        fields = lax.all_gather(fields, "sub", axis=0, tiled=True)
        upstream = lax.all_gather(upstream, "sub", axis=0, tiled=True)

    both = jnp.stack([fields, upstream]).transpose(3, 0, 2, 1, 4)
    columns = jnp.pad(both, ((0, 0),) * 4 + ((0, n - h),))
    blocks_shape = jax.ShapeDtypeStruct((plan.tiles, plan.faces, plan.block, c), BF16)
    (blocks,) = call(
        functools.partial(first_kernel, plan), ids, [plan.send_table(), columns], [blocks_shape]
    )
    passed = across_faces(plan, columns, 1)
    across = passed if g == 2 else across_faces(plan, columns, 2)
    got = spread_blocks(plan, blocks)
    sent, passed, _ = lax.optimization_barrier((columns, passed, blocks))
    halo = (*pair_up(plan, sent, passed), across, got)

    fwd_one = kernel_one.reshape(9 * c, c)
    bwd_two = kernel_two.reshape(9, c, c)
    fwd_two = lax.dynamic_slice_in_dim(kernel_two, sub * own, own, 3).reshape(9 * c, own)
    bwd_one = lax.dynamic_slice_in_dim(kernel_one, sub * own, own, 2).reshape(9, own, c)

    def taps(width):
        return [pltpu.VMEM((9 * c, width), BF16), pltpu.VMEM((21 * c, width), BF16)]

    piece = (plan.mid, plan.piece, plan.wide)
    rows = plan.near * plan.mid * plan.piece
    inner, outer = plan.inner * n, plan.outer * n
    given = [columns, *halo, *plan.take_tables()]
    hidden, pre_grad, mine, theirs = call(
        functools.partial(inner_kernel, plan),
        ids,
        given + [fwd_one, bwd_two],
        [jax.ShapeDtypeStruct((c, inner), BF16)] * 2
        + [jax.ShapeDtypeStruct(piece, F32), jax.ShapeDtypeStruct(piece, BF16)],
        taps(inner)
        + [pltpu.VMEM((plan.terms, c), F32), pltpu.VMEM((rows, plan.wide), F32)],
    )
    theirs, given, hidden, pre_grad = lax.optimization_barrier((theirs, given, hidden, pre_grad))

    def outer_forward(unused):
        return call(
            functools.partial(outer_forward_kernel, plan),
            ids,
            given + [fwd_one],
            [jax.ShapeDtypeStruct((c, outer), BF16), jax.ShapeDtypeStruct((c, outer), F32)],
            taps(outer)[:1],
        )

    def outer_back(kept):
        hidden_out, slope = kept
        (pre_grad_out,) = call(
            functools.partial(outer_back_kernel, plan),
            ids,
            given + [bwd_two, slope],
            [jax.ShapeDtypeStruct((c, outer), BF16)],
            taps(outer)[1:],
        )
        return hidden_out, pre_grad_out

    def finish(kept):
        return call(
            functools.partial(last_kernel, plan),
            ids,
            [hidden, pre_grad, *kept, fwd_two, bwd_one],
            [jax.ShapeDtypeStruct((own, g, w, h), BF16)] * 2,
            taps(inner),
        )

    mine, theirs, (result, fields_grad) = sum_all(
        plan, mine, theirs, (outer_forward, outer_back, finish)
    )
    scale = 1.0 / (plan.side * 12.0**0.5)
    sums = call(
        functools.partial(sum_kernel, plan, scale),
        ids,
        [mine, theirs],
        [jax.ShapeDtypeStruct((9 * c, c), F32)] * 2,
        [pltpu.VMEM((rows, plan.wide), F32), pltpu.VMEM((plan.terms, c), F32)],
    )
    grads = []
    for i in range(2):
        grad = sums[i].reshape(3, 3, c, c)
        grads.append(lax.dynamic_slice_in_dim(grad, sub * own, own, 3))
    return (
        result,
        fields_grad,
        grads[0],
        grads[1],
    )


def solution(mesh):
    placed = (P("sub", "face", "tile", "parts"), P("sub", "face", "tile", "parts"), P(), P())
    return jax.shard_map(
        functools.partial(on_device, dict(mesh.shape)),
        mesh=mesh,
        in_specs=placed,
        out_specs=(
            P("sub", "face", "tile", "parts"),
            P("sub", "face", "tile", "parts"),
            P("parts", None, None, "sub"),
            P("parts", None, None, "sub"),
        ),
        check_vma=False,
    )
```

```python
import functools

import jax
import jax.numpy as jnp
import numpy as np
from jax import lax
from jax.experimental import pallas as pl
from jax.experimental.pallas import tpu as pltpu
from jax.sharding import PartitionSpec as P

BOTH = ("tile", "face")
F32 = jnp.float32
BF16 = jnp.bfloat16
GELU_A = 0.7978845608028654
GELU_B = 0.044715


def up_to(value, step):
    return -(-value // step) * step


class Plan:
    def __init__(self, mesh_shape, block):
        self.tiles = mesh_shape["tile"]
        self.faces = mesh_shape["face"]
        self.stacks, self.cols, self.height = block[1:4]
        self.side = self.height // 3
        self.lanes = up_to(self.height + 2, 128)
        self.channels = block[0] * mesh_shape["sub"]
        self.own = block[0]
        w = self.cols
        assert w == 2
        self.reach = w + 4
        self.cells = 2 * self.reach
        self.block = 2 * self.cells
        self.kinds = 2 if self.stacks > 1 else 1
        self.inner = self.stacks * w
        self.outer = self.stacks * 2 + 1
        self.lines = up_to(16 * self.stacks, 32)
        assert self.lines + self.stacks * self.side <= self.lanes
        self.near = 2
        self.mid = 2 * self.faces
        self.far = self.tiles // 4
        self.terms = 2 * 9 * self.channels
        self.wide = self.channels
        rest = -self.channels % 128
        self.folds = 1
        if rest and self.channels % rest == 0 and self.terms % (8 * (self.channels // rest + 1)) == 0:
            self.folds = self.channels // rest + 1
            self.wide = self.channels + rest
        self.fold_rows = self.terms // self.folds
        packed = self.fold_rows * max(self.folds - 1, 1)
        self.piece = up_to(-(-packed // (self.near * self.mid)), 16)

    def segment(self, stack, slot):
        if 1 <= slot <= self.cols:
            return stack * self.cols + slot - 1
        return self.inner + 2 * stack + (1 if slot else 0)

    def spot(self, depth, e):
        return depth * self.reach + e

    def send_table(self):
        t, k, c = self.tiles, self.kinds, self.block
        g, w, n = self.stacks, self.cols, self.lanes
        high = self.height - 1
        table = np.full((3, t, k, c), -1, np.int32)
        for dest in range(t):
            for kind in range(k):
                same = kind == 0 and k == 2
                from_a = 1 if same else 0
                from_b = 0 if same else g - 1

                def cell(stack, col, row):
                    return (stack * w + col) * n + row

                for depth in range(2):
                    for e in range(self.reach):
                        at = self.spot(depth, e)
                        row = w * dest - 2 + e
                        if 0 <= row:
                            table[0, dest, kind, at] = cell(from_a, depth, row)
                        row = 2 * self.side + w * dest - 2 + e
                        if row <= high:
                            table[2, dest, kind, at] = cell(from_b, w - 1 - depth, row)
                    for e in range(w):
                        if dest == 0:
                            table[:2, dest, kind, self.spot(depth, e)] = cell(from_b, e, depth)
                        if dest == t - 1:
                            at = self.spot(depth, w + 2 + e)
                            table[1:, dest, kind, at] = cell(from_a, e, high - depth)
        return jnp.asarray(table.reshape(3, 1, -1))

    def take_tables(self):
        t, c, w, n = self.tiles, self.block, self.cols, self.lanes
        from_a = np.zeros((t, 2, self.cells, 2, 4, n), np.float32)
        from_b = np.zeros((t, 2, self.cells, 2, 4, n), np.float32)
        for depth in range(2):
            for k in range(2):
                for src in range(t):
                    for e in range(w):
                        if src > 0:
                            at = self.spot(depth, w + 2 + e)
                            from_a[src, k, at, k, depth, 2 * self.side + src * w + e] = 1
                        if src < t - 1:
                            from_b[src, k, self.spot(depth, e), k, depth, src * w + e] = 1
                for e in range(self.reach):
                    at = self.spot(depth, e)
                    from_a[0, k, at, k, 2 + depth, e] = 1
                    from_b[t - 1, k, at, k, 2 + depth, 8 + e] = 1
        ends = np.zeros((self.reach, n, n), np.float32)
        for e in range(self.reach):
            ends[e, 0, e] = 1
            ends[e, self.height - 1, 8 + e] = 1
        shape = (t * c, 8 * n)
        return (
            jnp.asarray(from_a.reshape(shape), BF16),
            jnp.asarray(from_b.reshape(shape), BF16),
            jnp.asarray(ends.reshape(-1, n), BF16),
        )


def first_kernel(plan, ids_ref, table_ref, columns_ref, blocks_ref):
    t, c, g, w = plan.tiles, plan.block, plan.stacks, plan.cols
    face = ids_ref[1]
    flat = [
        jnp.concatenate([columns_ref[i, k, j] for j in range(g) for i in range(w)], axis=1)
        for k in range(2)
    ]
    wanted = table_ref[ids_ref[5]]
    cell = lax.broadcasted_iota(jnp.int32, (flat[0].shape[1], wanted.shape[1]), 0)
    pick = jnp.where(cell == wanted, 1.0, 0.0).astype(BF16)
    picked = product(jnp.concatenate(flat, axis=0), pick, 1, 0)
    channels = flat[0].shape[0]
    both = jnp.transpose(picked[:channels] + pltpu.roll(picked[channels:], plan.cells, 1))
    both = both.reshape(t, plan.kinds, c, both.shape[-1])
    for dest in range(plan.faces):
        if plan.kinds == 2:
            block = jnp.where(face == dest, both[:, 0], both[:, 1])
        else:
            block = both[:, 0]
        blocks_ref[:, dest] = block.astype(BF16)


def product(x, y, x_dim, y_dim):
    return lax.dot_general(x, y, (((x_dim,), (y_dim,)), ((), ())), preferred_element_type=F32)


def shift(x, by):
    return pltpu.roll(x, by % x.shape[1], 1)


def seam_cells(plan, ids_ref, got_ref, tab_a, tab_b):
    face = ids_ref[1]
    after = lax.rem(face + 1, plan.faces)
    before = lax.rem(face + plan.faces - 1, plan.faces)
    result = []
    for g in range(plan.stacks):
        face_a = face if g < plan.stacks - 1 else after
        face_b = face if g > 0 else before
        pair = []
        for at, table in ((face_a, tab_a), (face_b, tab_b)):
            rows = got_ref[:, at].astype(F32)
            rows = rows.reshape(plan.tiles * plan.block, rows.shape[-1])
            pair.append(product(rows.astype(BF16), table[...], 0, 0))
        result.append(pair)
    return result


def surroundings(plan, ids_ref, k, columns_ref, inner_ref, outer_ref, across_ref, seams_of, tab_ends):
    w, n, side = plan.cols, plan.lanes, plan.side
    high, g_count = plan.height, plan.stacks
    first = ids_ref[0] == 0
    last = ids_ref[0] == plan.tiles - 1
    even = lax.rem(ids_ref[0], 2) == 0
    shape = (plan.channels, n)
    lane = lax.broadcasted_iota(jnp.int32, shape, 1)
    stacks = []
    line, deep, ends = [jnp.zeros(shape, F32) for _ in range(3)]
    for g in range(g_count):
        start = 4 * k * n
        seams = [
            [x[:, start + i * n : start + (i + 1) * n] for i in range(4)] for x in seams_of[g]
        ]
        line += shift(seams[0][2] + seams[1][2], 16 * g)
        deep += shift(seams[0][3] + seams[1][3], 16 * g)
        raw = [jnp.where(even, outer_ref[i, k, g], inner_ref[i, k, g]) for i in range(2)]
        raw += [columns_ref[i, k, g] for i in range(w)]
        raw += [jnp.where(even, inner_ref[i, k, g], outer_ref[i, k, g]) for i in range(2)]
        ends += shift(product(jnp.concatenate(raw, axis=1), tab_ends[...], 1, 0), 16 * g)
        raw = [x.astype(F32) for x in raw]
        for d in range(2):
            for i in range(2):
                here = lane == side - 2 + i
                seams[1][d] = jnp.where(here, shift(raw[i], side - 2 + i - d), seams[1][d])
                here = lane == 2 * side + i
                by = 2 * side + i - (high - 1 - d)
                seams[0][d] = jnp.where(here, shift(raw[w + 2 + i], by), seams[0][d])
        pole = [across_ref[i, k, g].astype(F32) for i in range(2)]
        north = [pole[0][:, :1], pole[1][:, :1], pole[0][:, 1:2]]
        south = [pole[1][:, high - 1 : high], pole[0][:, high - 1 : high]]
        south.append(pole[1][:, high - 2 : high - 1])
        stacks.append(
            dict(
                raw=raw,
                row_l=seams[1][:2],
                row_r=seams[0][:2],
                col_l=[shift(x, plan.side) for x in raw[:2]],
                col_r=[shift(x, -plan.side) for x in raw[w + 2 :]],
                north=north,
                south=south,
            )
        )
    spot = lane % 8
    is_top = (lane % 16) < 8
    unsent = (first & is_top & (spot < 2)) | (last & jnp.logical_not(is_top) & (spot >= w + 2))
    line = jnp.where(unsent, 0.0, line)
    deep = jnp.where(unsent, 0.0, deep)
    ends = jnp.where(first & (spot < 2), 0.0, ends)
    ends = jnp.where(last & (spot >= w + 2), 0.0, ends)
    rim = dict(line=line, deep=deep, ends=ends, spot=spot, is_top=is_top)
    return stacks, rim, lane, first, last


def rim_cell(plan, lane, g, bottom, e):
    return lane == 16 * g + 8 * bottom + e


def wide_forward(plan, found, taps_ref, inner):
    stacks, rim, lane, first, last = found
    w, n, side, high, c = plan.cols, plan.lanes, plan.side, plan.height, plan.channels

    def put(a, b, segment, value):
        if (segment < plan.inner) != inner:
            return
        segment -= 0 if inner else plan.inner
        row = (a * 3 + b) * c
        taps_ref[row : row + c, segment * n : (segment + 1) * n] = value.astype(BF16)

    rows_r = (lane >= 2 * side) & (lane < high)
    for g, h in enumerate(stacks):
        raw = h["raw"]
        x = []
        for q in range(w + 4):
            at = 16 * g + q
            y = jnp.where(lane == high, rim["line"][:, at + 8 : at + 9], raw[q])
            x.append(jnp.where(lane == n - 1, rim["line"][:, at : at + 1], y))
        edge_l = jnp.where(lane < side, h["row_l"][0], jnp.where(lane < high, h["col_l"][1], 0.0))
        edge_r = jnp.where(lane < 2 * side, h["col_r"][0], jnp.where(rows_r, h["row_r"][0], 0.0))
        x[0] = jnp.where(first, h["col_l"][0], x[0])
        x[1] = jnp.where(first, edge_l, x[1])
        x[w + 2] = jnp.where(last, edge_r, x[w + 2])
        x[w + 3] = jnp.where(last, h["col_r"][1], x[w + 3])
        moved = [[shift(y, 1 - b) if b != 1 else y for b in range(3)] for y in x]
        own0, own1, own30, own31 = raw[2], raw[3], raw[w], raw[w + 1]
        north, south = h["north"], h["south"]
        turned_l = [jnp.where(lane < side, own0, 0.0)]
        turned_r = []
        for d in range(2):
            y = jnp.where(lane < side, h["row_l"][d], shift(own0, -d))
            turned_l.append(jnp.where(lane == n - 1, north[d], y))
            y = jnp.where(rows_r, h["row_r"][d], shift(own31, d))
            turned_r.append(jnp.where(lane == high, south[d], y))
        turned_l[1:] = [
            jnp.where((lane > side) & (lane < n - 1), 0.0, y) for y in turned_l[1:]
        ]
        turned_r = [turned_r[1], turned_r[0], jnp.where(rows_r, own31, 0.0)]
        for b in range(3):
            for a in range(3):
                for j in range(1, w + 1):
                    put(a, b, plan.segment(g, j), moved[j + a][b])
                y = shift(h["col_l"][1], 1 - b) if a == 1 else moved[a][b]
                y = jnp.where(lane < side, shift(turned_l[b], 1 - a), y)
                if b == 0:
                    over = shift(own0, 2 - a) if a < 2 else 0.0
                    y = jnp.where(lane == side, over, y)
                elif a == 2:
                    y = jnp.where(lane == high, shift((own0, own1)[b - 1], 1), y)
                    if b == 2:
                        y = jnp.where(lane == high - 1, own0, y)
                put(a, b, plan.segment(g, 0), jnp.where(first, y, moved[a][b]))
                y = shift(h["col_r"][0], 1 - b) if a == 1 else moved[w + 1 + a][b]
                y = jnp.where(rows_r, shift(turned_r[b], 1 - a), y)
                if b == 2:
                    over = shift(own31, -a) if a > 0 else 0.0
                    y = jnp.where(lane == 2 * side - 1, over, y)
                if a == 0:
                    if b == 0:
                        y = jnp.where(lane == 0, own31, y)
                    y = jnp.where(lane == n - 1, shift(own30 if b == 0 else own31, -1), y)
                put(a, b, plan.segment(g, w + 1), jnp.where(last, y, moved[w + 1 + a][b]))
    line, deep, ends = rim["line"], rim["deep"], rim["ends"]
    is_top, spot = rim["is_top"], rim["spot"]
    ends = jnp.where(last & is_top & (spot == w + 2), shift(ends, 1), ends)
    ends = jnp.where(first & jnp.logical_not(is_top) & (spot == 1), shift(ends, -1), ends)
    for g, h in enumerate(stacks):
        north = first & rim_cell(plan, lane, g, 0, 1)
        south = last & rim_cell(plan, lane, g, 1, w + 2)
        line = jnp.where(north, h["north"][0], line)
        deep = jnp.where(north, h["north"][2], deep)
        line = jnp.where(south, h["south"][0], line)
        deep = jnp.where(south, h["south"][2], deep)
    by_a = (jnp.where(is_top, ends, deep), line, jnp.where(is_top, deep, ends))
    for a in range(3):
        for b in range(3):
            put(a, b, plan.inner + plan.outer - 1, shift(by_a[a], -b) if b else by_a[a])


def wide_backward(plan, found, taps_ref, inner, edge_ref=None):
    stacks, rim, lane, first, last = found
    w, n, side, high, c = plan.cols, plan.lanes, plan.side, plan.height, plan.channels

    def put(row, segment, value):
        if (segment < plan.inner) != inner or (inner and row >= 9):
            return
        segment -= 0 if inner else plan.inner
        taps_ref[row * c : (row + 1) * c, segment * n : (segment + 1) * n] = value.astype(BF16)

    zero = jnp.zeros(lane.shape, F32)
    rows_l = lane < side
    rows_r = (lane >= 2 * side) & (lane < high)
    lines = []
    for g, h in enumerate(stacks):
        raw = h["raw"]
        z = list(raw)
        edge_l = jnp.where((lane >= side) & (lane <= high), h["col_l"][1], 0.0)
        edge_r = jnp.where((lane < 2 * side) | (lane == n - 1), h["col_r"][0], 0.0)
        z[1] = jnp.where(first, edge_l, z[1])
        z[w + 2] = jnp.where(last, edge_r, z[w + 2])
        moved = [[shift(y, b - 1) if b != 1 else y for b in range(3)] for y in z]
        keep_l = (lane >= side) | jnp.logical_not(first)
        keep_r = (lane < 2 * side) | jnp.logical_not(last)
        own0, own1, own30, own31 = raw[2], raw[3], raw[w], raw[w + 1]
        north, south = h["north"], h["south"]
        line_l = [jnp.where(rows_l, y, 0.0) for y in h["row_l"]]
        line_r = [jnp.where(rows_r, y, 0.0) for y in h["row_r"]]
        line_l = [line_l[1], line_l[0], zero]
        line_r = [zero, line_r[0], line_r[1]]
        lines.append((line_l[1], line_r[1]))
        keep = (lane >= side) & (lane <= high + 1)
        deep_l = [zero] + [jnp.where(keep, h["col_l"][i], 0.0) for i in (1, 0)]
        keep = (lane < 2 * side) | (lane >= n - 2)
        deep_r = [jnp.where(keep, h["col_r"][i], 0.0) for i in (1, 0)] + [zero]
        for b in range(3):
            for a in range(3):
                tap = a * 3 + b
                for j in range(1, w + 1):
                    y = moved[j + 2 - a][b]
                    if j == 1 and a == 2:
                        y = jnp.where(keep_l, y, 0.0)
                    if j == w and a == 0:
                        y = jnp.where(keep_r, y, 0.0)
                    put(tap, plan.segment(g, j), y)
                y = jnp.where(rows_l, shift(line_l[b], a - 1), shift(deep_l[a], b - 1))
                if a == 0:
                    y = jnp.where(lane == side - 1, shift(own0, b - 2), y)
                    y = jnp.where(lane == side, shift(own0, b), y)
                put(tap, plan.segment(g, 0), jnp.where(first, y, moved[2 - a][b]))
                y = jnp.where(rows_r, shift(line_r[b], a - 1), shift(deep_r[a], b - 1))
                if a == 2:
                    y = jnp.where(lane == 2 * side - 1, shift(own31, b - 2), y)
                    y = jnp.where(lane == 2 * side, shift(own31, b), y)
                put(tap, plan.segment(g, w + 1), jnp.where(last, y, moved[w + 3 - a][b]))
        for j in range(w + 2):
            segment = plan.segment(g, j)
            for b in range(3):
                at = 16 * g + j + 2 - b
                top = jnp.where(lane == 0, rim["line"][:, at : at + 1], 0.0)
                bottom = jnp.where(lane == high - 1, rim["line"][:, at + 8 : at + 9], 0.0)
                left = right = zero
                if j == 0:
                    own = jnp.where(lane < high, shift(own0, b - 1), 0.0)
                    top = jnp.where(first, own, top)
                    bottom = jnp.where(first, 0.0, bottom)
                    if b < 2:
                        left = jnp.where(first & (lane == 0), north[1 - b], 0.0)
                        right = jnp.where(first & (lane == high), shift((own1, own0)[b], 1), 0.0)
                if j == 1:
                    left = jnp.where(first & rows_l, shift(line_l[1], b - 1), 0.0)
                if j == w:
                    right = jnp.where(last & rows_r, shift(line_r[1], b - 1), 0.0)
                if j == w + 1:
                    own = jnp.where(lane < high, shift(own31, b - 1), 0.0)
                    bottom = jnp.where(last, own, bottom)
                    top = jnp.where(last, 0.0, top)
                    if b > 0:
                        over = shift((own31, own30)[b - 1], -1)
                        left = jnp.where(last & (lane == n - 1), over, 0.0)
                        right = jnp.where(last & (lane == high - 1), south[b - 1], 0.0)
                for i, y in enumerate((top, bottom, left, right)):
                    put(9 + 3 * i + b, segment, y)
    line, deep, ends = rim["line"], rim["deep"], rim["ends"]
    is_top = rim["is_top"]
    if inner:
        here = (rim["spot"] >= 1) & (rim["spot"] <= w) & (lane < plan.lines)
        for b in range(3):
            near = jnp.where(here, shift(line, b - 2), 0.0)
            left = right = zero
            for g, (line_l, line_r) in enumerate(lines):
                at = plan.lines + g * side
                y = jnp.where(first & rows_l, shift(line_l, b - 1), 0.0)
                left += shift(y, at)
                y = jnp.where(last & rows_r, shift(line_r, b - 1), 0.0)
                right += shift(y, at - 2 * side)
            top, bottom = jnp.where(is_top, near, 0.0), jnp.where(is_top, 0.0, near)
            for i, y in enumerate((top, bottom, left, right)):
                row = (3 * i + b) * c
                edge_ref[row : row + c, :] = y.astype(BF16)
        return
    tops = [jnp.where(is_top, y, 0.0) for y in (deep, ends)]
    bottoms = [jnp.where(is_top, 0.0, y) for y in (deep, ends)]
    by_a = (tops[0], line, bottoms[0])
    segment = plan.inner + plan.outer - 1
    for b in range(3):
        for a in range(3):
            put(a * 3 + b, segment, shift(by_a[a], b - 2))
        top = bottom = zero
        for g, h in enumerate(stacks):
            if b < 2:
                over = h["north"][2 * (1 - b)]
                top = jnp.where(first & rim_cell(plan, lane, g, 0, 1), over, top)
            if b > 0:
                over = h["south"][2 * (b - 1)]
                bottom = jnp.where(last & rim_cell(plan, lane, g, 1, w), over, bottom)
        put(9 + b, segment, top)
        put(12 + b, segment, bottom)
        put(15 + b, segment, shift(tops[1], b - 2))
        put(18 + b, segment, shift(bottoms[1], b - 2))


def second_halos(plan, ids_ref, ref):
    w, n, high, side = plan.cols, plan.lanes, plan.height, plan.side
    first = ids_ref[0] == 0
    last = ids_ref[0] == plan.tiles - 1
    start = (plan.outer - 1) * n
    rim = ref[:, start : start + n].astype(F32)
    lane = lax.broadcasted_iota(jnp.int32, rim.shape, 1)
    result = []
    for g in range(plan.stacks):
        left, right = [
            ref[:, j * n : (j + 1) * n].astype(F32) for j in (2 * g, 2 * g + 1)
        ]
        top = [rim[:, 16 * g + e : 16 * g + e + 1] for e in range(w + 2)]
        bottom = [rim[:, 16 * g + 8 + e : 16 * g + 9 + e] for e in range(w + 2)]
        top[0] = jnp.where(first, 0.0, top[0])
        bottom[0] = jnp.where(first, left[:, high - 1 : high], bottom[0])
        top[w + 1] = jnp.where(last, right[:, 0:1], top[w + 1])
        bottom[w + 1] = jnp.where(last, 0.0, bottom[w + 1])
        result.append(
            dict(
                first=first,
                last=last,
                left=left,
                right=right,
                row_l=jnp.where(lane < side, left, 0.0),
                row_r=jnp.where((lane >= 2 * side) & (lane < high), right, 0.0),
                col_l=left,
                col_r=right,
                top=top,
                bottom=bottom,
            )
        )
    return result


def forward_operand(plan, own, halo, taps_ref):
    w, n, side, height = plan.cols, plan.lanes, plan.side, plan.height
    c = plan.channels
    lane = lax.broadcasted_iota(jnp.int32, (c, n), 1)
    for g in range(plan.stacks):
        h = halo[g]
        edge_l = jnp.where(lane < side, h["row_l"], jnp.where(lane < height, h["col_l"], 0.0))
        edge_r = jnp.where(
            lane < 2 * side, h["col_r"], jnp.where(lane < height, h["row_r"], 0.0)
        )
        columns = [h["left"]] + own[g] + [h["right"]]
        for j in range(w + 2):
            x = jnp.where(lane == height, h["bottom"][j], columns[j])
            x = jnp.where(lane == n - 1, h["top"][j], x)
            if j == 0:
                x = jnp.where(h["first"], edge_l, x)
            if j == w + 1:
                x = jnp.where(h["last"], edge_r, x)
            for b in range(3):
                y = (x if b == 1 else shift(x, 1 - b)).astype(BF16)
                for a in range(3):
                    out = j - a
                    if 0 <= out < w:
                        at = (g * w + out) * n
                        row = (a * 3 + b) * c
                        taps_ref[row : row + c, at : at + n] = y


def backward_operand(plan, own, halo, taps_ref):
    w, n, side, height = plan.cols, plan.lanes, plan.side, plan.height
    c = plan.channels
    lane = lax.broadcasted_iota(jnp.int32, (c, n), 1)
    zero = jnp.zeros((c, n), BF16)
    for g in range(plan.stacks):
        h = halo[g]
        first, last = h["first"], h["last"]
        edge_l = jnp.where((lane >= side) & (lane <= height), h["col_l"], 0.0)
        edge_r = jnp.where((lane < 2 * side) | (lane == n - 1), h["col_r"], 0.0)
        columns = [jnp.where(first, edge_l, h["left"])] + own[g]
        columns += [jnp.where(last, edge_r, h["right"])]
        keep_l = (lane >= side) | jnp.logical_not(first)
        keep_r = (lane < 2 * side) | jnp.logical_not(last)
        for j in range(w + 2):
            for b in range(3):
                y = columns[j] if b == 1 else shift(columns[j], b - 1)
                if j == 0:
                    y = jnp.where(keep_l, y, 0.0)
                if j == w + 1:
                    y = jnp.where(keep_r, y, 0.0)
                y = y.astype(BF16)
                for a in range(3):
                    out = j - 2 + a
                    if 0 <= out < w:
                        at = (g * w + out) * n
                        row = (a * 3 + b) * c
                        taps_ref[row : row + c, at : at + n] = y
        seam_l = first & (lane < side)
        seam_r = last & (lane >= 2 * side) & (lane < height)
        for out in range(w):
            at = (g * w + out) * n
            for b in range(3):
                y = jnp.where(lane == 0, h["top"][out + 2 - b], 0.0).astype(BF16)
                taps_ref[(9 + b) * c : (10 + b) * c, at : at + n] = y
                y = jnp.where(lane == height - 1, h["bottom"][out + 2 - b], 0.0).astype(BF16)
                taps_ref[(12 + b) * c : (13 + b) * c, at : at + n] = y
                y = zero
                if out == 0:
                    y = jnp.where(seam_l, shift(h["row_l"], b - 1), 0.0).astype(BF16)
                taps_ref[(15 + b) * c : (16 + b) * c, at : at + n] = y
                y = zero
                if out == w - 1:
                    y = jnp.where(seam_r, shift(h["row_r"], b - 1), 0.0).astype(BF16)
                taps_ref[(18 + b) * c : (19 + b) * c, at : at + n] = y


TAPS = list(range(9))
SEAMS = [0, 1, 2, 6, 7, 8, 0, 3, 6, 2, 5, 8]


def tap_weights(kernel_ref, order):
    return jnp.concatenate([kernel_ref[tap] for tap in order], axis=1)


def seam_weights(kernel_ref):
    return tap_weights(kernel_ref, TAPS + SEAMS)


def from_edges(plan, ids_ref, edges):
    w, n, side, high = plan.cols, plan.lanes, plan.side, plan.height
    first = ids_ref[0] == 0
    last = ids_ref[0] == plan.tiles - 1
    lane = lax.broadcasted_iota(jnp.int32, edges.shape, 1)
    result = []
    for g in range(plan.stacks):
        at = plan.lines + g * side
        for j in range(1, w + 1):
            top, bottom = 16 * g + j, 16 * g + 8 + j
            y = jnp.where(lane == 0, edges[:, top : top + 1], 0.0)
            y = jnp.where(lane == high - 1, edges[:, bottom : bottom + 1], y)
            if j == 1:
                y += jnp.where(first & (lane < side), shift(edges, -at), 0.0)
            if j == w:
                rows_r = last & (lane >= 2 * side) & (lane < high)
                y += jnp.where(rows_r, shift(edges, 2 * side - at), 0.0)
            result.append(y)
    return jnp.concatenate(result, axis=1)


def to_edges(plan, ids_ref, flat):
    w, n, side, high = plan.cols, plan.lanes, plan.side, plan.height
    first = ids_ref[0] == 0
    result = jnp.zeros((flat.shape[0], n), F32)
    lane = lax.broadcasted_iota(jnp.int32, result.shape, 1)
    for g in range(plan.stacks):
        own = [flat[:, (g * w + i) * n : (g * w + i + 1) * n] for i in range(w)]
        at = plan.lines + g * side
        line_l = shift(jnp.where(lane < side, own[0], 0.0), at)
        rows_r = (lane >= 2 * side) & (lane < high)
        line_r = shift(jnp.where(rows_r, own[-1], 0.0), at - 2 * side)
        result += jnp.where(first, line_l, line_r)
        for j in range(1, w + 1):
            top, bottom = 16 * g + j, 16 * g + 8 + j
            result = jnp.where(lane == top, own[j - 1][:, :1], result)
            result = jnp.where(lane == bottom, own[j - 1][:, high - 1 : high], result)
    return result.astype(BF16)


def own_columns(plan, ref):
    w, n = plan.cols, plan.lanes
    return [
        [ref[:, (g * w + i) * n : (g * w + i + 1) * n].astype(F32) for i in range(w)]
        for g in range(plan.stacks)
    ]


def kept_lanes(plan, ids_ref, shape, inner):
    flat = lax.broadcasted_iota(jnp.int32, shape, 1)
    segment, lane = flat // plan.lanes, flat % plan.lanes
    inside = lane < plan.height
    if not inner:
        first = ids_ref[0] == 0
        last = ids_ref[0] == plan.tiles - 1
        inside = inside | (segment == plan.outer - 1)
        inside = inside | ((segment % 2 == 0) & first & (lane == plan.height))
        inside = inside | ((segment % 2 == 1) & last & (lane == plan.lanes - 1))
    return inside


def with_seams(plan, ids_ref, around, tables):
    *around, got = around
    seams = seam_cells(plan, ids_ref, got, *tables[:2])
    return (*around, seams, tables[2])


def go_forward(plan, ids_ref, around, weight, fwd_ref, inner):
    wide_forward(plan, surroundings(plan, ids_ref, 0, *around), fwd_ref, inner)
    pre = product(weight[...], fwd_ref[...], 0, 0)
    bend = jnp.tanh(GELU_A * (pre + GELU_B * (pre * pre * pre)))
    half = 0.5 * (1.0 + bend)
    slope = half + 0.5 * pre * (1.0 - bend * bend) * (
        GELU_A * (1.0 + (3.0 * GELU_B) * (pre * pre))
    )
    inside = kept_lanes(plan, ids_ref, pre.shape, inner)
    return jnp.where(inside, pre * half, 0.0).astype(BF16), slope


def go_back(plan, ids_ref, around, weight, slope, bwd_ref, inner, edge_ref=None):
    wide_backward(plan, surroundings(plan, ids_ref, 1, *around), bwd_ref, inner, edge_ref)
    if inner:
        edges = product(tap_weights(weight, SEAMS), edge_ref[...], 1, 0)
        grad = product(tap_weights(weight, TAPS), bwd_ref[...], 1, 0)
        grad += from_edges(plan, ids_ref, edges)
    else:
        grad = product(seam_weights(weight), bwd_ref[...], 1, 0)
    inside = kept_lanes(plan, ids_ref, grad.shape, inner)
    return jnp.where(inside, grad * slope, 0.0).astype(BF16)


def outer_forward_kernel(plan, ids_ref, *refs):
    around, tables, (weight, hidden_ref, slope_ref, fwd_ref) = refs[:5], refs[5:8], refs[8:]
    around = with_seams(plan, ids_ref, around, tables)
    hidden_ref[...], slope_ref[...] = go_forward(plan, ids_ref, around, weight, fwd_ref, False)


def outer_back_kernel(plan, ids_ref, *refs):
    around, tables, (weight, slope_ref, pre_grad_ref, bwd_ref) = refs[:5], refs[5:8], refs[8:]
    around = with_seams(plan, ids_ref, around, tables)
    pre_grad_ref[...] = go_back(plan, ids_ref, around, weight, slope_ref[...], bwd_ref, False)


def inner_kernel(plan, ids_ref, *refs):
    c = plan.channels
    around, tables, weights, refs = refs[:5], refs[5:8], refs[8:10], refs[10:]
    hidden_ref, pre_grad_ref, mine_ref, theirs_ref, *refs = refs
    fwd_ref, bwd_ref, edge_ref, sums_ref, packed_ref = refs
    around = with_seams(plan, ids_ref, around, tables)
    hidden, slope = go_forward(plan, ids_ref, around, weights[0], fwd_ref, True)
    pre_grad = go_back(plan, ids_ref, around, weights[1], slope, bwd_ref, True, edge_ref)
    hidden_ref[...] = hidden
    pre_grad_ref[...] = pre_grad
    terms = product(fwd_ref[...], pre_grad, 1, 1)
    turned = product(bwd_ref[...], hidden, 1, 1)
    edge_cells = to_edges(plan, ids_ref, hidden.astype(F32))
    edges = product(edge_ref[...], edge_cells, 1, 1)
    tap = [turned[i * c : (i + 1) * c] for i in range(9)]
    tap += [edges[i * c : (i + 1) * c] for i in range(12)]
    for b in range(3):
        tap[b] = tap[b] + tap[9 + b]
        tap[6 + b] = tap[6 + b] + tap[12 + b]
    for a in range(3):
        tap[3 * a] = tap[3 * a] + tap[15 + a]
        tap[3 * a + 2] = tap[3 * a + 2] + tap[18 + a]
    sums_ref[0 : 9 * c, :] = terms
    for i in range(9):
        sums_ref[(9 + i) * c : (10 + i) * c, :] = jnp.transpose(tap[i])
    packed_rows = max(plan.folds - 1, 1) * plan.fold_rows
    shared = (plan.folds - 1) * plan.fold_rows
    for i in range(max(plan.folds - 1, 1)):
        at = i * plan.fold_rows
        block = sums_ref[at : at + plan.fold_rows, :]
        if plan.folds > 1:
            rest = plan.wide - c
            more = sums_ref[shared : shared + plan.fold_rows, i * rest : (i + 1) * rest]
            block = jnp.concatenate([block, more], axis=1)
        packed_ref[at : at + plan.fold_rows, :] = block
    spare = packed_ref.shape[0] - packed_rows
    if spare:
        packed_ref[packed_rows:, :] = jnp.zeros((spare, plan.wide), F32)
    near, mid = ids_ref[3], ids_ref[4]
    for d in range(plan.mid):
        spot = jnp.bitwise_xor(mid, d)
        for other, ref in ((0, mine_ref), (1, theirs_ref)):
            at = (jnp.bitwise_xor(near, other) * plan.mid + spot) * plan.piece
            rows = packed_ref[pl.ds(pl.multiple_of(at, 16), plan.piece), :]
            ref[d] = rows.astype(ref.dtype)


def last_kernel(plan, ids_ref, hidden_ref, pre_grad_ref, hidden_out, pre_grad_out, *refs):
    w_two, w_one, out_ref, back_ref, fwd_ref, bwd_ref = refs
    w, n = plan.cols, plan.lanes
    halo = second_halos(plan, ids_ref, hidden_out)
    forward_operand(plan, own_columns(plan, hidden_ref), halo, fwd_ref)
    halo = second_halos(plan, ids_ref, pre_grad_out)
    backward_operand(plan, own_columns(plan, pre_grad_ref), halo, bwd_ref)
    out = product(w_two[...], fwd_ref[...], 0, 0).astype(BF16)
    back = product(seam_weights(w_one), bwd_ref[...], 1, 0).astype(BF16)
    for g in range(plan.stacks):
        for i in range(w):
            at = (g * w + i) * n
            out_ref[:, g, i, :] = out[:, at : at + plan.height]
            back_ref[:, g, i, :] = back[:, at : at + plan.height]


def sum_kernel(plan, scale, ids_ref, mine_ref, theirs_ref, one_ref, two_ref, packed_ref):
    near, mid = ids_ref[3], ids_ref[4]
    for d in range(plan.mid):
        spot = jnp.bitwise_xor(mid, d)
        for other, ref in ((0, mine_ref), (1, theirs_ref)):
            at = (jnp.bitwise_xor(near, other) * plan.mid + spot) * plan.piece
            packed_ref[pl.ds(pl.multiple_of(at, 16), plan.piece), :] = ref[d].astype(F32) * scale
    c, rows = plan.channels, one_ref.shape[0]

    def store(at, value):
        for start, ref in ((0, one_ref), (rows, two_ref)):
            low = max(at, start)
            high = min(at + value.shape[0], start + rows)
            if low < high:
                ref[low - start : high - start, :] = value[low - at : high - at]

    more = []
    for i in range(max(plan.folds - 1, 1)):
        at = i * plan.fold_rows
        block = packed_ref[at : at + plan.fold_rows, :]
        store(at, block[:, :c])
        more.append(block[:, c:])
    if plan.folds > 1:
        store((plan.folds - 1) * plan.fold_rows, jnp.concatenate(more, axis=1))


VMEM = pl.BlockSpec(memory_space=pltpu.VMEM)
SMEM = pl.BlockSpec(memory_space=pltpu.SMEM)


def call(body, ids, inputs, outs, scratch=()):
    return pl.pallas_call(
        body,
        out_shape=outs,
        in_specs=[SMEM] + [VMEM] * len(inputs),
        out_specs=[VMEM] * len(outs),
        scratch_shapes=list(scratch),
        compiler_params=pltpu.CompilerParams(vmem_limit_bytes=48 * 2**20),
    )(ids, *inputs)


def across_faces(plan, columns, step):
    t, f = plan.tiles, plan.faces
    first = lax.axis_index("tile") == 0
    sent = jnp.where(first, columns[:2], columns[plan.cols - 2 :])
    pairs = [((t - 1) * f + i, (t - 1) * f + (i + step) % f) for i in range(f)]
    pairs += [((i + step) % f, i) for i in range(f)]
    return lax.ppermute(sent, BOTH, pairs)


def pair_up(plan, columns, passed):
    t, g = plan.tiles, plan.stacks
    tile = lax.axis_index("tile")
    even = tile % 2 == 0
    head, tail = columns[:2], columns[plan.cols - 2 :]
    inner = jnp.where(even, tail, head)
    outer = jnp.where(even, head, tail)
    passed = jnp.where(tile == 0, passed[:, :, :1], passed[:, :, g - 1 :])
    to_last = jnp.concatenate([head[:, :, 1:], passed], axis=2)
    to_first = jnp.concatenate([passed, tail[:, :, : g - 1]], axis=2)
    outer = jnp.where(tile == 0, to_last, jnp.where(tile == t - 1, to_first, outer))
    inner = lax.ppermute(inner, "tile", [(i, i ^ 1) for i in range(t)])
    outer = lax.ppermute(outer, "tile", [(i, ((i + 1) ^ 1) - 1 if i else t - 1) for i in range(t - 1)] + [(t - 1, 0)])
    return inner, outer


def spread_blocks(plan, blocks):
    count = plan.tiles * plan.faces
    flat = blocks.reshape((count,) + blocks.shape[2:])
    return lax.all_to_all(flat, BOTH, 0, 0, tiled=True).reshape(blocks.shape)


def swapped(plan, x, near=0, mid=0, far=0):
    f = plan.faces
    pairs = []
    for i in range(plan.tiles * f):
        tile, face = i // f, i % f
        tile = tile ^ near ^ ((mid // f) << 1) ^ (far << 2)
        pairs.append((i, tile * f + (face ^ (mid % f))))
    return lax.ppermute(x, BOTH, pairs)


def tree_sum(values):
    while len(values) > 1:
        values = [a + b for a, b in zip(values[::2], values[1::2])]
    return values[0]


def sum_all(plan, mine, theirs, beside):
    half = mine + swapped(plan, theirs, near=1).astype(F32)
    short = half.astype(BF16)
    got = [swapped(plan, short[d], mid=d) for d in range(1, plan.mid)]
    got, kept = lax.optimization_barrier((got, beside[0](None)))
    piece = tree_sum([half[0]] + [x.astype(F32) for x in got]).astype(BF16)
    got = [swapped(plan, piece, far=d) for d in range(1, plan.far)]
    got, kept = lax.optimization_barrier((got, beside[1](kept)))
    piece = tree_sum([x.astype(F32) for x in [piece] + got]).astype(BF16)
    pieces = [piece] + [swapped(plan, piece, mid=d) for d in range(1, plan.mid)]
    pieces, kept = lax.optimization_barrier((pieces, beside[2](kept)))
    half = jnp.stack(pieces)
    return half, swapped(plan, half, near=1), kept


def on_device(mesh_shape, fields, upstream, kernel_one, kernel_two):
    plan = Plan(mesh_shape, fields.shape)
    c, own, w, n = plan.channels, plan.own, plan.cols, plan.lanes
    g, h = plan.stacks, plan.height
    tile, face = lax.axis_index("tile"), lax.axis_index("face")
    sub = lax.axis_index("sub")
    mid = ((tile >> 1) & 1) * plan.faces + face
    kind = jnp.where(tile == 0, 0, jnp.where(tile == plan.tiles - 1, 2, 1))
    ids = jnp.stack([tile, face, sub, tile & 1, mid, kind]).astype(jnp.int32)
    if mesh_shape["sub"] > 1:
        fields = lax.all_gather(fields, "sub", axis=0, tiled=True)
        upstream = lax.all_gather(upstream, "sub", axis=0, tiled=True)

    both = jnp.stack([fields, upstream]).transpose(3, 0, 2, 1, 4)
    columns = jnp.pad(both, ((0, 0),) * 4 + ((0, n - h),))
    blocks_shape = jax.ShapeDtypeStruct((plan.tiles, plan.faces, plan.block, c), BF16)
    (blocks,) = call(
        functools.partial(first_kernel, plan), ids, [plan.send_table(), columns], [blocks_shape]
    )
    passed = across_faces(plan, columns, 1)
    across = passed if g == 2 else across_faces(plan, columns, 2)
    got = spread_blocks(plan, blocks)
    sent, passed, _ = lax.optimization_barrier((columns, passed, blocks))
    halo = (*pair_up(plan, sent, passed), across, got)

    fwd_one = kernel_one.reshape(9 * c, c)
    bwd_two = kernel_two.reshape(9, c, c)
    fwd_two = lax.dynamic_slice_in_dim(kernel_two, sub * own, own, 3).reshape(9 * c, own)
    bwd_one = lax.dynamic_slice_in_dim(kernel_one, sub * own, own, 2).reshape(9, own, c)

    def taps(width):
        return [pltpu.VMEM((9 * c, width), BF16), pltpu.VMEM((21 * c, width), BF16)]

    piece = (plan.mid, plan.piece, plan.wide)
    rows = plan.near * plan.mid * plan.piece
    inner, outer = plan.inner * n, plan.outer * n
    given = [columns, *halo, *plan.take_tables()]
    hidden, pre_grad, mine, theirs = call(
        functools.partial(inner_kernel, plan),
        ids,
        given + [fwd_one, bwd_two],
        [jax.ShapeDtypeStruct((c, inner), BF16)] * 2
        + [jax.ShapeDtypeStruct(piece, F32), jax.ShapeDtypeStruct(piece, BF16)],
        [pltpu.VMEM((9 * c, inner), BF16)] * 2
        + [pltpu.VMEM((12 * c, n), BF16)]
        + [pltpu.VMEM((plan.terms, c), F32), pltpu.VMEM((rows, plan.wide), F32)],
    )
    theirs, given, hidden, pre_grad = lax.optimization_barrier((theirs, given, hidden, pre_grad))

    def outer_forward(unused):
        return call(
            functools.partial(outer_forward_kernel, plan),
            ids,
            given + [fwd_one],
            [jax.ShapeDtypeStruct((c, outer), BF16), jax.ShapeDtypeStruct((c, outer), F32)],
            taps(outer)[:1],
        )

    def outer_back(kept):
        hidden_out, slope = kept
        (pre_grad_out,) = call(
            functools.partial(outer_back_kernel, plan),
            ids,
            given + [bwd_two, slope],
            [jax.ShapeDtypeStruct((c, outer), BF16)],
            taps(outer)[1:],
        )
        return hidden_out, pre_grad_out

    def finish(kept):
        return call(
            functools.partial(last_kernel, plan),
            ids,
            [hidden, pre_grad, *kept, fwd_two, bwd_one],
            [jax.ShapeDtypeStruct((own, g, w, h), BF16)] * 2,
            taps(inner),
        )

    mine, theirs, (result, fields_grad) = sum_all(
        plan, mine, theirs, (outer_forward, outer_back, finish)
    )
    scale = 1.0 / (plan.side * 12.0**0.5)
    sums = call(
        functools.partial(sum_kernel, plan, scale),
        ids,
        [mine, theirs],
        [jax.ShapeDtypeStruct((9 * c, c), F32)] * 2,
        [pltpu.VMEM((rows, plan.wide), F32)],
    )
    grads = []
    for i in range(2):
        grad = sums[i].reshape(3, 3, c, c)
        grads.append(lax.dynamic_slice_in_dim(grad, sub * own, own, 3))
    return (
        result,
        fields_grad,
        grads[0],
        grads[1],
    )


def solution(mesh):
    placed = (P("sub", "face", "tile", "parts"), P("sub", "face", "tile", "parts"), P(), P())
    return jax.shard_map(
        functools.partial(on_device, dict(mesh.shape)),
        mesh=mesh,
        in_specs=placed,
        out_specs=(
            P("sub", "face", "tile", "parts"),
            P("sub", "face", "tile", "parts"),
            P("parts", None, None, "sub"),
            P("parts", None, None, "sub"),
        ),
        check_vma=False,
    )
```

```python
import functools

import jax
import jax.numpy as jnp
import numpy as np
from jax import lax
from jax.experimental import pallas as pl
from jax.experimental.pallas import tpu as pltpu
from jax.sharding import PartitionSpec as P

BOTH = ("tile", "face")
F32 = jnp.float32
BF16 = jnp.bfloat16
GELU_A = 0.7978845608028654
GELU_B = 0.044715


def up_to(value, step):
    return -(-value // step) * step


class Plan:
    def __init__(self, mesh_shape, block):
        self.tiles = mesh_shape["tile"]
        self.faces = mesh_shape["face"]
        self.stacks, self.cols, self.height = block[1:4]
        self.side = self.height // 3
        self.lanes = up_to(self.height + 2, 128)
        self.channels = block[0] * mesh_shape["sub"]
        self.own = block[0]
        w = self.cols
        assert w == 2
        self.reach = w + 4
        self.cells = 2 * self.reach
        self.block = 2 * self.cells
        self.kinds = 2 if self.stacks > 1 else 1
        self.inner = self.stacks * w
        self.outer = self.stacks * 2 + 1
        self.lines = up_to(16 * self.stacks, 32)
        assert self.lines + self.stacks * self.side <= self.lanes
        self.near = 2
        self.mid = 2 * self.faces
        self.far = self.tiles // 4
        self.terms = 2 * 9 * self.channels
        self.wide = self.channels
        rest = -self.channels % 128
        self.folds = 1
        if rest and self.channels % rest == 0 and self.terms % (8 * (self.channels // rest + 1)) == 0:
            self.folds = self.channels // rest + 1
            self.wide = self.channels + rest
        self.fold_rows = self.terms // self.folds
        packed = self.fold_rows * max(self.folds - 1, 1)
        self.piece = up_to(-(-packed // (self.near * self.mid)), 16)

    def segment(self, stack, slot):
        if 1 <= slot <= self.cols:
            return stack * self.cols + slot - 1
        return self.inner + 2 * stack + (1 if slot else 0)

    def spot(self, depth, e):
        return depth * self.reach + e

    def send_table(self):
        t, k, c = self.tiles, self.kinds, self.block
        g, w, n = self.stacks, self.cols, self.lanes
        high = self.height - 1
        table = np.full((3, t, k, c), -1, np.int32)
        for dest in range(t):
            for kind in range(k):
                same = kind == 0 and k == 2
                from_a = 1 if same else 0
                from_b = 0 if same else g - 1

                def cell(stack, col, row):
                    return (stack * w + col) * n + row

                for depth in range(2):
                    for e in range(self.reach):
                        at = self.spot(depth, e)
                        row = w * dest - 2 + e
                        if 0 <= row:
                            table[0, dest, kind, at] = cell(from_a, depth, row)
                        row = 2 * self.side + w * dest - 2 + e
                        if row <= high:
                            table[2, dest, kind, at] = cell(from_b, w - 1 - depth, row)
                    for e in range(w):
                        if dest == 0:
                            table[:2, dest, kind, self.spot(depth, e)] = cell(from_b, e, depth)
                        if dest == t - 1:
                            at = self.spot(depth, w + 2 + e)
                            table[1:, dest, kind, at] = cell(from_a, e, high - depth)
        return jnp.asarray(table.reshape(3, 1, -1))

    def take_tables(self):
        t, c, w, n = self.tiles, self.block, self.cols, self.lanes
        from_a = np.zeros((t, 2, self.cells, 2, 4, n), np.float32)
        from_b = np.zeros((t, 2, self.cells, 2, 4, n), np.float32)
        for depth in range(2):
            for k in range(2):
                for src in range(t):
                    for e in range(w):
                        if src > 0:
                            at = self.spot(depth, w + 2 + e)
                            from_a[src, k, at, k, depth, 2 * self.side + src * w + e] = 1
                        if src < t - 1:
                            from_b[src, k, self.spot(depth, e), k, depth, src * w + e] = 1
                for e in range(self.reach):
                    at = self.spot(depth, e)
                    from_a[0, k, at, k, 2 + depth, e] = 1
                    from_b[t - 1, k, at, k, 2 + depth, 8 + e] = 1
        ends = np.zeros((self.reach, n, n), np.float32)
        for e in range(self.reach):
            ends[e, 0, e] = 1
            ends[e, self.height - 1, 8 + e] = 1
        shape = (t * c, 8 * n)
        return (
            jnp.asarray(from_a.reshape(shape), BF16),
            jnp.asarray(from_b.reshape(shape), BF16),
            jnp.asarray(ends.reshape(-1, n), BF16),
        )


def first_kernel(plan, ids_ref, table_ref, columns_ref, blocks_ref):
    t, c, g, w = plan.tiles, plan.block, plan.stacks, plan.cols
    face = ids_ref[1]
    flat = [
        jnp.concatenate([columns_ref[i, k, j] for j in range(g) for i in range(w)], axis=1)
        for k in range(2)
    ]
    wanted = table_ref[ids_ref[5]]
    cell = lax.broadcasted_iota(jnp.int32, (flat[0].shape[1], wanted.shape[1]), 0)
    pick = jnp.where(cell == wanted, 1.0, 0.0).astype(BF16)
    picked = product(jnp.concatenate(flat, axis=0), pick, 1, 0)
    channels = flat[0].shape[0]
    both = jnp.transpose(picked[:channels] + pltpu.roll(picked[channels:], plan.cells, 1))
    both = both.reshape(t, plan.kinds, c, both.shape[-1])
    for dest in range(plan.faces):
        if plan.kinds == 2:
            block = jnp.where(face == dest, both[:, 0], both[:, 1])
        else:
            block = both[:, 0]
        blocks_ref[dest] = block.astype(BF16)


def product(x, y, x_dim, y_dim):
    return lax.dot_general(x, y, (((x_dim,), (y_dim,)), ((), ())), preferred_element_type=F32)


def shift(x, by):
    return pltpu.roll(x, by % x.shape[1], 1)


def seam_cells(plan, ids_ref, got_ref, tab_a, tab_b):
    face = ids_ref[1]
    after = lax.rem(face + 1, plan.faces)
    before = lax.rem(face + plan.faces - 1, plan.faces)
    result = []
    for g in range(plan.stacks):
        face_a = face if g < plan.stacks - 1 else after
        face_b = face if g > 0 else before
        pair = []
        for at, table in ((face_a, tab_a), (face_b, tab_b)):
            rows = got_ref[at].astype(F32)
            rows = rows.reshape(plan.tiles * plan.block, rows.shape[-1])
            pair.append(product(rows.astype(BF16), table[...], 0, 0))
        result.append(pair)
    return result


def surroundings(plan, ids_ref, k, columns_ref, inner_ref, outer_ref, across_ref, seams_of, tab_ends):
    w, n, side = plan.cols, plan.lanes, plan.side
    high, g_count = plan.height, plan.stacks
    first = ids_ref[0] == 0
    last = ids_ref[0] == plan.tiles - 1
    even = lax.rem(ids_ref[0], 2) == 0
    shape = (plan.channels, n)
    lane = lax.broadcasted_iota(jnp.int32, shape, 1)
    stacks = []
    line, deep, ends = [jnp.zeros(shape, F32) for _ in range(3)]
    for g in range(g_count):
        start = 4 * k * n
        seams = [
            [x[:, start + i * n : start + (i + 1) * n] for i in range(4)] for x in seams_of[g]
        ]
        line += shift(seams[0][2] + seams[1][2], 16 * g)
        deep += shift(seams[0][3] + seams[1][3], 16 * g)
        raw = [jnp.where(even, outer_ref[i, k, g], inner_ref[i, k, g]) for i in range(2)]
        raw += [columns_ref[i, k, g] for i in range(w)]
        raw += [jnp.where(even, inner_ref[i, k, g], outer_ref[i, k, g]) for i in range(2)]
        ends += shift(product(jnp.concatenate(raw, axis=1), tab_ends[...], 1, 0), 16 * g)
        raw = [x.astype(F32) for x in raw]
        for d in range(2):
            for i in range(2):
                here = lane == side - 2 + i
                seams[1][d] = jnp.where(here, shift(raw[i], side - 2 + i - d), seams[1][d])
                here = lane == 2 * side + i
                by = 2 * side + i - (high - 1 - d)
                seams[0][d] = jnp.where(here, shift(raw[w + 2 + i], by), seams[0][d])
        pole = [across_ref[i, k, g].astype(F32) for i in range(2)]
        north = [pole[0][:, :1], pole[1][:, :1], pole[0][:, 1:2]]
        south = [pole[1][:, high - 1 : high], pole[0][:, high - 1 : high]]
        south.append(pole[1][:, high - 2 : high - 1])
        stacks.append(
            dict(
                raw=raw,
                row_l=seams[1][:2],
                row_r=seams[0][:2],
                col_l=[shift(x, plan.side) for x in raw[:2]],
                col_r=[shift(x, -plan.side) for x in raw[w + 2 :]],
                north=north,
                south=south,
            )
        )
    spot = lane % 8
    is_top = (lane % 16) < 8
    unsent = (first & is_top & (spot < 2)) | (last & jnp.logical_not(is_top) & (spot >= w + 2))
    line = jnp.where(unsent, 0.0, line)
    deep = jnp.where(unsent, 0.0, deep)
    ends = jnp.where(first & (spot < 2), 0.0, ends)
    ends = jnp.where(last & (spot >= w + 2), 0.0, ends)
    rim = dict(line=line, deep=deep, ends=ends, spot=spot, is_top=is_top)
    return stacks, rim, lane, first, last


def rim_cell(plan, lane, g, bottom, e):
    return lane == 16 * g + 8 * bottom + e


def wide_forward(plan, found, taps_ref, inner):
    stacks, rim, lane, first, last = found
    w, n, side, high, c = plan.cols, plan.lanes, plan.side, plan.height, plan.channels

    def put(a, b, segment, value):
        if (segment < plan.inner) != inner:
            return
        segment -= 0 if inner else plan.inner
        row = (a * 3 + b) * c
        taps_ref[row : row + c, segment * n : (segment + 1) * n] = value.astype(BF16)

    rows_r = (lane >= 2 * side) & (lane < high)
    for g, h in enumerate(stacks):
        raw = h["raw"]
        x = []
        for q in range(w + 4):
            at = 16 * g + q
            y = jnp.where(lane == high, rim["line"][:, at + 8 : at + 9], raw[q])
            x.append(jnp.where(lane == n - 1, rim["line"][:, at : at + 1], y))
        edge_l = jnp.where(lane < side, h["row_l"][0], jnp.where(lane < high, h["col_l"][1], 0.0))
        edge_r = jnp.where(lane < 2 * side, h["col_r"][0], jnp.where(rows_r, h["row_r"][0], 0.0))
        x[0] = jnp.where(first, h["col_l"][0], x[0])
        x[1] = jnp.where(first, edge_l, x[1])
        x[w + 2] = jnp.where(last, edge_r, x[w + 2])
        x[w + 3] = jnp.where(last, h["col_r"][1], x[w + 3])
        moved = [[shift(y, 1 - b) if b != 1 else y for b in range(3)] for y in x]
        own0, own1, own30, own31 = raw[2], raw[3], raw[w], raw[w + 1]
        north, south = h["north"], h["south"]
        turned_l = [jnp.where(lane < side, own0, 0.0)]
        turned_r = []
        for d in range(2):
            y = jnp.where(lane < side, h["row_l"][d], shift(own0, -d))
            turned_l.append(jnp.where(lane == n - 1, north[d], y))
            y = jnp.where(rows_r, h["row_r"][d], shift(own31, d))
            turned_r.append(jnp.where(lane == high, south[d], y))
        turned_l[1:] = [
            jnp.where((lane > side) & (lane < n - 1), 0.0, y) for y in turned_l[1:]
        ]
        turned_r = [turned_r[1], turned_r[0], jnp.where(rows_r, own31, 0.0)]
        for b in range(3):
            for a in range(3):
                for j in range(1, w + 1):
                    put(a, b, plan.segment(g, j), moved[j + a][b])
                y = shift(h["col_l"][1], 1 - b) if a == 1 else moved[a][b]
                y = jnp.where(lane < side, shift(turned_l[b], 1 - a), y)
                if b == 0:
                    over = shift(own0, 2 - a) if a < 2 else 0.0
                    y = jnp.where(lane == side, over, y)
                elif a == 2:
                    y = jnp.where(lane == high, shift((own0, own1)[b - 1], 1), y)
                    if b == 2:
                        y = jnp.where(lane == high - 1, own0, y)
                put(a, b, plan.segment(g, 0), jnp.where(first, y, moved[a][b]))
                y = shift(h["col_r"][0], 1 - b) if a == 1 else moved[w + 1 + a][b]
                y = jnp.where(rows_r, shift(turned_r[b], 1 - a), y)
                if b == 2:
                    over = shift(own31, -a) if a > 0 else 0.0
                    y = jnp.where(lane == 2 * side - 1, over, y)
                if a == 0:
                    if b == 0:
                        y = jnp.where(lane == 0, own31, y)
                    y = jnp.where(lane == n - 1, shift(own30 if b == 0 else own31, -1), y)
                put(a, b, plan.segment(g, w + 1), jnp.where(last, y, moved[w + 1 + a][b]))
    line, deep, ends = rim["line"], rim["deep"], rim["ends"]
    is_top, spot = rim["is_top"], rim["spot"]
    ends = jnp.where(last & is_top & (spot == w + 2), shift(ends, 1), ends)
    ends = jnp.where(first & jnp.logical_not(is_top) & (spot == 1), shift(ends, -1), ends)
    for g, h in enumerate(stacks):
        north = first & rim_cell(plan, lane, g, 0, 1)
        south = last & rim_cell(plan, lane, g, 1, w + 2)
        line = jnp.where(north, h["north"][0], line)
        deep = jnp.where(north, h["north"][2], deep)
        line = jnp.where(south, h["south"][0], line)
        deep = jnp.where(south, h["south"][2], deep)
    by_a = (jnp.where(is_top, ends, deep), line, jnp.where(is_top, deep, ends))
    for a in range(3):
        for b in range(3):
            put(a, b, plan.inner + plan.outer - 1, shift(by_a[a], -b) if b else by_a[a])


def wide_backward(plan, found, taps_ref, inner, edge_ref=None):
    stacks, rim, lane, first, last = found
    w, n, side, high, c = plan.cols, plan.lanes, plan.side, plan.height, plan.channels

    def put(row, segment, value):
        if (segment < plan.inner) != inner or (inner and row >= 9):
            return
        segment -= 0 if inner else plan.inner
        taps_ref[row * c : (row + 1) * c, segment * n : (segment + 1) * n] = value.astype(BF16)

    zero = jnp.zeros(lane.shape, F32)
    rows_l = lane < side
    rows_r = (lane >= 2 * side) & (lane < high)
    lines = []
    for g, h in enumerate(stacks):
        raw = h["raw"]
        z = list(raw)
        edge_l = jnp.where((lane >= side) & (lane <= high), h["col_l"][1], 0.0)
        edge_r = jnp.where((lane < 2 * side) | (lane == n - 1), h["col_r"][0], 0.0)
        z[1] = jnp.where(first, edge_l, z[1])
        z[w + 2] = jnp.where(last, edge_r, z[w + 2])
        moved = [[shift(y, b - 1) if b != 1 else y for b in range(3)] for y in z]
        keep_l = (lane >= side) | jnp.logical_not(first)
        keep_r = (lane < 2 * side) | jnp.logical_not(last)
        own0, own1, own30, own31 = raw[2], raw[3], raw[w], raw[w + 1]
        north, south = h["north"], h["south"]
        line_l = [jnp.where(rows_l, y, 0.0) for y in h["row_l"]]
        line_r = [jnp.where(rows_r, y, 0.0) for y in h["row_r"]]
        line_l = [line_l[1], line_l[0], zero]
        line_r = [zero, line_r[0], line_r[1]]
        lines.append((line_l[1], line_r[1]))
        keep = (lane >= side) & (lane <= high + 1)
        deep_l = [zero] + [jnp.where(keep, h["col_l"][i], 0.0) for i in (1, 0)]
        keep = (lane < 2 * side) | (lane >= n - 2)
        deep_r = [jnp.where(keep, h["col_r"][i], 0.0) for i in (1, 0)] + [zero]
        for b in range(3):
            for a in range(3):
                tap = a * 3 + b
                for j in range(1, w + 1):
                    y = moved[j + 2 - a][b]
                    if j == 1 and a == 2:
                        y = jnp.where(keep_l, y, 0.0)
                    if j == w and a == 0:
                        y = jnp.where(keep_r, y, 0.0)
                    put(tap, plan.segment(g, j), y)
                y = jnp.where(rows_l, shift(line_l[b], a - 1), shift(deep_l[a], b - 1))
                if a == 0:
                    y = jnp.where(lane == side - 1, shift(own0, b - 2), y)
                    y = jnp.where(lane == side, shift(own0, b), y)
                put(tap, plan.segment(g, 0), jnp.where(first, y, moved[2 - a][b]))
                y = jnp.where(rows_r, shift(line_r[b], a - 1), shift(deep_r[a], b - 1))
                if a == 2:
                    y = jnp.where(lane == 2 * side - 1, shift(own31, b - 2), y)
                    y = jnp.where(lane == 2 * side, shift(own31, b), y)
                put(tap, plan.segment(g, w + 1), jnp.where(last, y, moved[w + 3 - a][b]))
        for j in range(w + 2):
            segment = plan.segment(g, j)
            for b in range(3):
                at = 16 * g + j + 2 - b
                top = jnp.where(lane == 0, rim["line"][:, at : at + 1], 0.0)
                bottom = jnp.where(lane == high - 1, rim["line"][:, at + 8 : at + 9], 0.0)
                left = right = zero
                if j == 0:
                    own = jnp.where(lane < high, shift(own0, b - 1), 0.0)
                    top = jnp.where(first, own, top)
                    bottom = jnp.where(first, 0.0, bottom)
                    if b < 2:
                        left = jnp.where(first & (lane == 0), north[1 - b], 0.0)
                        right = jnp.where(first & (lane == high), shift((own1, own0)[b], 1), 0.0)
                if j == 1:
                    left = jnp.where(first & rows_l, shift(line_l[1], b - 1), 0.0)
                if j == w:
                    right = jnp.where(last & rows_r, shift(line_r[1], b - 1), 0.0)
                if j == w + 1:
                    own = jnp.where(lane < high, shift(own31, b - 1), 0.0)
                    bottom = jnp.where(last, own, bottom)
                    top = jnp.where(last, 0.0, top)
                    if b > 0:
                        over = shift((own31, own30)[b - 1], -1)
                        left = jnp.where(last & (lane == n - 1), over, 0.0)
                        right = jnp.where(last & (lane == high - 1), south[b - 1], 0.0)
                for i, y in enumerate((top, bottom, left, right)):
                    put(9 + 3 * i + b, segment, y)
    line, deep, ends = rim["line"], rim["deep"], rim["ends"]
    is_top = rim["is_top"]
    if inner:
        here = (rim["spot"] >= 1) & (rim["spot"] <= w) & (lane < plan.lines)
        for b in range(3):
            near = jnp.where(here, shift(line, b - 2), 0.0)
            left = right = zero
            for g, (line_l, line_r) in enumerate(lines):
                at = plan.lines + g * side
                y = jnp.where(first & rows_l, shift(line_l, b - 1), 0.0)
                left += shift(y, at)
                y = jnp.where(last & rows_r, shift(line_r, b - 1), 0.0)
                right += shift(y, at - 2 * side)
            top, bottom = jnp.where(is_top, near, 0.0), jnp.where(is_top, 0.0, near)
            for i, y in enumerate((top, bottom, left, right)):
                row = (3 * i + b) * c
                edge_ref[row : row + c, :] = y.astype(BF16)
        return
    tops = [jnp.where(is_top, y, 0.0) for y in (deep, ends)]
    bottoms = [jnp.where(is_top, 0.0, y) for y in (deep, ends)]
    by_a = (tops[0], line, bottoms[0])
    segment = plan.inner + plan.outer - 1
    for b in range(3):
        for a in range(3):
            put(a * 3 + b, segment, shift(by_a[a], b - 2))
        top = bottom = zero
        for g, h in enumerate(stacks):
            if b < 2:
                over = h["north"][2 * (1 - b)]
                top = jnp.where(first & rim_cell(plan, lane, g, 0, 1), over, top)
            if b > 0:
                over = h["south"][2 * (b - 1)]
                bottom = jnp.where(last & rim_cell(plan, lane, g, 1, w), over, bottom)
        put(9 + b, segment, top)
        put(12 + b, segment, bottom)
        put(15 + b, segment, shift(tops[1], b - 2))
        put(18 + b, segment, shift(bottoms[1], b - 2))


def second_halos(plan, ids_ref, ref):
    w, n, high, side = plan.cols, plan.lanes, plan.height, plan.side
    first = ids_ref[0] == 0
    last = ids_ref[0] == plan.tiles - 1
    start = (plan.outer - 1) * n
    rim = ref[:, start : start + n].astype(F32)
    lane = lax.broadcasted_iota(jnp.int32, rim.shape, 1)
    result = []
    for g in range(plan.stacks):
        left, right = [
            ref[:, j * n : (j + 1) * n].astype(F32) for j in (2 * g, 2 * g + 1)
        ]
        top = [rim[:, 16 * g + e : 16 * g + e + 1] for e in range(w + 2)]
        bottom = [rim[:, 16 * g + 8 + e : 16 * g + 9 + e] for e in range(w + 2)]
        top[0] = jnp.where(first, 0.0, top[0])
        bottom[0] = jnp.where(first, left[:, high - 1 : high], bottom[0])
        top[w + 1] = jnp.where(last, right[:, 0:1], top[w + 1])
        bottom[w + 1] = jnp.where(last, 0.0, bottom[w + 1])
        result.append(
            dict(
                first=first,
                last=last,
                left=left,
                right=right,
                row_l=jnp.where(lane < side, left, 0.0),
                row_r=jnp.where((lane >= 2 * side) & (lane < high), right, 0.0),
                col_l=left,
                col_r=right,
                top=top,
                bottom=bottom,
            )
        )
    return result


def forward_operand(plan, own, halo, taps_ref):
    w, n, side, height = plan.cols, plan.lanes, plan.side, plan.height
    c = plan.channels
    lane = lax.broadcasted_iota(jnp.int32, (c, n), 1)
    for g in range(plan.stacks):
        h = halo[g]
        edge_l = jnp.where(lane < side, h["row_l"], jnp.where(lane < height, h["col_l"], 0.0))
        edge_r = jnp.where(
            lane < 2 * side, h["col_r"], jnp.where(lane < height, h["row_r"], 0.0)
        )
        columns = [h["left"]] + own[g] + [h["right"]]
        for j in range(w + 2):
            x = jnp.where(lane == height, h["bottom"][j], columns[j])
            x = jnp.where(lane == n - 1, h["top"][j], x)
            if j == 0:
                x = jnp.where(h["first"], edge_l, x)
            if j == w + 1:
                x = jnp.where(h["last"], edge_r, x)
            for b in range(3):
                y = (x if b == 1 else shift(x, 1 - b)).astype(BF16)
                for a in range(3):
                    out = j - a
                    if 0 <= out < w:
                        at = (g * w + out) * n
                        row = (a * 3 + b) * c
                        taps_ref[row : row + c, at : at + n] = y


def backward_operand(plan, own, halo, taps_ref):
    w, n, side, height = plan.cols, plan.lanes, plan.side, plan.height
    c = plan.channels
    lane = lax.broadcasted_iota(jnp.int32, (c, n), 1)
    zero = jnp.zeros((c, n), BF16)
    for g in range(plan.stacks):
        h = halo[g]
        first, last = h["first"], h["last"]
        edge_l = jnp.where((lane >= side) & (lane <= height), h["col_l"], 0.0)
        edge_r = jnp.where((lane < 2 * side) | (lane == n - 1), h["col_r"], 0.0)
        columns = [jnp.where(first, edge_l, h["left"])] + own[g]
        columns += [jnp.where(last, edge_r, h["right"])]
        keep_l = (lane >= side) | jnp.logical_not(first)
        keep_r = (lane < 2 * side) | jnp.logical_not(last)
        for j in range(w + 2):
            for b in range(3):
                y = columns[j] if b == 1 else shift(columns[j], b - 1)
                if j == 0:
                    y = jnp.where(keep_l, y, 0.0)
                if j == w + 1:
                    y = jnp.where(keep_r, y, 0.0)
                y = y.astype(BF16)
                for a in range(3):
                    out = j - 2 + a
                    if 0 <= out < w:
                        at = (g * w + out) * n
                        row = (a * 3 + b) * c
                        taps_ref[row : row + c, at : at + n] = y
        seam_l = first & (lane < side)
        seam_r = last & (lane >= 2 * side) & (lane < height)
        for out in range(w):
            at = (g * w + out) * n
            for b in range(3):
                y = jnp.where(lane == 0, h["top"][out + 2 - b], 0.0).astype(BF16)
                taps_ref[(9 + b) * c : (10 + b) * c, at : at + n] = y
                y = jnp.where(lane == height - 1, h["bottom"][out + 2 - b], 0.0).astype(BF16)
                taps_ref[(12 + b) * c : (13 + b) * c, at : at + n] = y
                y = zero
                if out == 0:
                    y = jnp.where(seam_l, shift(h["row_l"], b - 1), 0.0).astype(BF16)
                taps_ref[(15 + b) * c : (16 + b) * c, at : at + n] = y
                y = zero
                if out == w - 1:
                    y = jnp.where(seam_r, shift(h["row_r"], b - 1), 0.0).astype(BF16)
                taps_ref[(18 + b) * c : (19 + b) * c, at : at + n] = y


TAPS = list(range(9))
SEAMS = [0, 1, 2, 6, 7, 8, 0, 3, 6, 2, 5, 8]


def tap_weights(kernel_ref, order):
    return jnp.concatenate([kernel_ref[tap] for tap in order], axis=1)


def seam_weights(kernel_ref):
    return tap_weights(kernel_ref, TAPS + SEAMS)


def from_edges(plan, ids_ref, edges):
    w, n, side, high = plan.cols, plan.lanes, plan.side, plan.height
    first = ids_ref[0] == 0
    last = ids_ref[0] == plan.tiles - 1
    lane = lax.broadcasted_iota(jnp.int32, edges.shape, 1)
    result = []
    for g in range(plan.stacks):
        at = plan.lines + g * side
        for j in range(1, w + 1):
            top, bottom = 16 * g + j, 16 * g + 8 + j
            y = jnp.where(lane == 0, edges[:, top : top + 1], 0.0)
            y = jnp.where(lane == high - 1, edges[:, bottom : bottom + 1], y)
            if j == 1:
                y += jnp.where(first & (lane < side), shift(edges, -at), 0.0)
            if j == w:
                rows_r = last & (lane >= 2 * side) & (lane < high)
                y += jnp.where(rows_r, shift(edges, 2 * side - at), 0.0)
            result.append(y)
    return jnp.concatenate(result, axis=1)


def to_edges(plan, ids_ref, flat):
    w, n, side, high = plan.cols, plan.lanes, plan.side, plan.height
    first = ids_ref[0] == 0
    result = jnp.zeros((flat.shape[0], n), F32)
    lane = lax.broadcasted_iota(jnp.int32, result.shape, 1)
    for g in range(plan.stacks):
        own = [flat[:, (g * w + i) * n : (g * w + i + 1) * n] for i in range(w)]
        at = plan.lines + g * side
        line_l = shift(jnp.where(lane < side, own[0], 0.0), at)
        rows_r = (lane >= 2 * side) & (lane < high)
        line_r = shift(jnp.where(rows_r, own[-1], 0.0), at - 2 * side)
        result += jnp.where(first, line_l, line_r)
        for j in range(1, w + 1):
            top, bottom = 16 * g + j, 16 * g + 8 + j
            result = jnp.where(lane == top, own[j - 1][:, :1], result)
            result = jnp.where(lane == bottom, own[j - 1][:, high - 1 : high], result)
    return result.astype(BF16)


def own_columns(plan, ref):
    w, n = plan.cols, plan.lanes
    return [
        [ref[:, (g * w + i) * n : (g * w + i + 1) * n].astype(F32) for i in range(w)]
        for g in range(plan.stacks)
    ]


def kept_lanes(plan, ids_ref, shape, inner):
    flat = lax.broadcasted_iota(jnp.int32, shape, 1)
    segment, lane = flat // plan.lanes, flat % plan.lanes
    inside = lane < plan.height
    if not inner:
        first = ids_ref[0] == 0
        last = ids_ref[0] == plan.tiles - 1
        inside = inside | (segment == plan.outer - 1)
        inside = inside | ((segment % 2 == 0) & first & (lane == plan.height))
        inside = inside | ((segment % 2 == 1) & last & (lane == plan.lanes - 1))
    return inside


def with_seams(plan, ids_ref, around, tables):
    *around, got = around
    seams = seam_cells(plan, ids_ref, got, *tables[:2])
    return (*around, seams, tables[2])


def go_forward(plan, ids_ref, around, weight, fwd_ref, inner):
    wide_forward(plan, surroundings(plan, ids_ref, 0, *around), fwd_ref, inner)
    pre = product(weight[...], fwd_ref[...], 0, 0)
    bend = jnp.tanh(GELU_A * (pre + GELU_B * (pre * pre * pre)))
    half = 0.5 * (1.0 + bend)
    slope = half + 0.5 * pre * (1.0 - bend * bend) * (
        GELU_A * (1.0 + (3.0 * GELU_B) * (pre * pre))
    )
    inside = kept_lanes(plan, ids_ref, pre.shape, inner)
    return jnp.where(inside, pre * half, 0.0).astype(BF16), slope


def go_back(plan, ids_ref, around, weight, slope, bwd_ref, inner, edge_ref=None):
    wide_backward(plan, surroundings(plan, ids_ref, 1, *around), bwd_ref, inner, edge_ref)
    if inner:
        edges = product(tap_weights(weight, SEAMS), edge_ref[...], 1, 0)
        grad = product(tap_weights(weight, TAPS), bwd_ref[...], 1, 0)
        grad += from_edges(plan, ids_ref, edges)
    else:
        grad = product(seam_weights(weight), bwd_ref[...], 1, 0)
    inside = kept_lanes(plan, ids_ref, grad.shape, inner)
    return jnp.where(inside, grad * slope, 0.0).astype(BF16)


def outer_forward_kernel(plan, ids_ref, *refs):
    around, tables, (weight, hidden_ref, slope_ref, fwd_ref) = refs[:5], refs[5:8], refs[8:]
    around = with_seams(plan, ids_ref, around, tables)
    hidden_ref[...], slope_ref[...] = go_forward(plan, ids_ref, around, weight, fwd_ref, False)


def outer_back_kernel(plan, ids_ref, *refs):
    around, tables, (weight, slope_ref, pre_grad_ref, bwd_ref) = refs[:5], refs[5:8], refs[8:]
    around = with_seams(plan, ids_ref, around, tables)
    pre_grad_ref[...] = go_back(plan, ids_ref, around, weight, slope_ref[...], bwd_ref, False)


def inner_kernel(plan, ids_ref, *refs):
    c = plan.channels
    around, tables, weights, refs = refs[:5], refs[5:8], refs[8:10], refs[10:]
    hidden_ref, pre_grad_ref, mine_ref, theirs_ref, *refs = refs
    fwd_ref, bwd_ref, edge_ref, sums_ref, packed_ref = refs
    around = with_seams(plan, ids_ref, around, tables)
    hidden, slope = go_forward(plan, ids_ref, around, weights[0], fwd_ref, True)
    pre_grad = go_back(plan, ids_ref, around, weights[1], slope, bwd_ref, True, edge_ref)
    hidden_ref[...] = hidden
    pre_grad_ref[...] = pre_grad
    terms = product(fwd_ref[...], pre_grad, 1, 1)
    turned = product(bwd_ref[...], hidden, 1, 1)
    edge_cells = to_edges(plan, ids_ref, hidden.astype(F32))
    edges = product(edge_ref[...], edge_cells, 1, 1)
    tap = [turned[i * c : (i + 1) * c] for i in range(9)]
    tap += [edges[i * c : (i + 1) * c] for i in range(12)]
    for b in range(3):
        tap[b] = tap[b] + tap[9 + b]
        tap[6 + b] = tap[6 + b] + tap[12 + b]
    for a in range(3):
        tap[3 * a] = tap[3 * a] + tap[15 + a]
        tap[3 * a + 2] = tap[3 * a + 2] + tap[18 + a]
    sums_ref[0 : 9 * c, :] = terms
    for i in range(9):
        sums_ref[(9 + i) * c : (10 + i) * c, :] = jnp.transpose(tap[i])
    packed_rows = max(plan.folds - 1, 1) * plan.fold_rows
    shared = (plan.folds - 1) * plan.fold_rows
    for i in range(max(plan.folds - 1, 1)):
        at = i * plan.fold_rows
        block = sums_ref[at : at + plan.fold_rows, :]
        if plan.folds > 1:
            rest = plan.wide - c
            more = sums_ref[shared : shared + plan.fold_rows, i * rest : (i + 1) * rest]
            block = jnp.concatenate([block, more], axis=1)
        packed_ref[at : at + plan.fold_rows, :] = block
    spare = packed_ref.shape[0] - packed_rows
    if spare:
        packed_ref[packed_rows:, :] = jnp.zeros((spare, plan.wide), F32)
    near, mid = ids_ref[3], ids_ref[4]
    for d in range(plan.mid):
        spot = jnp.bitwise_xor(mid, d)
        for other, ref in ((0, mine_ref), (1, theirs_ref)):
            at = (jnp.bitwise_xor(near, other) * plan.mid + spot) * plan.piece
            rows = packed_ref[pl.ds(pl.multiple_of(at, 16), plan.piece), :]
            ref[d] = rows.astype(ref.dtype)


def last_kernel(plan, ids_ref, hidden_ref, pre_grad_ref, hidden_out, pre_grad_out, *refs):
    w_two, w_one, out_ref, back_ref, fwd_ref, bwd_ref = refs
    w, n = plan.cols, plan.lanes
    halo = second_halos(plan, ids_ref, hidden_out)
    forward_operand(plan, own_columns(plan, hidden_ref), halo, fwd_ref)
    halo = second_halos(plan, ids_ref, pre_grad_out)
    backward_operand(plan, own_columns(plan, pre_grad_ref), halo, bwd_ref)
    out = product(w_two[...], fwd_ref[...], 0, 0).astype(BF16)
    back = product(seam_weights(w_one), bwd_ref[...], 1, 0).astype(BF16)
    for g in range(plan.stacks):
        for i in range(w):
            at = (g * w + i) * n
            out_ref[:, g, i, :] = out[:, at : at + plan.height]
            back_ref[:, g, i, :] = back[:, at : at + plan.height]


def sum_kernel(plan, scale, ids_ref, mine_ref, theirs_ref, one_ref, two_ref, packed_ref):
    near, mid = ids_ref[3], ids_ref[4]
    for d in range(plan.mid):
        spot = jnp.bitwise_xor(mid, d)
        for other, ref in ((0, mine_ref), (1, theirs_ref)):
            at = (jnp.bitwise_xor(near, other) * plan.mid + spot) * plan.piece
            packed_ref[pl.ds(pl.multiple_of(at, 16), plan.piece), :] = ref[d].astype(F32) * scale
    c, rows = plan.channels, one_ref.shape[0]

    def store(at, value):
        for start, ref in ((0, one_ref), (rows, two_ref)):
            low = max(at, start)
            high = min(at + value.shape[0], start + rows)
            if low < high:
                ref[low - start : high - start, :] = value[low - at : high - at]

    more = []
    for i in range(max(plan.folds - 1, 1)):
        at = i * plan.fold_rows
        block = packed_ref[at : at + plan.fold_rows, :]
        store(at, block[:, :c])
        more.append(block[:, c:])
    if plan.folds > 1:
        store((plan.folds - 1) * plan.fold_rows, jnp.concatenate(more, axis=1))


VMEM = pl.BlockSpec(memory_space=pltpu.VMEM)
SMEM = pl.BlockSpec(memory_space=pltpu.SMEM)


def call(body, ids, inputs, outs, scratch=()):
    return pl.pallas_call(
        body,
        out_shape=outs,
        in_specs=[SMEM] + [VMEM] * len(inputs),
        out_specs=[VMEM] * len(outs),
        scratch_shapes=list(scratch),
        compiler_params=pltpu.CompilerParams(vmem_limit_bytes=48 * 2**20),
    )(ids, *inputs)


def across_faces(plan, columns, step):
    t, f = plan.tiles, plan.faces
    first = lax.axis_index("tile") == 0
    sent = jnp.where(first, columns[:2], columns[plan.cols - 2 :])
    pairs = [((t - 1) * f + i, (t - 1) * f + (i + step) % f) for i in range(f)]
    pairs += [((i + step) % f, i) for i in range(f)]
    return lax.ppermute(sent, BOTH, pairs)


def pair_up(plan, columns, passed):
    t, g = plan.tiles, plan.stacks
    tile = lax.axis_index("tile")
    even = tile % 2 == 0
    head, tail = columns[:2], columns[plan.cols - 2 :]
    inner = jnp.where(even, tail, head)
    outer = jnp.where(even, head, tail)
    passed = jnp.where(tile == 0, passed[:, :, :1], passed[:, :, g - 1 :])
    to_last = jnp.concatenate([head[:, :, 1:], passed], axis=2)
    to_first = jnp.concatenate([passed, tail[:, :, : g - 1]], axis=2)
    outer = jnp.where(tile == 0, to_last, jnp.where(tile == t - 1, to_first, outer))
    inner = lax.ppermute(inner, "tile", [(i, i ^ 1) for i in range(t)])
    outer = lax.ppermute(outer, "tile", [(i, ((i + 1) ^ 1) - 1 if i else t - 1) for i in range(t - 1)] + [(t - 1, 0)])
    return inner, outer


def spread_blocks(plan, blocks):
    count = plan.tiles * plan.faces
    flat = blocks.reshape((count,) + blocks.shape[2:])
    return lax.all_to_all(flat, ("face", "tile"), 0, 0, tiled=True).reshape(blocks.shape)


def swapped(plan, x, near=0, mid=0, far=0):
    f = plan.faces
    pairs = []
    for i in range(plan.tiles * f):
        tile, face = i // f, i % f
        tile = tile ^ near ^ ((mid // f) << 1) ^ (far << 2)
        pairs.append((i, tile * f + (face ^ (mid % f))))
    return lax.ppermute(x, BOTH, pairs)


def tree_sum(values):
    while len(values) > 1:
        values = [a + b for a, b in zip(values[::2], values[1::2])]
    return values[0]


def sum_all(plan, mine, theirs, beside):
    half = mine + swapped(plan, theirs, near=1).astype(F32)
    short = half.astype(BF16)
    got = [swapped(plan, short[d], mid=d) for d in range(1, plan.mid)]
    got, kept = lax.optimization_barrier((got, beside[0](None)))
    piece = tree_sum([half[0]] + [x.astype(F32) for x in got]).astype(BF16)
    got = [swapped(plan, piece, far=d) for d in range(1, plan.far)]
    got, kept = lax.optimization_barrier((got, beside[1](kept)))
    piece = tree_sum([x.astype(F32) for x in [piece] + got]).astype(BF16)
    pieces = [piece] + [swapped(plan, piece, mid=d) for d in range(1, plan.mid)]
    pieces, kept = lax.optimization_barrier((pieces, beside[2](kept)))
    half = jnp.stack(pieces)
    return half, swapped(plan, half, near=1), kept


def on_device(mesh_shape, fields, upstream, kernel_one, kernel_two):
    plan = Plan(mesh_shape, fields.shape)
    c, own, w, n = plan.channels, plan.own, plan.cols, plan.lanes
    g, h = plan.stacks, plan.height
    tile, face = lax.axis_index("tile"), lax.axis_index("face")
    sub = lax.axis_index("sub")
    mid = ((tile >> 1) & 1) * plan.faces + face
    kind = jnp.where(tile == 0, 0, jnp.where(tile == plan.tiles - 1, 2, 1))
    ids = jnp.stack([tile, face, sub, tile & 1, mid, kind]).astype(jnp.int32)
    if mesh_shape["sub"] > 1:
        fields = lax.all_gather(fields, "sub", axis=0, tiled=True)
        upstream = lax.all_gather(upstream, "sub", axis=0, tiled=True)

    both = jnp.stack([fields, upstream]).transpose(3, 0, 2, 1, 4)
    columns = jnp.pad(both, ((0, 0),) * 4 + ((0, n - h),))
    blocks_shape = jax.ShapeDtypeStruct((plan.faces, plan.tiles, plan.block, c), BF16)
    (blocks,) = call(
        functools.partial(first_kernel, plan), ids, [plan.send_table(), columns], [blocks_shape]
    )
    passed = across_faces(plan, columns, 1)
    across = passed if g == 2 else across_faces(plan, columns, 2)
    got = spread_blocks(plan, blocks)
    sent, passed, _ = lax.optimization_barrier((columns, passed, blocks))
    halo = (*pair_up(plan, sent, passed), across, got)

    fwd_one = kernel_one.reshape(9 * c, c)
    bwd_two = kernel_two.reshape(9, c, c)
    fwd_two = lax.dynamic_slice_in_dim(kernel_two, sub * own, own, 3).reshape(9 * c, own)
    bwd_one = lax.dynamic_slice_in_dim(kernel_one, sub * own, own, 2).reshape(9, own, c)

    def taps(width):
        return [pltpu.VMEM((9 * c, width), BF16), pltpu.VMEM((21 * c, width), BF16)]

    piece = (plan.mid, plan.piece, plan.wide)
    rows = plan.near * plan.mid * plan.piece
    inner, outer = plan.inner * n, plan.outer * n
    given = [columns, *halo, *plan.take_tables()]
    hidden, pre_grad, mine, theirs = call(
        functools.partial(inner_kernel, plan),
        ids,
        given + [fwd_one, bwd_two],
        [jax.ShapeDtypeStruct((c, inner), BF16)] * 2
        + [jax.ShapeDtypeStruct(piece, F32), jax.ShapeDtypeStruct(piece, BF16)],
        [pltpu.VMEM((9 * c, inner), BF16)] * 2
        + [pltpu.VMEM((12 * c, n), BF16)]
        + [pltpu.VMEM((plan.terms, c), F32), pltpu.VMEM((rows, plan.wide), F32)],
    )
    theirs, given, hidden, pre_grad = lax.optimization_barrier((theirs, given, hidden, pre_grad))

    def outer_forward(unused):
        return call(
            functools.partial(outer_forward_kernel, plan),
            ids,
            given + [fwd_one],
            [jax.ShapeDtypeStruct((c, outer), BF16), jax.ShapeDtypeStruct((c, outer), F32)],
            taps(outer)[:1],
        )

    def outer_back(kept):
        hidden_out, slope = kept
        (pre_grad_out,) = call(
            functools.partial(outer_back_kernel, plan),
            ids,
            given + [bwd_two, slope],
            [jax.ShapeDtypeStruct((c, outer), BF16)],
            taps(outer)[1:],
        )
        return hidden_out, pre_grad_out

    def finish(kept):
        return call(
            functools.partial(last_kernel, plan),
            ids,
            [hidden, pre_grad, *kept, fwd_two, bwd_one],
            [jax.ShapeDtypeStruct((own, g, w, h), BF16)] * 2,
            taps(inner),
        )

    mine, theirs, (result, fields_grad) = sum_all(
        plan, mine, theirs, (outer_forward, outer_back, finish)
    )
    scale = 1.0 / (plan.side * 12.0**0.5)
    sums = call(
        functools.partial(sum_kernel, plan, scale),
        ids,
        [mine, theirs],
        [jax.ShapeDtypeStruct((9 * c, c), F32)] * 2,
        [pltpu.VMEM((rows, plan.wide), F32)],
    )
    grads = []
    for i in range(2):
        grad = sums[i].reshape(3, 3, c, c)
        grads.append(lax.dynamic_slice_in_dim(grad, sub * own, own, 3))
    return (
        result,
        fields_grad,
        grads[0],
        grads[1],
    )


def solution(mesh):
    placed = (P("sub", "face", "tile", "parts"), P("sub", "face", "tile", "parts"), P(), P())
    return jax.shard_map(
        functools.partial(on_device, dict(mesh.shape)),
        mesh=mesh,
        in_specs=placed,
        out_specs=(
            P("sub", "face", "tile", "parts"),
            P("sub", "face", "tile", "parts"),
            P("parts", None, None, "sub"),
            P("parts", None, None, "sub"),
        ),
        check_vma=False,
    )
```
